32 devices in a mesh: dp: 8 (over y, x, core), tp: 4 (over z).
Axes of the slice: x: 2, y: 2, z: 4, core: 2. Of those that a mesh axis runs over, the one named last changes fastest.
Arguments:
- mel_frames: bfloat16 [16384, 100], P(('dp', 'tp')), may hold values from -6 to 6
- noise_frames: bfloat16 [16384, 100], P(('dp', 'tp')), may hold values from -6 to 6
- text_ids: int32 [16384], P(('dp', 'tp')), may hold values from 0 to 2559
- span_mask: int32 [16384], P(('dp', 'tp')), may hold values 0 or 1
- lengths: int32 [16], P('dp'), may hold values from 256 to 1024, as said below
- audio_drop: int32 [16], P('dp'), may hold values 0 or 1
- text_drop: int32 [16], P('dp'), may hold values 0 or 1
- flow_times: float32 [16], P('dp'), may hold values from 0.05 to 0.95
- in_proj: bfloat16 [712, 1024], replicated, may hold values from -0.21875 to 0.21875
- text_table: bfloat16 [2560, 512], replicated, may hold values from -6 to 6
- time_proj: bfloat16 [256, 1024], replicated, may hold values from -0.375 to 0.375
- mod_proj: bfloat16 [1024, 6144], P(None, 'tp'), may hold values from -0.1875 to 0.1875
- qkv_proj: bfloat16 [1024, 3, 1024], P(None, None, 'tp'), may hold values from -0.1875 to 0.1875
- out_proj: bfloat16 [1024, 1024], P('tp'), may hold values from -3 to 3
- up_proj: bfloat16 [1024, 2048], P(None, 'tp'), may hold values from -0.1875 to 0.1875
- down_proj: bfloat16 [2048, 1024], P('tp'), may hold values from -0.125 to 0.125
- cotangent: bfloat16 [16384, 1024], P(('dp', 'tp')), may hold values from -6 to 6
Outputs:
- layer_out: bfloat16 [16384, 1024], P(('dp', 'tp'))
- mel_grad: float32 [16384, 100], P(('dp', 'tp'))
- in_proj_grad: float32 [712, 1024], P('tp')
- table_grad: float32 [2560, 512], P('tp')
- time_grad: float32 [256, 1024], P('tp')
- mod_grad: float32 [1024, 6144], P(None, 'tp')
- qkv_grad: float32 [1024, 3, 1024], P(None, None, 'tp')
- out_proj_grad: float32 [1024, 1024], P('tp')
- up_grad: float32 [1024, 2048], P(None, 'tp')
- down_grad: float32 [2048, 1024], P('tp')
The draws below stay inside these ranges and needn't reach their ends.
Inputs may be any that keep to these rules, and one draw needn't show every extreme that they name: Utterance lengths; in every draw one utterance has exactly 1024 frames.
All inputs are finite; a program needn't handle non-finite values. No bound on the sum of `span_mask` or of `audio_drop` or of `text_drop` on one device may be relied on, other than what follows from the above.
Results may differ from the reference program's by a relative error of at most 0.024.
Values may be sent and summed in bfloat16 or wider, within the bound.
A program may use at most 192 MiB of HBM per device.

```python
import math
import jax
import jax.numpy as jnp
from jax import lax

MODEL_WIDTH = 1024
HEAD_COUNT = 16
HEAD_DIM = 64
FFN_DIM = 2048
MEL_BINS = 100
TEXT_DIM = 512
TIME_DIM = 256
VOCABULARY = 2560
MAX_FRAMES = 1024
UTT_TOTAL = 16
FRAMES = 16384
FEATURES = 712
N_TP = 4


def draw_lengths(key, part):
    first_key, second_key = jax.random.split(jax.random.fold_in(key, 17))
    drawn = jax.random.randint(first_key, (UTT_TOTAL,), MAX_FRAMES // 4, MAX_FRAMES + 1)
    chosen = jax.random.randint(second_key, (), 0, UTT_TOTAL)
    return jnp.where(jnp.arange(UTT_TOTAL) == chosen, MAX_FRAMES, drawn).astype(jnp.int32)


def plant(array, stream_key, low, largest):
    shape = array.shape
    index_at = [jax.random.randint(jax.random.fold_in(stream_key, axis), (), 0, shape[axis]) for axis in range(len(shape))]
    array = array.at[tuple(index_at)].set(low)
    longest = shape.index(max(shape))
    index_at[longest] = (index_at[longest] + 1) % shape[longest]
    return array.at[tuple(index_at)].set(largest)


def steps_of(rng, shape, cuts, least, high):
    def one(position, shards_of):
        steps = jax.random.uniform(jax.random.fold_in(jax.random.fold_in(rng, 6), position), (shards_of,), jnp.float32, least / len(cuts), high / len(cuts))
        return jnp.repeat(jnp.exp(steps), shape[position] // shards_of).reshape((-1,) + (1,) * (len(shape) - position - 1))

    loudness = one(*cuts[0])
    for cut in cuts[1:]:
        loudness = loudness * one(*cut)
    return loudness


def noise(stream_key, shape, scale, most, pieces=(), kind=jnp.bfloat16):
    entries = scale * jax.random.normal(stream_key, shape, jnp.float32)
    if pieces:
        entries = entries * steps_of(stream_key, shape, pieces, -0.22, 0.18)
    return jnp.clip(entries, -most, most).astype(kind)


def setup_inputs(seed: int = 0) -> dict:
    key_list = jax.random.split(jax.random.key(seed), 18)
    return {
        "mel_frames": noise(key_list[0], (FRAMES, MEL_BINS), 1.0, 6.0, ((0, 32),)),
        "noise_frames": noise(key_list[1], (FRAMES, MEL_BINS), 1.0, 6.0, ((0, 32),)),
        "text_ids": plant(jax.random.randint(key_list[2], (FRAMES,), 0, VOCABULARY), jax.random.fold_in(key_list[2], 1), 0, VOCABULARY - 1).astype(jnp.int32),
        "span_mask": plant((jax.random.randint(key_list[3], (FRAMES,), 0, 10) < 7).astype(jnp.int32), jax.random.fold_in(key_list[3], 1), 0, 1),
        "lengths": draw_lengths(jax.random.fold_in(key_list[17], 71), 0),
        "audio_drop": plant((jax.random.randint(key_list[5], (UTT_TOTAL,), 0, 10) < 3).astype(jnp.int32), jax.random.fold_in(key_list[5], 1), 0, 1),
        "text_drop": plant((jax.random.randint(key_list[6], (UTT_TOTAL,), 0, 5) < 1).astype(jnp.int32), jax.random.fold_in(key_list[6], 1), 0, 1),
        "flow_times": jnp.clip(0.05 + 0.9 * jax.random.uniform(key_list[7], (UTT_TOTAL,), jnp.float32) ** steps_of(key_list[7], (UTT_TOTAL,), ((0, 8),), -0.2, 0.2), 0.05, 0.95),
        "in_proj": noise(key_list[8], (FEATURES, MODEL_WIDTH), FEATURES ** -0.5, 0.21875),
        "text_table": noise(key_list[9], (VOCABULARY, TEXT_DIM), 1.0, 6.0),
        "time_proj": noise(key_list[10], (TIME_DIM, MODEL_WIDTH), TIME_DIM ** -0.5, 0.375),
        "mod_proj": noise(key_list[11], (MODEL_WIDTH, 6 * MODEL_WIDTH), MODEL_WIDTH ** -0.5, 0.1875, ((1, 4),)),
        "qkv_proj": noise(key_list[12], (MODEL_WIDTH, 3, MODEL_WIDTH), MODEL_WIDTH ** -0.5, 0.1875, ((2, 4),)),
        "out_proj": noise(key_list[13], (MODEL_WIDTH, MODEL_WIDTH), (max(MODEL_WIDTH // 256, 1)) ** -0.5, 3.0, ((0, 4),)),
        "up_proj": noise(key_list[14], (MODEL_WIDTH, FFN_DIM), MODEL_WIDTH ** -0.5, 0.1875, ((1, 4),)),
        "down_proj": noise(key_list[15], (FFN_DIM, MODEL_WIDTH), FFN_DIM ** -0.5, 0.125, ((0, 4),)),
        "cotangent": noise(key_list[16], (FRAMES, MODEL_WIDTH), 1.0, 6.0, ((0, 32),)),
    }


PRECISE = lax.Precision.HIGHEST

@jax.custom_vjp
def low(v):
    return lax.optimization_barrier(v.astype(jnp.bfloat16)).astype(jnp.float32)

@jax.custom_vjp
def low_back(v):
    return v

def low_keep(v):
    return (low(v), None)

def low_pass(kept, grad):
    return (grad,)

def back_keep(v):
    return (v, None)

def back_low(kept, grad):
    return (low(grad),)
low.defvjp(low_keep, low_pass)
low_back.defvjp(back_keep, back_low)

def layer_norm(values):
    average = lax.optimization_barrier(jnp.mean(values, axis=-1, keepdims=True))
    centered = values - average
    spread = lax.optimization_barrier(jnp.mean(centered * centered, axis=-1, keepdims=True))
    return centered * lax.rsqrt(spread + 1e-06)

def modulate(values, scale_part, shift_part):
    return layer_norm(values) * (1.0 + scale_part) + shift_part

def time_features(flow_times, width):
    half_dim = width // 2
    frequency = jnp.exp(jnp.arange(half_dim, dtype=jnp.float32) * (-math.log(10000.0) / (half_dim - 1)))
    angles = 1000.0 * flow_times[:, None] * frequency[None, :]
    return jnp.concatenate([jnp.sin(angles), jnp.cos(angles)], axis=1)

def rope_tables(positions, head_dim):
    half_dim = head_dim // 2
    inverse = jnp.exp(jnp.arange(half_dim, dtype=jnp.float32) * (-2.0 * math.log(10000.0) / head_dim))
    angles = positions.astype(jnp.float32)[:, None] * inverse[None, :]
    return (jnp.cos(angles), jnp.sin(angles))

def rotate(values, cosine, sine):
    paired = values.reshape(values.shape[:-1] + (values.shape[-1] // 2, 2))
    first_part = paired[..., 0]
    second_part = paired[..., 1]
    cos_part = cosine[:, None, :]
    sin_part = sine[:, None, :]
    turned = jnp.stack([first_part * cos_part - second_part * sin_part, second_part * cos_part + first_part * sin_part], axis=-1)
    return turned.reshape(values.shape)

def reference(mel_frames, noise_frames, text_ids, span_mask, lengths, audio_drop, text_drop, flow_times, in_proj, text_table, time_proj, mod_proj, qkv_proj, out_proj, up_proj, down_proj, cotangent):
    utt_total = flow_times.shape[0]
    group_width = MODEL_WIDTH // N_TP
    unit_width = FFN_DIM // N_TP
    scale_factor = 1.0 / math.sqrt(HEAD_DIM)
    keep_audio = (1 - audio_drop).astype(jnp.float32)
    keep_text = (1 - text_drop).astype(jnp.float32)
    keep_span = (1 - span_mask).astype(jnp.float32).reshape(utt_total, MAX_FRAMES)
    noise_three = noise_frames.astype(jnp.float32).reshape(utt_total, MAX_FRAMES, MEL_BINS)
    token_rows = text_ids.reshape(utt_total, MAX_FRAMES)
    time_col = flow_times.astype(jnp.float32)[:, None, None]
    cos_table, sin_table = rope_tables(jnp.arange(MAX_FRAMES, dtype=jnp.int32), HEAD_DIM)
    key_valid = jnp.arange(MAX_FRAMES, dtype=jnp.int32)[None, :] < lengths[:, None]

    def attend(inputs):
        queries, keys_rot, values, valid = inputs
        scores = low_back(jnp.einsum('qhd,khd->hqk', queries, keys_rot, precision=PRECISE) * scale_factor)
        scores = jnp.where(valid[None, None, :], scores, -1e+30)
        peak = lax.optimization_barrier(jnp.max(scores, axis=2, keepdims=True))
        expd = jnp.exp(scores - peak)
        probs = low(expd / lax.optimization_barrier(jnp.sum(expd, axis=2, keepdims=True)))
        return jnp.einsum('hqk,khd->qhd', probs, values, precision=PRECISE)

    def forward(mel_in, table_in, w_in, w_time, w_mod, w_qkv, w_out, w_up, w_down):
        mel_three = mel_in.reshape(utt_total, MAX_FRAMES, MEL_BINS)
        noisy = (1.0 - time_col) * noise_three + time_col * mel_three
        cond = mel_three * (keep_span * keep_audio[:, None])[:, :, None]
        text_emb = low_back(table_in[token_rows] * keep_text[:, None, None])
        features = low(jnp.concatenate([noisy, cond, text_emb], axis=2))
        hidden = low_back(jnp.einsum('ulf,fd->uld', features, w_in, precision=PRECISE))
        sinus = low(time_features(flow_times.astype(jnp.float32), TIME_DIM))
        time_embed = low_back(jnp.dot(sinus, w_time, precision=PRECISE))
        time_act = low(jax.nn.silu(time_embed))
        modulation = low_back(jnp.dot(time_act, w_mod, precision=PRECISE))
        blocks = [part[:, None, :] for part in jnp.split(modulation, 6, axis=1)]
        shift_attn, scale_attn, gate_attn, shift_mlp, scale_mlp, gate_mlp = blocks
        normed_attn = low(modulate(hidden, scale_attn, shift_attn))
        qkv_parts = []
        for group in range(N_TP):
            qkv_parts.append(jnp.einsum('uld,dce->ulce', low_back(normed_attn), w_qkv[:, :, group * group_width:(group + 1) * group_width], precision=PRECISE))
        qkv_all = jnp.concatenate(qkv_parts, axis=3).reshape(utt_total, MAX_FRAMES, 3, HEAD_COUNT, HEAD_DIM)
        queries = low(rotate(low_back(qkv_all[:, :, 0]), cos_table, sin_table))
        keys_rot = low(rotate(low_back(qkv_all[:, :, 1]), cos_table, sin_table))
        values = low(low_back(qkv_all[:, :, 2]))
        heads_out = lax.map(jax.checkpoint(attend), (queries, keys_rot, values, key_valid))
        heads_out = low(low_back(heads_out.reshape(utt_total, MAX_FRAMES, MODEL_WIDTH)))
        attn_total = jnp.zeros((utt_total, MAX_FRAMES, MODEL_WIDTH), jnp.float32)
        for group in range(N_TP):
            attn_total = attn_total + low(jnp.einsum('uld,de->ule', heads_out[:, :, group * group_width:(group + 1) * group_width], w_out[group * group_width:(group + 1) * group_width], precision=PRECISE))
        attn_sum = low_back(attn_total)
        hidden_mid = hidden + gate_attn * attn_sum
        normed_mlp = low(modulate(hidden_mid, scale_mlp, shift_mlp))
        mlp_total = jnp.zeros((utt_total, MAX_FRAMES, MODEL_WIDTH), jnp.float32)
        for group in range(N_TP):
            up_act = low_back(jnp.einsum('uld,df->ulf', low_back(normed_mlp), w_up[:, group * unit_width:(group + 1) * unit_width], precision=PRECISE))
            gelu_act = low(jax.nn.gelu(up_act, approximate=True))
            mlp_total = mlp_total + low(jnp.einsum('ulf,fd->uld', gelu_act, w_down[group * unit_width:(group + 1) * unit_width], precision=PRECISE))
        mlp_sum = low_back(mlp_total)
        result = hidden_mid + gate_mlp * mlp_sum
        return result.reshape(utt_total * MAX_FRAMES, MODEL_WIDTH)
    primal, pullback = jax.vjp(forward, mel_frames.astype(jnp.float32), text_table.astype(jnp.float32), in_proj.astype(jnp.float32), time_proj.astype(jnp.float32), mod_proj.astype(jnp.float32), qkv_proj.astype(jnp.float32), out_proj.astype(jnp.float32), up_proj.astype(jnp.float32), down_proj.astype(jnp.float32))
    grads = pullback(cotangent.astype(jnp.float32))
    return (primal.astype(jnp.bfloat16), grads[0], grads[2], grads[1], grads[3], grads[4], grads[5], grads[6], grads[7], grads[8])
```

```python
import functools
import math

import jax
import jax.numpy as jnp
from jax import lax
from jax.experimental import pallas as pl
from jax.experimental.pallas import tpu as pltpu
from jax.sharding import PartitionSpec as P

WIDTH = 1024
HEAD_DIM = 64
MEL_BINS = 100
TEXT_DIM = 512
TIME_DIM = 256
VOCABULARY = 2560
FFN_DIM = 2048
AXES = ("dp", "tp")
BF = jnp.bfloat16
F32 = jnp.float32


def dot(left, right, left_dim=1, right_dim=0):
    return lax.dot_general(
        left, right, (((left_dim,), (right_dim,)), ((), ())), preferred_element_type=F32
    )


def time_features(flow_times, width):
    half_dim = width // 2
    frequency = jnp.exp(
        jnp.arange(half_dim, dtype=F32) * (-math.log(10000.0) / (half_dim - 1))
    )
    angles = 1000.0 * flow_times[:, None] * frequency[None, :]
    return jnp.concatenate([jnp.sin(angles), jnp.cos(angles)], axis=1)


def rope_tables(positions):
    lane = jnp.arange(WIDTH, dtype=jnp.int32)
    pair = ((lane % HEAD_DIM) // 2).astype(F32)
    inverse = jnp.exp(pair * (-2.0 * math.log(10000.0) / HEAD_DIM))
    angles = positions.astype(F32)[:, None] * inverse[None, :]
    sign = jnp.where(lane % 2 == 0, -1.0, 1.0)
    return jnp.cos(angles), jnp.sin(angles) * sign[None, :]


def swap_pairs(values):
    shape = values.shape
    return jnp.flip(values.reshape(shape[0], shape[1] // 2, 2), axis=2).reshape(shape)


def norm_parts(values):
    average = jnp.mean(values, axis=-1, keepdims=True)
    centered = values - average
    spread = jnp.mean(centered * centered, axis=-1, keepdims=True)
    inverse = lax.rsqrt(spread + 1e-06)
    return centered * inverse, inverse


def norm_back(normed, inverse, scale_part, grad):
    inner = grad * (1.0 + scale_part)
    first = jnp.mean(inner, axis=-1, keepdims=True)
    second = jnp.mean(inner * normed, axis=-1, keepdims=True)
    return inverse * (inner - first - normed * second)


def head_masks(rows):
    lane = lax.broadcasted_iota(jnp.int32, (rows, 2 * HEAD_DIM), 1)
    return [lane < HEAD_DIM, lane >= HEAD_DIM]


def key_bias(info_ref, which, rows, lanes):
    position = lax.broadcasted_iota(jnp.int32, (rows, lanes), 0) + info_ref[1 + which]
    return position < info_ref[0]


def attend_kernel(info_ref, q_ref, k0_ref, v0_ref, k1_ref, v1_ref, o_ref, lse_ref):
    rows = q_ref.shape[0]
    keys = k0_ref.shape[0]
    query = q_ref[...] * jnp.asarray(1.0 / math.sqrt(HEAD_DIM), BF)
    masks = head_masks(rows)
    valid0 = key_bias(info_ref, 0, keys, rows)
    valid1 = key_bias(info_ref, 1, keys, rows)
    vt0 = v0_ref[...].T
    vt1 = v1_ref[...].T
    parts = []
    for head in range(2):
        masked = jnp.where(masks[head], query, jnp.zeros_like(query))
        s0 = jnp.where(valid0, dot(k0_ref[...], masked, 1, 1), -1e30)
        s1 = jnp.where(valid1, dot(k1_ref[...], masked, 1, 1), -1e30)
        peak = jnp.maximum(
            jnp.max(s0, axis=0, keepdims=True), jnp.max(s1, axis=0, keepdims=True)
        )
        e0 = jnp.exp(s0 - peak)
        e1 = jnp.exp(s1 - peak)
        total = jnp.sum(e0, axis=0, keepdims=True) + jnp.sum(e1, axis=0, keepdims=True)
        side = slice(head * HEAD_DIM, (head + 1) * HEAD_DIM)
        acc = dot(vt0[side], e0.astype(BF)) + dot(vt1[side], e1.astype(BF))
        parts.append(acc / total)
        lse_ref[head] = peak + jnp.log(total)
    o_ref[...] = jnp.concatenate(parts, axis=0).T.astype(BF)


def attend_back_kernel(
    info_ref, q_ref, k0_ref, v0_ref, k1_ref, v1_ref, do_ref, o_ref, lse_ref,
    dq_ref, dk0_ref, dv0_ref, dk1_ref, dv1_ref,
):
    rows = q_ref.shape[0]
    keys = k0_ref.shape[0]
    scale = 1.0 / math.sqrt(HEAD_DIM)
    query = q_ref[...] * jnp.asarray(scale, BF)
    grads = do_ref[...]
    masks = head_masks(rows)
    product = (grads.astype(F32) * o_ref[...].astype(F32)).T
    dq_parts = [None, None]
    for which, (k_ref, v_ref, dk_ref, dv_ref) in enumerate(
        ((k0_ref, v0_ref, dk0_ref, dv0_ref), (k1_ref, v1_ref, dk1_ref, dv1_ref))
    ):
        valid = key_bias(info_ref, which, keys, rows)
        kt = k_ref[...].T
        dk = jnp.zeros(k_ref.shape, F32)
        dv = jnp.zeros(v_ref.shape, F32)
        for head in range(2):
            side = slice(head * HEAD_DIM, (head + 1) * HEAD_DIM)
            masked = jnp.where(masks[head], query, jnp.zeros_like(query))
            gmask = jnp.where(masks[head], grads, jnp.zeros_like(grads))
            delta = jnp.sum(product[side], axis=0, keepdims=True)
            scores = jnp.where(valid, dot(k_ref[...], masked, 1, 1), -1e30)
            probs = jnp.exp(scores - lse_ref[head])
            prob_grad = dot(v_ref[...], gmask, 1, 1)
            score_grad = (probs * (prob_grad - delta)).astype(BF)
            dv += dot(probs.astype(BF), gmask)
            dk += dot(score_grad, masked)
            part = dot(kt[side], score_grad)
            dq_parts[head] = part if which == 0 else dq_parts[head] + part
        dk_ref[...] = dk.astype(dk_ref.dtype)
        dv_ref[...] = dv.astype(dv_ref.dtype)
    dq_ref[...] = jnp.concatenate(dq_parts, axis=0).T * scale


def attend(info, query, own, other):
    rows = query.shape[0]
    pairs = WIDTH // (2 * HEAD_DIM)
    tile = lambda offset: pl.BlockSpec((rows, 2 * HEAD_DIM), lambda i: (0, i + offset))
    return pl.pallas_call(
        attend_kernel,
        grid=(pairs,),
        in_specs=[pl.BlockSpec(memory_space=pltpu.SMEM), tile(0), tile(0), tile(pairs), tile(0), tile(pairs)],
        out_specs=[tile(0), pl.BlockSpec((2, 1, rows), lambda i: (i, 0, 0))],
        out_shape=[
            jax.ShapeDtypeStruct((rows, WIDTH), BF),
            jax.ShapeDtypeStruct((2 * pairs, 1, rows), F32),
        ],
        compiler_params=pltpu.CompilerParams(vmem_limit_bytes=48 * 1024 * 1024),
    )(info, query, own, own, other, other)


def attend_back(info, query, own, other, grads, outputs, lse):
    rows = query.shape[0]
    pairs = WIDTH // (2 * HEAD_DIM)
    tile = lambda offset: pl.BlockSpec((rows, 2 * HEAD_DIM), lambda i: (0, i + offset))
    return pl.pallas_call(
        attend_back_kernel,
        grid=(pairs,),
        in_specs=[
            pl.BlockSpec(memory_space=pltpu.SMEM),
            tile(0), tile(0), tile(pairs), tile(0), tile(pairs), tile(0), tile(0),
            pl.BlockSpec((2, 1, rows), lambda i: (i, 0, 0)),
        ],
        out_specs=[tile(0)] * 5,
        out_shape=[
            jax.ShapeDtypeStruct((rows, WIDTH), F32),
            jax.ShapeDtypeStruct((rows, WIDTH), F32),
            jax.ShapeDtypeStruct((rows, WIDTH), F32),
            jax.ShapeDtypeStruct((rows, WIDTH), BF),
            jax.ShapeDtypeStruct((rows, WIDTH), BF),
        ],
        compiler_params=pltpu.CompilerParams(vmem_limit_bytes=48 * 1024 * 1024),
    )(info, query, own, own, other, other, grads, outputs, lse)


def body(
    mel_frames, noise_frames, text_ids, span_mask, lengths, audio_drop, text_drop, flow_times,
    in_proj, text_table, time_proj, mod_proj, qkv_proj, out_proj, up_proj, down_proj, cotangent,
):
    dp_size = lax.axis_size("dp")
    tp_size = lax.axis_size("tp")
    dp_rank = lax.axis_index("dp")
    tp_rank = lax.axis_index("tp")
    local_rows = mel_frames.shape[0]
    per_group = flow_times.shape[0]
    utt_total = per_group * dp_size
    dp_low = dp_rank % 2
    tp_low = tp_rank % 2
    stay = dp_low == tp_low
    pairs = []
    for d in range(dp_size):
        for t in range(tp_size):
            if d % 2 != t % 2:
                pairs.append((d * tp_size + t, (d ^ 1) * tp_size + (t ^ 1)))

    def swap(values):
        return jnp.where(stay, values, lax.ppermute(values, AXES, pairs))

    sibling = [(d, d ^ 1) for d in range(dp_size)]
    source_dp = dp_rank - dp_low + tp_low
    utterance = source_dp * per_group + tp_rank // 2
    half = dp_low

    def gather(shard, axis):
        size = shard.shape[axis] // dp_size
        piece = lax.dynamic_slice_in_dim(shard, dp_rank * size, size, axis)
        return lax.all_gather(piece, AXES, axis=0, tiled=False).reshape(
            (dp_size, tp_size) + piece.shape
        )

    qkv_full = gather(qkv_proj, 0).transpose(0, 2, 3, 1, 4).reshape(WIDTH, 3 * WIDTH)
    out_full = gather(out_proj, 0).transpose(1, 0, 2, 3).reshape(WIDTH, WIDTH)
    up_full = gather(up_proj, 0).transpose(0, 2, 1, 3).reshape(WIDTH, FFN_DIM)
    down_full = gather(down_proj, 0).transpose(1, 0, 2, 3).reshape(FFN_DIM, WIDTH)

    facts = jnp.stack(
        [flow_times, lengths.astype(F32), 1.0 - audio_drop.astype(F32), 1.0 - text_drop.astype(F32)],
        axis=1,
    )
    facts_all = lax.all_gather(facts, "dp", axis=0, tiled=True)
    sinus = time_features(facts_all[:, 0], TIME_DIM).astype(BF)
    time_embed = dot(sinus, time_proj)
    time_act = jax.nn.silu(time_embed).astype(BF)
    first_utt = (dp_rank - dp_low) * per_group
    act_near = lax.dynamic_slice_in_dim(time_act, first_utt, 2 * per_group, 0)
    mod_cols = dot(act_near, mod_proj)
    modulation = lax.all_gather(mod_cols, "tp", axis=1, tiled=True)
    mod_row = lax.dynamic_slice_in_dim(modulation, utterance - first_utt, 1, 0)
    shift_attn, scale_attn, gate_attn, shift_mlp, scale_mlp, gate_mlp = jnp.split(mod_row, 6, axis=1)
    mine = lax.dynamic_slice_in_dim(facts_all, utterance, 1, 0)
    time_here = mine[0, 0]
    keep_audio = mine[0, 2]
    keep_text = mine[0, 3]
    length = mine[0, 1].astype(jnp.int32)

    mel = swap(mel_frames).astype(F32)
    noise = swap(noise_frames).astype(F32)
    ids = swap(text_ids)
    mask = swap(span_mask)
    out_grad = swap(cotangent).astype(F32)

    keep_cond = (1 - mask).astype(F32)[:, None] * keep_audio
    noisy = (1.0 - time_here) * noise + time_here * mel
    cond = mel * keep_cond
    text_emb = jnp.take(text_table, ids, axis=0).astype(F32) * keep_text
    features = jnp.concatenate([noisy, cond, text_emb], axis=1).astype(BF)
    hidden = dot(features, in_proj)
    norm_a, inv_a = norm_parts(hidden)
    normed_attn = (norm_a * (1.0 + scale_attn) + shift_attn).astype(BF)
    qkv = dot(normed_attn, qkv_full)
    positions = half * local_rows + jnp.arange(local_rows, dtype=jnp.int32)
    cosine, sine = rope_tables(positions)

    def rotate(values):
        return values * cosine + swap_pairs(values) * sine

    def rotate_back(values):
        return values * cosine - swap_pairs(values) * sine

    query = rotate(qkv[:, :WIDTH]).astype(BF)
    own = jnp.concatenate(
        [rotate(qkv[:, WIDTH : 2 * WIDTH]).astype(BF), qkv[:, 2 * WIDTH :].astype(BF)], axis=1
    )
    other = lax.ppermute(own, "dp", sibling)
    info = jnp.stack([length, half * local_rows, (1 - half) * local_rows])
    heads_out, lse = attend(info, query, own, other)
    attn_sum = dot(heads_out, out_full)
    hidden_mid = hidden + gate_attn * attn_sum
    norm_m, inv_m = norm_parts(hidden_mid)
    normed_mlp = (norm_m * (1.0 + scale_mlp) + shift_mlp).astype(BF)
    up_act = dot(normed_mlp, up_full)
    gelu_value, gelu_pull = jax.vjp(lambda inner: jax.nn.gelu(inner, approximate=True), up_act)
    gelu_act = gelu_value.astype(BF)
    mlp_sum = dot(gelu_act, down_full)
    layer_out = swap((hidden_mid + gate_mlp * mlp_sum).astype(BF))

    mlp_grad = (gate_mlp * out_grad).astype(BF)
    down_grad = dot(gelu_act, mlp_grad, 0, 0).astype(BF)
    up_act_grad = gelu_pull(dot(mlp_grad, down_full, 1, 1))[0].astype(BF)
    up_grad = dot(normed_mlp, up_act_grad, 0, 0).astype(BF)
    normed_mlp_grad = dot(up_act_grad, up_full, 1, 1)
    mid_grad = out_grad + norm_back(norm_m, inv_m, scale_mlp, normed_mlp_grad)
    attn_grad = (gate_attn * mid_grad).astype(BF)
    out_proj_grad = dot(heads_out, attn_grad, 0, 0).astype(BF)
    heads_grad = dot(attn_grad, out_full, 1, 1).astype(BF)
    dq, dk_own, dv_own, dk_other, dv_other = attend_back(
        info, query, own, other, heads_grad, heads_out, lse
    )
    dk_in = lax.ppermute(dk_other, "dp", sibling)
    dv_in = lax.ppermute(dv_other, "dp", sibling)
    qkv_act_grad = jnp.concatenate(
        [
            rotate_back(dq).astype(BF),
            rotate_back(dk_own + dk_in.astype(F32)).astype(BF),
            (dv_own + dv_in.astype(F32)).astype(BF),
        ],
        axis=1,
    )
    qkv_grad = dot(normed_attn, qkv_act_grad, 0, 0).astype(BF)
    normed_attn_grad = dot(qkv_act_grad, qkv_full, 1, 1)
    hidden_grad = (mid_grad + norm_back(norm_a, inv_a, scale_attn, normed_attn_grad)).astype(BF)
    in_grad = dot(features, hidden_grad, 0, 0).astype(BF)
    feature_grad = dot(hidden_grad, in_proj, 1, 1)
    mel_grad = swap(
        time_here * feature_grad[:, :MEL_BINS]
        + keep_cond * feature_grad[:, MEL_BINS : 2 * MEL_BINS]
    )
    text_grad = feature_grad[:, 2 * MEL_BINS :].astype(BF) * keep_text.astype(BF)
    one_hot = (ids[:, None] == jnp.arange(VOCABULARY, dtype=jnp.int32)[None, :]).astype(BF)
    table_grad = dot(one_hot, text_grad, 0, 0).astype(BF)

    column_sum = lambda values: jnp.sum(values, axis=0, keepdims=True)
    mod_part = jnp.concatenate(
        [
            column_sum(normed_attn_grad),
            column_sum(normed_attn_grad * norm_a),
            column_sum(attn_sum * mid_grad),
            column_sum(normed_mlp_grad),
            column_sum(normed_mlp_grad * norm_m),
            column_sum(out_grad * mlp_sum),
        ],
        axis=1,
    )
    slot = (jnp.arange(utt_total, dtype=jnp.int32) == utterance).astype(F32)[:, None]
    mod_sums = lax.psum(
        lax.psum_scatter(slot * mod_part, "tp", scatter_dimension=1, tiled=True), "dp"
    ).astype(BF)
    mod_grad = dot(time_act, mod_sums, 0, 0)
    act_grad = lax.psum(dot(mod_sums, mod_proj, 1, 1), "tp")
    embed_grad = jax.vjp(jax.nn.silu, time_embed)[1](act_grad)[0].astype(BF)
    time_rows = TIME_DIM // tp_size
    sinus_share = lax.dynamic_slice_in_dim(sinus, tp_rank * time_rows, time_rows, 1)
    time_grad = dot(sinus_share, embed_grad, 0, 0)

    def reduce(values, axis):
        small = lax.psum_scatter(values, "dp", scatter_dimension=axis + 1, tiled=True)
        piece = lax.psum_scatter(small, "tp", scatter_dimension=0, tiled=True)[0]
        return lax.all_gather(piece, "dp", axis=axis, tiled=True).astype(F32)

    head_cols = WIDTH // tp_size
    unit_cols = FFN_DIM // tp_size
    down_out = reduce(down_grad.reshape(tp_size, unit_cols, WIDTH), 0)
    up_out = reduce(up_grad.reshape(WIDTH, tp_size, unit_cols).transpose(1, 0, 2), 0)
    out_out = reduce(out_proj_grad.reshape(tp_size, head_cols, WIDTH), 0)
    qkv_out = reduce(
        qkv_grad.reshape(WIDTH, 3, tp_size, head_cols).transpose(2, 0, 1, 3), 0
    )
    in_out = reduce(in_grad.reshape(tp_size, in_grad.shape[0] // tp_size, WIDTH), 1)
    table_out = reduce(table_grad.reshape(tp_size, VOCABULARY // tp_size, TEXT_DIM), 0)
    return (
        layer_out, mel_grad, in_out, table_out, time_grad, mod_grad, qkv_out, out_out, up_out, down_out,
    )


def solution(mesh):
    frames = P(("dp", "tp"), None)
    frame = P(("dp", "tp"))
    return jax.shard_map(
        body,
        mesh=mesh,
        in_specs=(
            frames, frames, frame, frame, P("dp"), P("dp"), P("dp"), P("dp"),
            P(), P(), P(), P(None, "tp"), P(None, None, "tp"), P("tp", None), P(None, "tp"),
            P("tp", None), frames,
        ),
        out_specs=(
            frames, frames, P("tp", None), P("tp", None), P("tp", None), P(None, "tp"),
            P(None, None, "tp"), P("tp", None), P(None, "tp"), P("tp", None),
        ),
        check_vma=False,
    )
```

```python
import functools
import math

import jax
import jax.numpy as jnp
from jax import lax
from jax.experimental import pallas as pl
from jax.experimental.pallas import tpu as pltpu
from jax.sharding import PartitionSpec as P

WIDTH = 1024
HEAD_DIM = 64
MEL_BINS = 100
TEXT_DIM = 512
TIME_DIM = 256
VOCABULARY = 2560
FFN_DIM = 2048
AXES = ("dp", "tp")
BF = jnp.bfloat16
F32 = jnp.float32
MESH = pl.DeviceIdType.MESH
VMEM_LIMIT = 60 * 1024 * 1024
ANY = pl.BlockSpec(memory_space=pl.ANY)


def dot(left, right, left_dim=1, right_dim=0):
    return lax.dot_general(
        left, right, (((left_dim,), (right_dim,)), ((), ())), preferred_element_type=F32
    )


def flip(index, bit):
    return index + bit - 2 * bit * ((index // bit) % 2)


class Place:
    def __init__(self):
        self.dp = lax.axis_index("dp")
        self.tp = lax.axis_index("tp")
        self.core = self.dp % 2
        self.x = (self.dp // 2) % 2
        self.y = self.dp // 4

    def plane(self, bit):
        return (flip(self.dp, bit), self.tp)

    def ahead(self, step):
        return (self.dp, (self.tp + step) % 4)


def greet(devices):
    barrier = pltpu.get_barrier_semaphore()
    for device in devices:
        pl.semaphore_signal(barrier, inc=1, device_id=device, device_id_type=MESH)
    pl.semaphore_wait(barrier, len(devices))


def remote(source, target, sems, index, device):
    return pltpu.make_async_remote_copy(
        src_ref=source,
        dst_ref=target,
        send_sem=sems[0].at[index],
        recv_sem=sems[1].at[index],
        device_id=device,
        device_id_type=MESH,
    )


GATHER_COPIES = 13


class Gather:
    def __init__(self, place, shard, full, scratch, slots=(1, 2, 3), part=slice(None)):
        self.p, self.shard, self.full = place, shard, full
        self.sems, self.held = scratch[:2], (scratch[2:] or [None])[0]
        self.slots, self.part = slots, part

    @staticmethod
    def scratch(shape=None):
        dma = pltpu.SemaphoreType.DMA
        held = [] if shape is None else [pltpu.VMEM(shape, BF)]
        return [dma((GATHER_COPIES,)), dma((GATHER_COPIES,))] + held

    def view(self, *index):
        return self.full.at[(slice(self.slots[0], self.slots[-1] + 1), self.part) + index]

    def copy(self, kind):
        p = self.p
        dp = p.dp
        beside, above = flip(dp, 2), flip(dp, 4)
        across = flip(above, 2)
        if kind[0] == "z":
            step = int(kind[1])
            return remote(
                self.shard.at[self.part, dp],
                self.full.at[step, self.part, dp],
                self.sems,
                step - 1,
                p.ahead(4 - step),
            )
        index, bit, sem = {
            "x": ((dp,), 2, 3),
            "y": ((dp,), 4, 4),
            "c": ((dp,), 1, 5),
            "ya": ((beside, 0), 4, 6),
            "xb": ((above, 1), 2, 7),
            "cx": ((beside,), 1, 8),
            "cy": ((above,), 1, 9),
            "cd": ((across,), 1, 10),
        }[kind]
        return remote(self.view(*index), self.view(*index), self.sems, sem, p.plane(bit))

    def fetch(self):
        return pltpu.make_async_copy(self.shard.at[self.part], self.held, self.sems[0].at[11])

    def keep(self):
        return pltpu.make_async_copy(self.held, self.full.at[0, self.part], self.sems[0].at[12])

    def start(self, *kinds):
        for kind in kinds:
            self.copy(kind).start()

    def arrived(self, *kinds):
        for kind in kinds:
            self.copy(kind).wait_recv()

    def lines(self):
        return ["z%d" % slot for slot in self.slots]

    def stage0(self):
        self.start(*self.lines())
        if self.held is not None:
            self.fetch().start()

    def stage1(self):
        if self.held is not None:
            self.fetch().wait()
            self.keep().start()
        self.arrived(*self.lines())
        self.start("x", "y", "c")

    def stage2(self):
        self.arrived("x")
        self.start("ya", "cx")
        self.arrived("y")
        self.start("xb", "cy")

    def stage3(self):
        self.arrived("ya", "xb")
        self.start("cd")

    def stage4(self):
        self.arrived("c", "cx", "cy", "cd")

    def finish(self):
        if self.held is not None:
            self.keep().wait()
        for kind in self.lines() + ["x", "y", "c", "ya", "xb", "cx", "cy", "cd"]:
            self.copy(kind).wait_send()

    stages = property(lambda s: [s.stage0, s.stage1, s.stage2, s.stage3, s.stage4])


REDUCE_COPIES = 18


def add_into(target, source):
    for index in range(4):
        target[index] = (target[index].astype(F32) + source[index].astype(F32)).astype(BF)


class Reduce:
    @staticmethod
    def scratch(rows, columns, held=False):
        r = rows // 16
        shapes = [
            (4, 2, 2, 2, r, columns),
            (4, 2, r, columns),
            (4, 2, r, columns),
            (4, r, columns),
            (4, r, columns),
            (3, 2, r, columns),
            (2, r, columns),
        ]
        if not held:
            shapes.append((4, 2, 2, 2, r, columns))
        return [
            pltpu.SemaphoreType.DMA((REDUCE_COPIES,)),
            pltpu.SemaphoreType.DMA((REDUCE_COPIES,)),
        ] + [pltpu.VMEM(shape, BF) for shape in shapes]

    def __init__(self, place, grads, out, scratch, held=False, absolute=False):
        self.p, self.grads, self.out, self.held = place, grads, out, held
        self.sems = scratch[:2]
        self.rc, self.rx, self.ry, self.ra, self.rb, self.rz, self.fin = scratch[2:9]
        self.acc = grads.at[:, place.core] if held else scratch[9]
        self.first = place.tp if absolute else 0

    def slot(self, step):
        return (self.first + step) % 4

    def copy(self, kind):
        p, acc, out, fin = self.p, self.acc, self.out, self.fin
        c, x, y = p.core, p.x, p.y
        if kind in ("z1", "z2", "z3"):
            step = int(kind[1])
            return remote(
                acc.at[self.slot(step), x, y], self.rz.at[step - 1], self.sems, 4 + step, p.ahead(step)
            )
        table = {
            "c": (lambda: self.grads.at[:, 1 - c], lambda: self.rc, 1, 0),
            "x": (lambda: acc.at[:, 1 - x, :, 0], lambda: self.rx, 2, 1),
            "y": (lambda: acc.at[:, :, 1 - y, 1], lambda: self.ry, 4, 2),
            "ya": (lambda: acc.at[:, x, 1 - y, 0], lambda: self.ra, 4, 3),
            "xb": (lambda: acc.at[:, 1 - x, y, 1], lambda: self.rb, 2, 4),
            "gx": (lambda: fin, lambda: out.at[c, x, y], 2, 8),
            "gy": (lambda: fin, lambda: out.at[c, x, y], 4, 9),
            "gc": (lambda: fin, lambda: out.at[c, x, y], 1, 10),
            "gya": (lambda: out.at[c, 1 - x, y, 0], lambda: out.at[c, 1 - x, y, 0], 4, 11),
            "gxb": (lambda: out.at[c, x, 1 - y, 1], lambda: out.at[c, x, 1 - y, 1], 2, 12),
            "gcx": (lambda: out.at[c, 1 - x, y], lambda: out.at[c, 1 - x, y], 1, 13),
            "gcy": (lambda: out.at[c, x, 1 - y], lambda: out.at[c, x, 1 - y], 1, 14),
            "gcd": (lambda: out.at[c, 1 - x, 1 - y], lambda: out.at[c, 1 - x, 1 - y], 1, 15),
        }
        source, target, bit, index = table[kind]
        return remote(source(), target(), self.sems, index, p.plane(bit))

    def load(self):
        return pltpu.make_async_copy(self.grads.at[:, self.p.core], self.acc, self.sems[0].at[16])

    def keep(self):
        p = self.p
        return pltpu.make_async_copy(self.fin, self.out.at[p.core, p.x, p.y], self.sems[0].at[17])

    def start(self, *kinds):
        for kind in kinds:
            self.copy(kind).start()

    def arrived(self, *kinds):
        for kind in kinds:
            self.copy(kind).wait_recv()

    def stage0(self):
        self.start("c")
        if not self.held:
            self.load().start()

    def stage1(self):
        if not self.held:
            self.load().wait()
        self.arrived("c")
        add_into(self.acc, self.rc)
        self.start("x", "y")

    def stage2(self):
        p = self.p
        self.arrived("x")
        add_into(self.acc.at[:, p.x, :, 0], self.rx)
        self.start("ya")
        self.arrived("y")
        add_into(self.acc.at[:, :, p.y, 1], self.ry)
        self.start("xb")

    def stage3(self):
        p = self.p
        self.arrived("ya")
        add_into(self.acc.at[:, p.x, p.y, 0], self.ra)
        self.arrived("xb")
        add_into(self.acc.at[:, p.x, p.y, 1], self.rb)
        self.start("z1", "z2", "z3")

    def stage4(self):
        p = self.p
        self.arrived("z1", "z2", "z3")
        total = self.acc[self.slot(0), p.x, p.y].astype(F32)
        for step in range(3):
            total += self.rz[step].astype(F32)
        self.fin[...] = total.astype(BF)
        self.keep().start()
        self.start("gx", "gy", "gc")

    def stage5(self):
        self.arrived("gx")
        self.start("gya", "gcx")
        self.arrived("gy")
        self.start("gxb", "gcy")

    def stage6(self):
        self.arrived("gya", "gxb")
        self.start("gcd")

    def stage7(self):
        self.arrived("gc", "gcx", "gcy", "gcd")
        self.keep().wait()
        for kind in (
            "c", "x", "y", "ya", "xb", "z1", "z2", "z3", "gx", "gy", "gc", "gya", "gxb", "gcx", "gcy", "gcd",
        ):
            self.copy(kind).wait_send()

    stages = property(
        lambda s: [s.stage0, s.stage1, s.stage2, s.stage3, s.stage4, s.stage5, s.stage6, s.stage7]
    )


def pipeline(items, first=0):
    stages = [item.stages[first:] for item in items]
    depth = max(len(held) for held in stages)
    beats = []
    for beat in range(len(items) + depth - 1):
        beats.append(
            [held[beat - j] for j, held in enumerate(stages) if 0 <= beat - j < len(held)][::-1]
        )
    return beats


class Flow:
    def __init__(self):
        self.items = []

    def add(self, item):
        self.items.append(list(item.stages))

    def beat(self):
        for stages in self.items[::-1]:
            if stages:
                stages.pop(0)()
        return any(self.items)


def plane_and_line(place):
    return [place.plane(bit) for bit in (1, 2, 4)] + [place.ahead(step) for step in (1, 2, 3)]


def flip3(index, mask):
    for bit in (1, 2, 4):
        if mask & bit:
            index = flip(index, bit)
    return index


def comm_params(collective_id):
    return pltpu.CompilerParams(
        vmem_limit_bytes=VMEM_LIMIT, collective_id=collective_id, has_side_effects=True
    )


def pieces(shape):
    return tuple(shape[:-2]) + (8, 2, shape[-2] // 16, shape[-1])


def blocks(shape):
    return tuple(shape[:-2]) + (2, 2, 2, 2, shape[-2] // 16, shape[-1])


def head_masks(rows):
    lane = lax.broadcasted_iota(jnp.int32, (rows, 2 * HEAD_DIM), 1)
    return [lane < HEAD_DIM, lane >= HEAD_DIM]


def key_bias(length, start, rows):
    position = lax.broadcasted_iota(jnp.int32, (rows, 1), 0) + start
    return jnp.where(position < length, 0.0, -1e30)


def attend_pair(bias0, bias1, q_ref, k0_ref, v0_ref, k1_ref, v1_ref):
    rows = q_ref.shape[0]
    query = q_ref[...] * jnp.asarray(1.0 / math.sqrt(HEAD_DIM), BF)
    masks = head_masks(rows)
    vt0 = v0_ref[...].T
    vt1 = v1_ref[...].T
    parts, totals = [], []
    for head in range(2):
        masked = jnp.where(masks[head], query, jnp.zeros_like(query))
        s0 = dot(k0_ref[...], masked, 1, 1) + bias0
        s1 = dot(k1_ref[...], masked, 1, 1) + bias1
        peak = jnp.maximum(
            jnp.max(s0, axis=0, keepdims=True), jnp.max(s1, axis=0, keepdims=True)
        )
        e0 = jnp.exp(s0 - peak)
        e1 = jnp.exp(s1 - peak)
        total = jnp.sum(e0, axis=0, keepdims=True) + jnp.sum(e1, axis=0, keepdims=True)
        side = slice(head * HEAD_DIM, (head + 1) * HEAD_DIM)
        acc = dot(vt0[side], e0.astype(BF)) + dot(vt1[side], e1.astype(BF))
        parts.append(acc / total)
        totals.append(peak + jnp.log(total))
    return jnp.concatenate(parts, axis=0).T.astype(BF), totals


def attend_back_pair(info_ref, q_ref, k0_ref, v0_ref, k1_ref, v1_ref, do_ref, o_ref, lse_ref):
    rows = q_ref.shape[0]
    keys = k0_ref.shape[0]
    scale = 1.0 / math.sqrt(HEAD_DIM)
    query = q_ref[...] * jnp.asarray(scale, BF)
    grads = do_ref[...]
    masks = head_masks(rows)
    product = (grads.astype(F32) * o_ref[...].astype(F32)).T
    dq_parts = [None, None]
    results = []
    for which, (k_ref, v_ref) in enumerate(((k0_ref, v0_ref), (k1_ref, v1_ref))):
        bias = key_bias(info_ref[0], info_ref[1 + which], keys)
        kt = k_ref[...].T
        dk = jnp.zeros(k_ref.shape, F32)
        dv = jnp.zeros(v_ref.shape, F32)
        for head in range(2):
            side = slice(head * HEAD_DIM, (head + 1) * HEAD_DIM)
            masked = jnp.where(masks[head], query, jnp.zeros_like(query))
            gmask = jnp.where(masks[head], grads, jnp.zeros_like(grads))
            delta = jnp.sum(product[side], axis=0, keepdims=True)
            scores = dot(k_ref[...], masked, 1, 1) + bias
            probs = jnp.exp(scores - lse_ref[head])
            prob_grad = dot(v_ref[...], gmask, 1, 1)
            score_grad = (probs * (prob_grad - delta)).astype(BF)
            dv += dot(probs.astype(BF), gmask)
            dk += dot(score_grad, masked)
            part = dot(kt[side], score_grad)
            dq_parts[head] = part if which == 0 else dq_parts[head] + part
        results.append((dk, dv))
    return jnp.concatenate(dq_parts, axis=0).T * scale, results


def turn(values, cosine, sine):
    lane = lax.broadcasted_iota(jnp.int32, values.shape, 1)
    width = values.shape[1]
    other = jnp.where(
        lane % 2 == 0, pltpu.roll(values, width - 1, 1), pltpu.roll(values, 1, 1)
    )
    return values * cosine + other * sine


def attend_kernel(info_ref, q, k0, v0, k1, v1, o_ref, lse_ref):
    keys = k0.shape[0]
    biases = [key_bias(info_ref[0], info_ref[1 + which], keys) for which in range(2)]
    o_ref[...], (lse_ref[0], lse_ref[1]) = attend_pair(*biases, q, k0, v0, k1, v1)


def attend(info, query, own, other):
    rows = query.shape[0]
    pairs = WIDTH // (2 * HEAD_DIM)
    tile = pl.BlockSpec((rows, 2 * HEAD_DIM), lambda i: (0, i))
    return pl.pallas_call(
        attend_kernel,
        grid=(pairs,),
        in_specs=[pl.BlockSpec(memory_space=pltpu.SMEM)] + [tile] * 5,
        out_specs=[tile, pl.BlockSpec((2, 1, rows), lambda i: (i, 0, 0))],
        out_shape=[
            jax.ShapeDtypeStruct((rows, WIDTH), BF),
            jax.ShapeDtypeStruct((2 * pairs, 1, rows), F32),
        ],
        compiler_params=pltpu.CompilerParams(vmem_limit_bytes=VMEM_LIMIT),
        name="attend",
    )(info, query, *own, *other)


def attend_back_kernel(reduces, spread, info_ref, q, k0, v0, k1, v1, do, o, lse, cos, sin, *refs):
    grads = refs[:reduces]
    dq_ref, dk_ref, dv_ref, dk_in, dv_in = refs[reduces : reduces + 5]
    outs = refs[reduces + 5 : 2 * reduces + 5]
    sent, send_sems, recv_sems = refs[2 * reduces + 5 : 2 * reduces + 8]
    scratch = refs[2 * reduces + 8 :]
    step = pl.program_id(0)
    last = pl.num_programs(0) - 1
    width = 2 * HEAD_DIM
    sibling = (flip(lax.axis_index("dp"), 1), lax.axis_index("tp"))
    beats = []
    if reduces:
        place = Place()
        items = []
        for j in range(reduces):
            for h in range(grads[j].shape[1]):
                index = 10 * len(items)
                items.append(
                    Reduce(place, grads[j].at[:, h], outs[j].at[h], scratch[index : index + 10])
                )
        beats = pipeline(items)

    @pl.when(step == 0)
    def _():
        greet(plane_and_line(place) if reduces else [sibling])

    for index, beat in enumerate(beats):
        if spread[index] <= 7:

            @pl.when(step == spread[index])
            def _(beat=beat):
                for stage in beat:
                    stage()

    dq, results = attend_back_pair(info_ref, q, k0, v0, k1, v1, do, o, lse)
    dq_ref[...] = turn(dq, cos[...], -sin[...]).astype(BF)
    dk_ref[...], dv_ref[...] = results[0]

    def copies(index):
        columns = pl.ds(pl.multiple_of(index * width, width), width)
        made = []
        for kind, target in ((0, dk_in), (1, dv_in)):
            made.append(
                pltpu.make_async_remote_copy(
                    src_ref=sent.at[kind, index],
                    dst_ref=target.at[:, columns],
                    send_sem=send_sems.at[kind, index],
                    recv_sem=recv_sems.at[kind, index],
                    device_id=sibling,
                    device_id_type=MESH,
                )
            )
        return made

    sent[0, step] = results[1][0].astype(BF)
    sent[1, step] = results[1][1].astype(BF)
    for copy in copies(step):
        copy.start()

    @pl.when(step == last)
    def _():
        for index, beat in enumerate(beats):
            if spread[index] > 7:
                for stage in beat:
                    stage()
        for index in range(WIDTH // width):
            for copy in copies(index):
                copy.wait()


def attend_back(info, query, own, other, heads_grad, outputs, lse, cosine, sine, grads):
    rows = query.shape[0]
    pairs = WIDTH // (2 * HEAD_DIM)
    width = 2 * HEAD_DIM
    tile = pl.BlockSpec((rows, width), lambda i: (0, i))
    fixed = pl.BlockSpec((rows, width), lambda i: (0, 0))
    reduces = len(grads)
    dma = pltpu.SemaphoreType.DMA
    spread = (0, 1, 2, 4, 5, 6, 7) + (8,) * 8
    scratch = []
    for grad in grads:
        for _ in range(grad.shape[1]):
            scratch += Reduce.scratch(*grad.shape[2:])
    outs = pl.pallas_call(
        functools.partial(attend_back_kernel, reduces, spread),
        grid=(pairs,),
        in_specs=[pl.BlockSpec(memory_space=pltpu.SMEM)]
        + [tile] * 7
        + [pl.BlockSpec((2, 1, rows), lambda i: (i, 0, 0)), fixed, fixed]
        + [ANY] * reduces,
        out_specs=[tile] * 3 + [ANY] * 2 + [ANY] * reduces,
        out_shape=[
            jax.ShapeDtypeStruct((rows, WIDTH), BF),
            jax.ShapeDtypeStruct((rows, WIDTH), F32),
            jax.ShapeDtypeStruct((rows, WIDTH), F32),
            jax.ShapeDtypeStruct((rows, WIDTH), BF),
            jax.ShapeDtypeStruct((rows, WIDTH), BF),
        ]
        + [jax.ShapeDtypeStruct(blocks(g.shape[1:]), BF) for g in grads],
        scratch_shapes=[
            pltpu.VMEM((2, pairs, rows, width), BF),
            dma((2, pairs)),
            dma((2, pairs)),
        ]
        + scratch,
        compiler_params=comm_params(3),
        name="attend_back",
    )(
        info, query, *own, *other, heads_grad, outputs, lse, cosine, sine,
        *[g.reshape(blocks(g.shape)) for g in grads],
    )
    return outs[:5], [o.reshape((-1,) + g.shape[3:]) for o, g in zip(outs[5:], grads)]


def forward_kernel(
    mel, noise, extra, facts, mods, cot, qkv, out_w, up_w, down_w, table, mel_w, text_w, cos, sin,
    facts_all, mod_row, mine_out, extra_out, cot_in, qkv_full, out_full, up_full, down_full,
    sum_out, mid_out, normed_out, feats_out, text_out, hidden_out, x_out, q_out, k_out, v_out, ki_out, vi_out, heads_out, lse_out,
    mel_in, noise_in, extra_in, facts_v, mods_v, table_v, mel_wv, text_wv, cos_v, sin_v,
    feats_v, text_v, hidden_v, x_v, q_v, k_v, v_v, ki_v, vi_v, heads_v, lse_v, full_v, outw_v, sum_v, mid_v, normed_v, rows_v, mine_v,
    load_sems, save_sems, fact_sends, fact_recvs, mod_sends, mod_recvs, swap_sends, swap_recvs,
    kv_sends, kv_recvs, *scratch
):
    step = pl.program_id(0)
    last = pl.num_programs(0) - 1
    place = Place()
    dp, tp = place.dp, place.tp
    rows = x_v.shape[0]
    width = full_v.shape[-1]
    partner = (flip(dp, 1), flip(tp, 1))
    sibling = place.plane(1)
    moves = place.core != tp % 2
    stays = jnp.logical_not(moves)
    gathers = [
        Gather(place, qkv, full_v, scratch[2 * j : 2 * j + 2], (j + 1,)) for j in range(3)
    ] + [Gather(place, out_w, outw_v, scratch[6:8])] + [
        Gather(place, shard, full, scratch[8 + 3 * j : 11 + 3 * j], part=j % 2)
        for j, (shard, full) in enumerate(
            ((up_w, up_full), (up_w, up_full), (down_w, down_full), (down_w, down_full))
        )
    ]
    swaps = [
        remote(source, target, (swap_sends, swap_recvs), index, partner)
        for index, (source, target) in enumerate(
            ((mel, mel_in), (noise, noise_in), (extra, extra_in), (cot, cot_in))
        )
    ]
    own_qkv = pltpu.make_async_copy(qkv, full_v.at[0], load_sems.at[0])
    own_out = pltpu.make_async_copy(out_w, outw_v.at[0], load_sems.at[11])
    loads = [
        pltpu.make_async_copy(source, target, load_sems.at[index + 1])
        for index, (source, target) in enumerate(
            (
                (facts, facts_v.at[dp]),
                (mods, mods_v.at[place.core, tp]),
                (table, table_v),
                (mel_w, mel_wv),
                (text_w, text_wv),
                (cos, cos_v),
                (sin, sin_v),
            )
        )
    ]
    frames_own = [
        pltpu.make_async_copy(source, target, load_sems.at[8 + index])
        for index, (source, target) in enumerate(((mel, mel_in), (noise, noise_in), (extra, extra_in)))
    ]
    early_saves = [(feats_v, feats_out), (text_v, text_out), (hidden_v, hidden_out), (x_v, x_out)]
    early_saves += [(facts_v, facts_all), (rows_v, mod_row), (mine_v, mine_out), (extra_in, extra_out)]
    late_saves = [(q_v, q_out), (k_v, k_out), (v_v, v_out), (ki_v, ki_out), (vi_v, vi_out)]
    late_saves += [(full_v, qkv_full), (outw_v, out_full)]
    final_saves = [(heads_v, heads_out), (lse_v, lse_out)]
    final_saves += [(sum_v, sum_out), (mid_v, mid_out), (normed_v, normed_out)]
    saves = [
        pltpu.make_async_copy(source, target, save_sems.at[index])
        for index, (source, target) in enumerate(early_saves + late_saves + final_saves)
    ]
    n_early, n_late = len(early_saves), len(late_saves)

    def kv_copies(rank):
        columns = pl.ds(pl.multiple_of(rank * width, width), width)
        return [
            remote(
                source.at[:, columns], target.at[:, columns],
                (kv_sends.at[kind], kv_recvs.at[kind]), rank, sibling,
            )
            for kind, (source, target) in enumerate(((k_v, ki_v), (v_v, vi_v)))
        ]

    @pl.when(step == 0)
    def _():
        for copy in loads:
            copy.start()
        own_qkv.start()
        own_out.start()
        greet(
            [(flip3(dp, k), tp) for k in range(1, 8)]
            + [place.ahead(step) for step in (1, 2, 3)]
            + [(flip(dp, 1), (tp + step) % 4) for step in (1, 2, 3)]
        )
        fact_copies = [
            remote(facts, facts_v.at[dp], (fact_sends, fact_recvs), k - 1, (flip3(dp, k), tp))
            for k in range(1, 8)
        ]
        mod_copies = []
        for index in range(1, 8):
            target = (flip(dp, 1) if index >= 4 else dp, (tp + index) % 4)
            mod_copies.append(
                remote(mods, mods_v.at[place.core, tp], (mod_sends, mod_recvs), index - 1, target)
            )
        @pl.when(moves)
        def _():
            for copy in swaps[:3]:
                copy.start()

        @pl.when(stays)
        def _():
            for copy in frames_own:
                copy.start()

        for copy in fact_copies + mod_copies:
            copy.start()
        gathers[0].stage0()

        @pl.when(moves)
        def _():
            for copy in swaps[:3]:
                copy.wait()

        @pl.when(stays)
        def _():
            for copy in frames_own:
                copy.wait()

        gathers[1].stage0()
        gathers[0].stage1()
        for copy in loads[:2] + fact_copies + mod_copies:
            copy.wait()
        gathers[2].stage0()
        pick = lambda pair: jnp.where(tp // 2 == 0, pair[0:1], pair[1:2])
        source = dp - place.core + tp % 2
        mine = pick(facts_v[source, 0:8, TIME_DIM : TIME_DIM + 128])
        mine_v[...] = jnp.broadcast_to(mine, mine_v.shape)
        time_here, keep_audio, keep_text = mine[:, 0:1], mine[:, 2:3], mine[:, 3:4]
        chunk = WIDTH // 2
        per_rank = mods_v.shape[-1] // chunk
        for index in range(12):
            lane = index % per_rank * chunk
            rows_v[index // 2 : index // 2 + 1, index % 2 * chunk : (index % 2 + 1) * chunk] = pick(
                mods_v[tp % 2, index // per_rank, 0:8, lane : lane + chunk]
            )
        bins = mel_wv.shape[0] // 2
        extras = extra_in[...].astype(F32)
        mel_f = mel_in[...].astype(F32)
        keep_cond = (1.0 - extras[0:1]) * keep_audio
        feats_v[0:bins] = ((1.0 - time_here) * noise_in[...].astype(F32) + time_here * mel_f).astype(BF)
        feats_v[bins : 2 * bins] = (mel_f * keep_cond).astype(BF)
        ids = (extras[1:2] * 256.0 + extras[2:3]).astype(jnp.int32)
        ids = jnp.broadcast_to(ids, (8, rows)).T[:, 0:1]
        for copy in loads[2:]:
            copy.wait()
        vocabulary = table_v.shape[0]
        span = 512
        for first in range(0, vocabulary, span):
            lane = lax.broadcasted_iota(jnp.int32, (rows, span), 1) + first
            one_hot = (lane == ids).astype(F32).astype(BF)
            term = dot(one_hot, table_v[first : first + span])
            if first == 0:
                hidden_v[:, :TEXT_DIM] = term
            else:
                hidden_v[:, :TEXT_DIM] += term
        text_v[...] = (hidden_v[:, :TEXT_DIM] * keep_text).astype(BF)
        gathers[1].stage1()
        gathers[3].stage0()
        hidden_v[...] = dot(text_v[...], text_wv[...]) + dot(feats_v[...], mel_wv[...], 0, 0)
        gathers[0].stage2()
        block = 128
        for first in range(0, rows, block):
            values = hidden_v[first : first + block]
            normed, _ = norm_parts(values)
            x_v[first : first + block] = (normed * (1.0 + rows_v[1:2]) + rows_v[0:1]).astype(BF)
        gathers[2].stage1()
        gathers[4].stage0()
        gathers[5].stage0()
        for copy in saves[:n_early]:
            copy.start()
        own_qkv.wait()

    g = gathers
    schedule = {
        1: [g[0].stage3, g[1].stage2, g[3].stage1, g[6].stage0, g[7].stage0],
        2: [g[0].stage4, g[2].stage2, g[1].stage3],
        3: [g[3].stage2, g[2].stage3, g[4].stage1],
        4: [g[1].stage4, g[5].stage1, g[3].stage3],
        5: [g[2].stage4, g[4].stage2],
        6: [g[3].stage4, g[6].stage1, g[4].stage3, g[5].stage2],
        7: [g[7].stage1, g[5].stage3],
    }
    for index, stages in schedule.items():

        @pl.when(step == index)
        def _(stages=stages):
            for stage in stages:
                stage()

    @pl.when(step % 2 == 0)
    def _():
        rank = step // 2
        columns = pl.ds(pl.multiple_of(rank * width, width), width)
        x = x_v[...]
        wide = lambda v: jnp.concatenate([v, v], axis=1)
        cosine, sine = wide(cos_v[...]), wide(sin_v[...])
        weight = lambda part: full_v[rank, part].reshape(WIDTH, width)
        k_v[:, columns] = turn(dot(x, weight(1)), cosine, sine).astype(BF)
        v_v[:, columns] = dot(x, weight(2)).astype(BF)
        for copy in kv_copies(rank):
            copy.start()
        q_v[:, columns] = turn(dot(x, weight(0)), cosine, sine).astype(BF)

        @pl.when(jnp.logical_and(step == 4, moves))
        def _():
            swaps[3].start()

        for copy in kv_copies(rank):
            copy.wait()

    @pl.when(step == last - 1)
    def _():
        own_out.wait()
        for copy in saves[n_early : n_early + n_late]:
            copy.start()

    length = mine_v[0:1, 1:2].astype(jnp.int32)
    biases = [
        key_bias(length, place.core * rows, rows),
        key_bias(length, (1 - place.core) * rows, rows),
    ]
    columns = pl.ds(pl.multiple_of(step * 2 * HEAD_DIM, 2 * HEAD_DIM), 2 * HEAD_DIM)
    output, totals = attend_pair(
        *biases, *[ref.at[:, columns] for ref in (q_v, k_v, v_v, ki_v, vi_v)]
    )
    heads_v[:, columns] = output
    lse_v[2 * step], lse_v[2 * step + 1] = totals

    @pl.when(step == last)
    def _():
        g[6].stage2()
        sum_v[...] = dot(heads_v[...], outw_v[...].reshape(WIDTH, WIDTH))
        g[7].stage2()
        block = 128
        for first in range(0, rows, block):
            here = slice(first, first + block)
            values = hidden_v[here] + rows_v[2:3] * sum_v[here]
            mid_v[here] = values
            normed, _ = norm_parts(values)
            normed_v[here] = (normed * (1.0 + rows_v[4:5]) + rows_v[3:4]).astype(BF)
        for copy in saves[n_early + n_late :]:
            copy.start()
        g[6].stage3()
        g[7].stage3()
        g[4].stage4()
        g[5].stage4()
        g[6].stage4()
        g[7].stage4()

        @pl.when(moves)
        def _():
            swaps[3].wait()

        for gather in gathers:
            gather.finish()
        for copy in saves:
            copy.wait()


def forward(mel, noise, extra, facts, mods, cot, qkv, out_w, up_w, down_w, table, mel_w, text_w, cosine, sine):
    rows = cot.shape[0]
    width = qkv.shape[2]
    dma = pltpu.SemaphoreType.DMA
    shape = lambda s, t=BF: jax.ShapeDtypeStruct(s, t)
    full = (4, 3) + pieces(qkv.shape)[1:]
    parted = [
        out_w.reshape((1,) + pieces(out_w.shape)),
        up_w.reshape((2,) + pieces((up_w.shape[0] // 2, up_w.shape[1]))),
        down_w.reshape((2,) + pieces((down_w.shape[0] // 2, down_w.shape[1]))),
    ]
    head_count = WIDTH // HEAD_DIM
    frames = (rows, WIDTH)
    feats = (mel_w.shape[0], rows)
    text = (rows, TEXT_DIM)
    all_facts = (8,) + facts.shape
    lse = (head_count, 1, rows)
    scratch = Gather.scratch() * 4
    for w in parted[1:]:
        scratch += Gather.scratch(w.shape[1:]) * 2
    outs = pl.pallas_call(
        forward_kernel,
        grid=(WIDTH // (2 * HEAD_DIM),),
        in_specs=[ANY] * 15,
        out_specs=[ANY] * 23,
        out_shape=[
            shape(all_facts, F32), shape((8, WIDTH), F32), shape((8, 128), F32), shape(extra.shape),
            shape(cot.shape), shape(full),
        ]
        + [shape((4,) + w.shape) for w in parted]
        + [shape(frames, F32), shape(frames, F32), shape(frames)]
        + [shape(feats), shape(text), shape(frames, F32), shape(frames)]
        + [shape(frames)] * 6
        + [shape(lse, F32)],
        scratch_shapes=[
            *[pltpu.VMEM(v.shape, BF) for v in (mel, noise, extra)], pltpu.VMEM(all_facts, F32),
            pltpu.VMEM((2, 4) + mods.shape, F32), pltpu.VMEM(table.shape, BF),
            pltpu.VMEM(mel_w.shape, BF), pltpu.VMEM(text_w.shape, BF),
            pltpu.VMEM(cosine.shape, F32), pltpu.VMEM(sine.shape, F32),
            pltpu.VMEM(feats, BF), pltpu.VMEM(text, BF), pltpu.VMEM(frames, F32), pltpu.VMEM(frames, BF),
        ]
        + [pltpu.VMEM(frames, BF)] * 6
        + [
            pltpu.VMEM(lse, F32), pltpu.VMEM(full, BF), pltpu.VMEM((4,) + parted[0].shape, BF),
            pltpu.VMEM(frames, F32), pltpu.VMEM(frames, F32), pltpu.VMEM(frames, BF),
            pltpu.VMEM((8, WIDTH), F32), pltpu.VMEM((8, 128), F32),
            dma((12,)), dma((20,)), dma((7,)), dma((7,)), dma((7,)), dma((7,)), dma((4,)), dma((4,)),
            dma((2, 4)), dma((2, 4)),
        ]
        + scratch,
        compiler_params=comm_params(0),
        name="forward",
    )(
        mel, noise, extra, facts, mods, cot, qkv.reshape(pieces(qkv.shape)), *parted, table, mel_w,
        text_w, cosine, sine,
    )
    outs = list(outs)
    outs[5] = outs[5].reshape(4, 3, WIDTH, width)
    outs[6:9] = [f.reshape((4,) + w.shape) for f, w in zip(outs[6:9], (out_w, up_w, down_w))]
    return outs


def qkv_kernel(x_ref, w_ref, cos_ref, sin_ref, q_ref, k_ref, v_ref, ko_ref, vo_ref, sent, send_sems, recv_sems):
    step = pl.program_id(0)
    last = pl.num_programs(0) - 1
    width = q_ref.shape[1]
    sibling = (flip(lax.axis_index("dp"), 1), lax.axis_index("tp"))

    def copies(index):
        columns = pl.ds(pl.multiple_of(index * width, width), width)
        return [
            pltpu.make_async_remote_copy(
                src_ref=sent.at[kind, index],
                dst_ref=target.at[:, columns],
                send_sem=send_sems.at[kind, index],
                recv_sem=recv_sems.at[kind, index],
                device_id=sibling,
                device_id_type=MESH,
            )
            for kind, target in ((0, ko_ref), (1, vo_ref))
        ]

    @pl.when(step == 0)
    def _():
        greet([sibling])

    x = x_ref[...]
    key = turn(dot(x, w_ref[0, 1]), cos_ref[...], sin_ref[...]).astype(BF)
    value = dot(x, w_ref[0, 2]).astype(BF)
    k_ref[...] = key
    v_ref[...] = value
    sent[0, step] = key
    sent[1, step] = value
    for copy in copies(step):
        copy.start()
    q_ref[...] = turn(dot(x, w_ref[0, 0]), cos_ref[...], sin_ref[...]).astype(BF)

    @pl.when(step == last)
    def _():
        for index in range(WIDTH // width):
            for copy in copies(index):
                copy.wait()


def project_qkv(x, weights, cosine, sine):
    rows = x.shape[0]
    ranks, width = weights.shape[0], weights.shape[3]
    tile = pl.BlockSpec((rows, width), lambda r: (0, r))
    whole = lambda shape: pl.BlockSpec(shape, lambda r: (0, 0))
    dma = pltpu.SemaphoreType.DMA
    return pl.pallas_call(
        qkv_kernel,
        grid=(ranks,),
        in_specs=[
            whole(x.shape),
            pl.BlockSpec((1, 3, WIDTH, width), lambda r: (r, 0, 0, 0)),
            whole((rows, width)),
            whole((rows, width)),
        ],
        out_specs=[tile] * 3 + [ANY] * 2,
        out_shape=[jax.ShapeDtypeStruct((rows, WIDTH), BF)] * 5,
        scratch_shapes=[pltpu.VMEM((2, ranks, rows, width), BF), dma((2, ranks)), dma((2, ranks))],
        compiler_params=comm_params(1),
        name="project_qkv",
    )(x, weights, cosine, sine)


def qkv_back_kernel(
    x_ref, w_ref, cos_ref, sin_ref, dq_ref, dk_ref, dv_ref, dki_ref, dvi_ref, grad_ref, dx_ref, xt
):
    step = pl.program_id(0)

    @pl.when(step == 0)
    def _():
        xt[...] = x_ref[...].T

    dq = dq_ref[...]
    dk = turn(dk_ref[...] + dki_ref[...].astype(F32), cos_ref[...], -sin_ref[...]).astype(BF)
    dv = (dv_ref[...] + dvi_ref[...].astype(F32)).astype(BF)
    total = None
    for part, grad in enumerate((dq, dk, dv)):
        grad_ref[0, part] = dot(xt[...], grad).astype(BF)
        term = dot(grad, w_ref[0, part], 1, 1)
        total = term if total is None else total + term

    @pl.when(step == 0)
    def _():
        dx_ref[...] = total

    @pl.when(step > 0)
    def _():
        dx_ref[...] += total


def project_qkv_back(x, weights, cosine, sine, dq, dk, dv, dk_in, dv_in):
    rows = x.shape[0]
    ranks, width = weights.shape[0], weights.shape[3]
    tile = pl.BlockSpec((rows, width), lambda r: (0, r))
    whole = lambda shape: pl.BlockSpec(shape, lambda r: (0, 0))
    wide = pl.BlockSpec((1, 3, WIDTH, width), lambda r: (r, 0, 0, 0))
    return pl.pallas_call(
        qkv_back_kernel,
        grid=(ranks,),
        in_specs=[whole(x.shape), wide, whole((rows, width)), whole((rows, width))] + [tile] * 5,
        out_specs=[wide, whole((rows, WIDTH))],
        out_shape=[
            jax.ShapeDtypeStruct(weights.shape, BF),
            jax.ShapeDtypeStruct((rows, WIDTH), F32),
        ],
        scratch_shapes=[pltpu.VMEM((WIDTH, rows), BF)],
        compiler_params=pltpu.CompilerParams(vmem_limit_bytes=VMEM_LIMIT),
        name="project_qkv_back",
    )(x, weights, cosine, sine, dq, dk, dv, dk_in, dv_in)


def mlp_kernel(x_ref, g_ref, wu_ref, wd_ref, y_ref, dx_ref, du_ref, dd_ref, xt):
    step = pl.program_id(0)

    @pl.when(step == 0)
    def _():
        xt[...] = x_ref[...].T

    up = dot(x_ref[...], wu_ref[0])
    root = math.sqrt(2.0 / math.pi)
    square = up * up
    bent = jnp.tanh(root * (up + 0.044715 * up * square))
    half = 0.5 * (1.0 + bent)
    slope = half + 0.5 * up * (1.0 - bent * bent) * root * (1.0 + 3 * 0.044715 * square)
    act = (up * half).astype(BF)
    grad = g_ref[...]
    up_grad = (dot(grad, wd_ref[0], 1, 1) * slope).astype(BF)
    dd_ref[0] = dot(act, grad, 0, 0).astype(BF)
    du_ref[0] = dot(xt[...], up_grad).astype(BF)
    y = dot(act, wd_ref[0])
    dx = dot(up_grad, wu_ref[0], 1, 1)

    @pl.when(step == 0)
    def _():
        y_ref[...] = y
        dx_ref[...] = dx

    @pl.when(step > 0)
    def _():
        y_ref[...] += y
        dx_ref[...] += dx


def mlp(x, grad, up_full, down_full):
    rows = x.shape[0]
    ranks, _, units = up_full.shape
    whole = pl.BlockSpec((rows, WIDTH), lambda r: (0, 0))
    up_spec = pl.BlockSpec((1, WIDTH, units), lambda r: (r, 0, 0))
    down_spec = pl.BlockSpec((1, units, WIDTH), lambda r: (r, 0, 0))
    return pl.pallas_call(
        mlp_kernel,
        grid=(ranks,),
        in_specs=[whole, whole, up_spec, down_spec],
        out_specs=[whole, whole, up_spec, down_spec],
        out_shape=[
            jax.ShapeDtypeStruct((rows, WIDTH), F32),
            jax.ShapeDtypeStruct((rows, WIDTH), F32),
            jax.ShapeDtypeStruct(up_full.shape, BF),
            jax.ShapeDtypeStruct(down_full.shape, BF),
        ],
        scratch_shapes=[pltpu.VMEM((WIDTH, rows), BF)],
        compiler_params=pltpu.CompilerParams(vmem_limit_bytes=VMEM_LIMIT),
        name="mlp",
    )(x, grad, up_full, down_full)


def tail_kernel(
    info_ref, x_ref, w_ref, cos_ref, sin_ref, dq_ref, dk_ref, dv_ref, dki_ref, dvi_ref,
    value_ref, mid_ref, scale_ref, feat_ref, mel_w_ref, text_w_ref, ids_ref, keep_ref,
    mod_in_ref, proj_ref,
    sums_ref, act_ref, mel_ref, mel_in_ref, qkv_out, misc_out,
    xt, weights, total_ref, hidden_ref, text_ref, qkv_grads, misc_grads,
    mod_ref, line, every, part_ref, load_sems, line_sends, line_recvs, every_sends, every_recvs,
    act_sends, act_recvs, mel_sems, *scratch
):
    place = Place()
    dp, tp = place.dp, place.tp
    partner = (flip(dp, 1), flip(tp, 1))
    moves = place.core != tp % 2
    rows = x_ref.shape[0]
    ranks, width = w_ref.shape[0], w_ref.shape[3]
    loads = [
        pltpu.make_async_copy(w_ref.at[:, part], weights.at[part % 2], load_sems.at[part])
        for part in range(3)
    ]
    loads[0].start()
    loads[1].start()
    greet(
        [(flip3(dp, k), tp) for k in range(1, 8)]
        + [place.ahead(step) for step in (1, 2, 3)]
        + [(flip(dp, 1), flip(tp, 1))]
    )
    size = 9
    items = [
        Reduce(place, qkv_grads.at[part], qkv_out.at[part], scratch[size * part : size * part + size], True)
        for part in range(3)
    ] + [
        Reduce(
            place, misc_grads.at[h], misc_out.at[h],
            scratch[size * (3 + h) : size * (4 + h)], True, True,
        )
        for h in range(2)
    ]
    flow = Flow()
    xt[...] = x_ref[...].T
    for part in range(3):
        loads[part].wait()
        for rank in range(ranks):
            side = slice(rank * width, (rank + 1) * width)
            if part == 0:
                grad = dq_ref[:, side]
            elif part == 1:
                grad = turn(
                    dk_ref[:, side] + dki_ref[:, side].astype(F32), cos_ref[...], -sin_ref[...]
                ).astype(BF)
            else:
                grad = (dv_ref[:, side] + dvi_ref[:, side].astype(F32)).astype(BF)
            qkv_grads[part, rank] = (
                dot(xt[...], grad).astype(BF).reshape(qkv_grads.shape[2:])
            )
            term = dot(grad, weights[part % 2, rank], 1, 1)
            if part == 0 and rank == 0:
                total_ref[...] = term
            else:
                total_ref[...] += term
        if part == 0:
            loads[2].start()
        flow.add(items[part])
        flow.beat()

    normed_grad = total_ref[...]
    normed, inverse = norm_parts(value_ref[...])
    inner = normed_grad * (1.0 + scale_ref[...])
    first = jnp.mean(inner, axis=-1, keepdims=True)
    second = jnp.mean(inner * normed, axis=-1, keepdims=True)
    hidden_ref[...] = (
        mid_ref[...] + inverse * (inner - first - normed * second)
    ).astype(BF)
    chunks = mod_ref.shape[1]
    lanes = mod_ref.shape[2]
    mod_ref[...] = mod_in_ref[...]
    for index, sums in enumerate(
        (jnp.sum(normed_grad, axis=0, keepdims=True), jnp.sum(normed_grad * normed, axis=0, keepdims=True))
    ):
        for chunk in range(WIDTH // lanes):
            row = index * (WIDTH // lanes) + chunk
            mod_ref[row // chunks, row % chunks : row % chunks + 1, :] = sums[
                :, chunk * lanes : (chunk + 1) * lanes
            ]
    line_copies = [
        remote(
            mod_ref.at[(tp + step) % 4], line.at[tp], (line_sends, line_recvs), step - 1, place.ahead(step)
        )
        for step in (1, 2, 3)
    ]
    every_copies = [
        remote(line, every.at[dp], (every_sends, every_recvs), k - 1, (flip3(dp, k), tp))
        for k in range(1, 8)
    ]
    act_copies = [
        remote(part_ref, act_ref.at[tp], (act_sends, act_recvs), step - 1, place.ahead(step))
        for step in (1, 2, 3)
    ]
    for copy in line_copies:
        copy.start()
    line[tp] = mod_ref[tp]
    flow.beat()

    hidden = hidden_ref[...]
    text_ref[...] = dot(hidden, text_w_ref[...], 1, 1).astype(BF) * info_ref[2].astype(BF)
    table_rows = VOCABULARY // ranks
    split = misc_grads.shape[-2] * 16
    block = misc_grads.shape[2:]
    for rank in range(ranks):
        row = lax.broadcasted_iota(jnp.int32, (split, rows), 0) + rank * table_rows
        one_hot = (row == ids_ref[...]).astype(F32).astype(BF)
        misc_grads[0, rank] = dot(one_hot, text_ref[...]).astype(BF).reshape(block)
    flow.add(items[3])
    flow.beat()
    for copy in line_copies:
        copy.wait()
    every[dp] = line[...]
    for copy in every_copies:
        copy.start()
    feat_rows = feat_ref.shape[1] // ranks
    rest = table_rows - split
    for rank in range(ranks):
        row = lax.broadcasted_iota(jnp.int32, (rest, rows), 0) + (rank * table_rows + split)
        one_hot = (row == ids_ref[...]).astype(F32).astype(BF)
        table = dot(one_hot, text_ref[...]).astype(BF)
        share = dot(feat_ref[:, rank * feat_rows : (rank + 1) * feat_rows], hidden, 0, 0).astype(BF)
        misc_grads[1, rank] = jnp.concatenate(
            [table, share[:, :TEXT_DIM], share[:, TEXT_DIM:]], axis=0
        ).reshape(block)
    flow.add(items[4])
    flow.beat()
    mel_part = dot(mel_w_ref[...], hidden, 1, 1)
    bins = mel_part.shape[0] // 2
    mel_ref[...] = info_ref[0] * mel_part[:bins] + keep_ref[...] * mel_part[bins:]
    mel_copy = pltpu.make_async_remote_copy(
        src_ref=mel_ref, dst_ref=mel_in_ref, send_sem=mel_sems.at[0], recv_sem=mel_sems.at[1],
        device_id=partner, device_id_type=MESH,
    )

    @pl.when(moves)
    def _():
        mel_copy.start()

    flow.beat()
    for copy in every_copies:
        copy.wait()
    for pair in range(4):
        sums_ref[pair] = every[2 * pair] + every[2 * pair + 1]
    total = None
    for chunk in range(chunks):
        held = sums_ref[:, :, chunk, :].reshape(16, lanes).astype(BF)
        term = dot(held, proj_ref[:, chunk * lanes : (chunk + 1) * lanes], 1, 1)
        total = term if total is None else total + term
    part_ref[...] = total
    act_ref[tp] = total
    for copy in act_copies:
        copy.start()
    while flow.beat():
        pass
    for copy in act_copies:
        copy.wait()

    @pl.when(moves)
    def _():
        mel_copy.wait()


def tail(
    info, x, weights, cosine, sine, dq, dk, dv, dk_in, dv_in, values, mid_grad, scale,
    feats, mel_w, text_w, ids, keep, mod_part, mod_proj,
):
    rows = x.shape[0]
    ranks, width = weights.shape[0], weights.shape[3]
    table_rows = VOCABULARY // ranks
    misc_rows = table_rows + 2 * (feats.shape[1] // ranks)
    chunks = mod_part.shape[1]
    qkv_block = blocks((WIDTH, width))
    misc_block = blocks((misc_rows // 2, TEXT_DIM))
    dma = pltpu.SemaphoreType.DMA
    vmem = pl.BlockSpec(memory_space=pltpu.VMEM)
    smem = pl.BlockSpec(memory_space=pltpu.SMEM)
    scratch = []
    for _ in range(3):
        scratch += Reduce.scratch(WIDTH, width, True)
    for _ in range(2):
        scratch += Reduce.scratch(misc_rows // 2, TEXT_DIM, True)
    mel_shape = jax.ShapeDtypeStruct((mel_w.shape[0] // 2, rows), F32)
    outs = pl.pallas_call(
        tail_kernel,
        in_specs=[smem, vmem, ANY] + [vmem] * 17,
        out_specs=[vmem] * 3 + [ANY] * 3,
        out_shape=[
            jax.ShapeDtypeStruct((4, 4, chunks, 128), F32),
            jax.ShapeDtypeStruct((4, 16, WIDTH), F32),
            mel_shape,
            mel_shape,
            jax.ShapeDtypeStruct((3,) + qkv_block, BF),
            jax.ShapeDtypeStruct((2,) + misc_block, BF),
        ],
        scratch_shapes=[
            pltpu.VMEM((WIDTH, rows), BF),
            pltpu.VMEM((2, ranks, WIDTH, width), BF),
            pltpu.VMEM((rows, WIDTH), F32),
            pltpu.VMEM((rows, WIDTH), BF),
            pltpu.VMEM((rows, TEXT_DIM), BF),
            pltpu.VMEM((3, ranks) + qkv_block, BF),
            pltpu.VMEM((2, ranks) + misc_block, BF),
            pltpu.VMEM((4, chunks, 128), F32),
            pltpu.VMEM((4, chunks, 128), F32),
            pltpu.VMEM((8, 4, chunks, 128), F32),
            pltpu.VMEM((16, WIDTH), F32),
            dma((3,)), dma((3,)), dma((3,)), dma((7,)), dma((7,)), dma((3,)), dma((3,)), dma((2,)),
        ]
        + scratch,
        compiler_params=comm_params(4),
        name="tail",
    )(
        info, x, weights, cosine, sine, dq, dk, dv, dk_in, dv_in, values, mid_grad, scale,
        feats, mel_w, text_w, ids, keep, mod_part, mod_proj,
    )
    return list(outs[:4]) + [
        outs[4].reshape(3, WIDTH, width), outs[5].reshape(misc_rows, TEXT_DIM)
    ]


def time_features(flow_times, width):
    half_dim = width // 2
    frequency = jnp.exp(
        jnp.arange(half_dim, dtype=F32) * (-math.log(10000.0) / (half_dim - 1))
    )
    angles = 1000.0 * flow_times[:, None] * frequency[None, :]
    return jnp.concatenate([jnp.sin(angles), jnp.cos(angles)], axis=1)


def rope_tables(positions, width):
    lane = jnp.arange(width, dtype=jnp.int32)
    pair = ((lane % HEAD_DIM) // 2).astype(F32)
    inverse = jnp.exp(pair * (-2.0 * math.log(10000.0) / HEAD_DIM))
    angles = positions.astype(F32)[:, None] * inverse[None, :]
    sign = jnp.where(lane % 2 == 0, -1.0, 1.0)
    return jnp.cos(angles), jnp.sin(angles) * sign[None, :]


def norm_parts(values):
    average = jnp.mean(values, axis=-1, keepdims=True)
    centered = values - average
    spread = jnp.mean(centered * centered, axis=-1, keepdims=True)
    inverse = lax.rsqrt(spread + 1e-06)
    return centered * inverse, inverse


def norm_back(normed, inverse, scale_part, grad):
    inner = grad * (1.0 + scale_part)
    first = jnp.mean(inner, axis=-1, keepdims=True)
    second = jnp.mean(inner * normed, axis=-1, keepdims=True)
    return inverse * (inner - first - normed * second)


def body(
    mel_frames, noise_frames, text_ids, span_mask, lengths, audio_drop, text_drop, flow_times,
    in_proj, text_table, time_proj, mod_proj, qkv_proj, out_proj, up_proj, down_proj, cotangent,
):
    dp_size = lax.axis_size("dp")
    tp_size = lax.axis_size("tp")
    dp_rank = lax.axis_index("dp")
    tp_rank = lax.axis_index("tp")
    local_rows = mel_frames.shape[0]
    per_group = flow_times.shape[0]
    utt_total = per_group * dp_size
    dp_low = dp_rank % 2
    tp_low = tp_rank % 2
    stay = dp_low == tp_low
    direct = dp_size == 8 and tp_size == 4
    pairs = []
    for d in range(dp_size):
        for t in range(tp_size):
            if d % 2 != t % 2:
                pairs.append((d * tp_size + t, (d ^ 1) * tp_size + (t ^ 1)))

    def swap(values):
        return jnp.where(stay, values, lax.ppermute(values, AXES, pairs))

    source_dp = dp_rank - dp_low + tp_low
    utterance = source_dp * per_group + tp_rank // 2
    half = dp_low

    def relative(values):
        return jnp.roll(values, -tp_rank, axis=0)

    def gather(shard):
        return relative(lax.all_gather(shard, "tp", axis=0))

    sinus_own = time_features(flow_times, TIME_DIM)
    facts = jnp.concatenate(
        [
            sinus_own,
            flow_times[:, None],
            lengths.astype(F32)[:, None],
            1.0 - audio_drop.astype(F32)[:, None],
            1.0 - text_drop.astype(F32)[:, None],
            jnp.zeros((per_group, 124), F32),
        ],
        axis=1,
    )
    act_own = jax.nn.silu(dot(sinus_own.astype(BF), time_proj)).astype(BF)
    mod_cols = dot(act_own, mod_proj)
    spare = -MEL_BINS % 16
    bins = MEL_BINS + spare
    extra = jnp.stack(
        [span_mask.astype(BF), (text_ids // 256).astype(BF), (text_ids % 256).astype(BF)]
        + [jnp.zeros((local_rows,), BF)] * 13,
        axis=0,
    )
    padded = lambda v: jnp.pad(v, ((0, spare), (0, 0)))
    mel, noise = padded(mel_frames.T), padded(noise_frames.T)
    mel_w = jnp.concatenate(
        [padded(in_proj[:MEL_BINS]), padded(in_proj[MEL_BINS : 2 * MEL_BINS])], axis=0
    )
    text_w = in_proj[2 * MEL_BINS :]
    qkv_shard = qkv_proj.transpose(1, 0, 2)
    positions = half * local_rows + jnp.arange(local_rows, dtype=jnp.int32)
    cosine, sine = rope_tables(positions, WIDTH // tp_size)
    narrow = lambda table: table[:, : 2 * HEAD_DIM]
    if direct:
        pad = ((0, 8 - per_group), (0, 0))
        (
            facts_all, mod_rows, mine, extra, cot, qkv_full, out_full, up_full, down_full,
            attn_sum, hidden_mid, normed_mlp, feats, text_emb, hidden, normed_attn, query, key, value, key_in, value_in, heads_out, lse,
        ) = forward(
            mel, noise, extra, jnp.pad(facts, pad), jnp.pad(mod_cols, pad), cotangent, qkv_shard, out_proj, up_proj,
            down_proj, text_table, mel_w, text_w, narrow(cosine), narrow(sine),
        )
        cot = jnp.where(stay, cotangent, cot)
        facts_all = facts_all[:, :per_group].reshape(utt_total, -1)
        mod_row = mod_rows[:6].reshape(1, 6 * WIDTH)
        mine = mine[:1]
    else:
        facts_all = lax.all_gather(facts, "dp", axis=0, tiled=True)
        near = lax.all_gather(lax.all_gather(mod_cols, "tp", axis=1, tiled=True), "dp", axis=0, tiled=True)
        mod_row = lax.dynamic_slice_in_dim(near, utterance, 1, 0)
        mel, noise, extra, cot = swap(mel), swap(noise), swap(extra), swap(cotangent)
        mine = lax.dynamic_slice_in_dim(facts_all, utterance, 1, 0)[:, TIME_DIM:]
    shift_attn, scale_attn, gate_attn, shift_mlp, scale_mlp, gate_mlp = jnp.split(mod_row, 6, axis=1)
    time_here, length, keep_audio, keep_text = (mine[0, i] for i in range(4))
    length = length.astype(jnp.int32)
    extra = extra[:3].astype(jnp.int32)
    ids = extra[1] * 256 + extra[2]
    out_grad = cot.astype(F32)
    keep_cond = (1.0 - extra[0].astype(F32))[None, :] * keep_audio
    info = jnp.stack([length, half * local_rows, (1 - half) * local_rows])
    if not direct:
        mel, noise = mel.astype(F32), noise.astype(F32)
        noisy = (1.0 - time_here) * noise + time_here * mel
        feats = jnp.concatenate([noisy, mel * keep_cond], axis=0).astype(BF)
        text_emb = (jnp.take(text_table, ids, axis=0).astype(F32) * keep_text).astype(BF)
    features = jnp.concatenate([feats[:MEL_BINS].T, feats[bins : bins + MEL_BINS].T, text_emb], axis=1)
    if not direct:
        qkv_full = gather(qkv_shard)
        hidden = dot(features, in_proj)
        norm_a, inv_a = norm_parts(hidden)
        normed_attn = (norm_a * (1.0 + scale_attn) + shift_attn).astype(BF)
        query, key, value, key_in, value_in = project_qkv(normed_attn, qkv_full, cosine, sine)
        heads_out, lse = attend(info, query, (key, value), (key_in, value_in))
        out_full, up_full, down_full = (gather(shard) for shard in (out_proj, up_proj, down_proj))
    own, other = (key, value), (key_in, value_in)
    out_full = out_full.reshape(WIDTH, WIDTH)
    if not direct:
        attn_sum = dot(heads_out, out_full)
        hidden_mid = hidden + gate_attn * attn_sum
    norm_m, inv_m = norm_parts(hidden_mid)
    if not direct:
        normed_mlp = (norm_m * (1.0 + scale_mlp) + shift_mlp).astype(BF)
    mlp_grad = (gate_mlp * out_grad).astype(BF)
    mlp_sum, normed_mlp_grad, up_grad, down_grad = mlp(normed_mlp, mlp_grad, up_full, down_full)
    layer_out = swap((hidden_mid + gate_mlp * mlp_sum).astype(BF))
    mid_grad = out_grad + norm_back(norm_m, inv_m, scale_mlp, normed_mlp_grad)
    attn_grad = (gate_attn * mid_grad).astype(BF)
    out_grad_w = dot(heads_out, attn_grad, 0, 0).astype(BF).reshape(tp_size, -1, WIDTH)
    heads_grad = dot(attn_grad, out_full, 1, 1).astype(BF)
    halves = lambda v, count: v.reshape((tp_size, count, v.shape[1] // count) + v.shape[2:])
    early = (halves(up_grad, 2), halves(down_grad, 2), halves(out_grad_w, 1))
    (dq, dk, dv, dk_in, dv_in), early_out = attend_back(
        info, query, own, other, heads_grad, heads_out, lse, narrow(cosine), narrow(sine),
        early if direct else (),
    )
    column_sum = lambda values: jnp.sum(values, axis=0, keepdims=True)
    mod_rest = jnp.concatenate(
        [
            column_sum(attn_sum * mid_grad),
            column_sum(normed_mlp_grad),
            column_sum(normed_mlp_grad * norm_m),
            column_sum(out_grad * mlp_sum),
        ],
        axis=1,
    )
    sinus = facts_all[:, :TIME_DIM].astype(BF)
    time_embed = dot(sinus, time_proj)
    time_act = jax.nn.silu(time_embed).astype(BF)
    in_rows = in_proj.shape[0] // tp_size
    in_pad = -in_rows % 64
    table_rows = VOCABULARY // tp_size
    spaced = lambda v, axis: jnp.concatenate(
        [
            jnp.pad(
                lax.slice_in_dim(v, i * in_rows, (i + 1) * in_rows, axis=axis),
                [(0, in_pad if d == axis else 0) for d in range(2)],
            )
            for i in range(tp_size)
        ],
        axis=axis,
    )
    if direct:
        sums, act_parts, mel_own, mel_came, qkv_out, misc_out = tail(
            jnp.stack([time_here, keep_audio, keep_text, keep_text]),
            normed_attn, qkv_full, cosine, sine, dq, dk, dv, dk_in, dv_in, hidden, mid_grad,
            scale_attn, spaced(features, 1), mel_w, text_w, ids[None, :], keep_cond,
            jnp.pad(mod_rest, ((0, 0), (2 * WIDTH, 0))).reshape(tp_size, -1, 128), mod_proj,
        )
        mel_grad = jnp.where(stay, mel_own, mel_came)[:MEL_BINS].T
        order = lambda v: v.reshape((4, 2, 2) + v.shape[2:]).swapaxes(1, 2)
        mod_sums = order(sums).reshape(utt_total, -1).astype(BF)
        act_grad = jnp.sum(act_parts, axis=0)
        act_grad = order(act_grad.reshape(4, 4, WIDTH)).reshape(utt_total, WIDTH)
    else:
        qkv_grad, normed_attn_grad = project_qkv_back(
            normed_attn, qkv_full, cosine, sine, dq, dk, dv, dk_in, dv_in
        )
        hidden_grad = (mid_grad + norm_back(norm_a, inv_a, scale_attn, normed_attn_grad)).astype(BF)
        in_grad = dot(features, hidden_grad, 0, 0).astype(BF)
        mel_part = dot(in_proj[: 2 * MEL_BINS], hidden_grad, 1, 1)
        mel_grad = swap(
            (time_here * mel_part[:MEL_BINS] + keep_cond * mel_part[MEL_BINS:]).T
        )
        text_grad = dot(hidden_grad, in_proj[2 * MEL_BINS :], 1, 1).astype(BF) * keep_text.astype(BF)
        one_hot = (ids[None, :] == jnp.arange(VOCABULARY, dtype=jnp.int32)[:, None]).astype(BF)
        table_grad = dot(one_hot, text_grad).astype(BF).reshape(tp_size, table_rows, TEXT_DIM)
        in_grad = spaced(in_grad, 0).reshape(tp_size, in_rows + in_pad, WIDTH)
        misc = jnp.concatenate(
            [table_grad, in_grad[:, :, :TEXT_DIM], in_grad[:, :, TEXT_DIM:]], axis=1
        )
        mod_part = jnp.concatenate(
            [column_sum(normed_attn_grad), column_sum(normed_attn_grad * norm_a), mod_rest], axis=1
        )
        slot = (jnp.arange(utt_total, dtype=jnp.int32) == utterance).astype(F32)[:, None]
        mod_sums = lax.psum(
            lax.psum_scatter(slot * mod_part, "tp", scatter_dimension=1, tiled=True), "dp"
        ).astype(BF)
        act_grad = lax.psum(dot(mod_sums, mod_proj, 1, 1), "tp")

        def reduce(values):
            return lax.psum(
                lax.psum_scatter(values, "tp", scatter_dimension=0, tiled=True)[0], "dp"
            )

        absolute = lambda values: jnp.roll(values, tp_rank, axis=0)
        early_out = [reduce(absolute(values)) for values in (up_grad, down_grad, out_grad_w)]
        qkv_out = reduce(absolute(qkv_grad))
        misc_out = reduce(misc)
    mod_grad = dot(time_act, mod_sums, 0, 0)
    embed_grad = jax.vjp(jax.nn.silu, time_embed)[1](act_grad)[0].astype(BF)
    time_rows = TIME_DIM // tp_size
    sinus_share = lax.dynamic_slice_in_dim(sinus, tp_rank * time_rows, time_rows, 1)
    time_grad = dot(sinus_share, embed_grad, 0, 0)
    up_out, down_out, out_out = (values.astype(F32) for values in early_out)
    misc_out = misc_out.astype(F32)
    right = table_rows + in_rows + in_pad
    in_out = jnp.concatenate(
        [misc_out[table_rows : table_rows + in_rows], misc_out[right : right + in_rows]], axis=1
    )
    return (
        layer_out, mel_grad, in_out, misc_out[:table_rows], time_grad, mod_grad,
        qkv_out.astype(F32).transpose(1, 0, 2), out_out, up_out, down_out,
    )


def solution(mesh):
    frames = P(("dp", "tp"), None)
    frame = P(("dp", "tp"))
    return jax.shard_map(
        body,
        mesh=mesh,
        in_specs=(
            frames, frames, frame, frame, P("dp"), P("dp"), P("dp"), P("dp"),
            P(), P(), P(), P(None, "tp"), P(None, None, "tp"), P("tp", None), P(None, "tp"),
            P("tp", None), frames,
        ),
        out_specs=(
            frames, frames, P("tp", None), P("tp", None), P("tp", None), P(None, "tp"),
            P(None, None, "tp"), P("tp", None), P(None, "tp"), P("tp", None),
        ),
        check_vma=False,
    )
```

```python
import functools
import math

import jax
import jax.numpy as jnp
from jax import lax
from jax.experimental import pallas as pl
from jax.experimental.pallas import tpu as pltpu
from jax.sharding import PartitionSpec as P

WIDTH = 1024
HEAD_DIM = 64
MEL_BINS = 100
TEXT_DIM = 512
TIME_DIM = 256
VOCABULARY = 2560
FFN_DIM = 2048
AXES = ("dp", "tp")
BF = jnp.bfloat16
F32 = jnp.float32
MESH = pl.DeviceIdType.MESH
VMEM_LIMIT = 60 * 1024 * 1024
ANY = pl.BlockSpec(memory_space=pl.ANY)


def dot(left, right, left_dim=1, right_dim=0):
    return lax.dot_general(
        left, right, (((left_dim,), (right_dim,)), ((), ())), preferred_element_type=F32
    )


def flip(index, bit):
    return index + bit - 2 * bit * ((index // bit) % 2)


class Place:
    def __init__(self):
        self.dp = lax.axis_index("dp")
        self.tp = lax.axis_index("tp")
        self.core = self.dp % 2
        self.x = (self.dp // 2) % 2
        self.y = self.dp // 4

    def plane(self, bit):
        return (flip(self.dp, bit), self.tp)

    def ahead(self, step):
        return (self.dp, (self.tp + step) % 4)


def greet(devices):
    barrier = pltpu.get_barrier_semaphore()
    for device in devices:
        pl.semaphore_signal(barrier, inc=1, device_id=device, device_id_type=MESH)
    pl.semaphore_wait(barrier, len(devices))


def remote(source, target, sems, index, device):
    return pltpu.make_async_remote_copy(
        src_ref=source,
        dst_ref=target,
        send_sem=sems[0].at[index],
        recv_sem=sems[1].at[index],
        device_id=device,
        device_id_type=MESH,
    )


GATHER_COPIES = 13


class Gather:
    def __init__(self, place, shard, full, scratch, slots=(1, 2, 3), part=slice(None)):
        self.p, self.shard, self.full = place, shard, full
        self.sems, self.held = scratch[:2], (scratch[2:] or [None])[0]
        self.slots, self.part = slots, part

    @staticmethod
    def scratch(shape=None):
        dma = pltpu.SemaphoreType.DMA
        held = [] if shape is None else [pltpu.VMEM(shape, BF)]
        return [dma((GATHER_COPIES,)), dma((GATHER_COPIES,))] + held

    def view(self, *index):
        return self.full.at[(slice(self.slots[0], self.slots[-1] + 1), self.part) + index]

    def copy(self, kind):
        p = self.p
        dp = p.dp
        beside, above = flip(dp, 2), flip(dp, 4)
        across = flip(above, 2)
        if kind[0] == "z":
            step = int(kind[1])
            return remote(
                self.shard.at[self.part, dp],
                self.full.at[step, self.part, dp],
                self.sems,
                step - 1,
                p.ahead(4 - step),
            )
        index, bit, sem = {
            "x": ((dp,), 2, 3),
            "y": ((dp,), 4, 4),
            "c": ((dp,), 1, 5),
            "ya": ((beside, 0), 4, 6),
            "xb": ((above, 1), 2, 7),
            "cx": ((beside,), 1, 8),
            "cy": ((above,), 1, 9),
            "cd": ((across,), 1, 10),
        }[kind]
        return remote(self.view(*index), self.view(*index), self.sems, sem, p.plane(bit))

    def fetch(self):
        return pltpu.make_async_copy(self.shard.at[self.part], self.held, self.sems[0].at[11])

    def keep(self):
        return pltpu.make_async_copy(self.held, self.full.at[0, self.part], self.sems[0].at[12])

    def start(self, *kinds):
        for kind in kinds:
            self.copy(kind).start()

    def arrived(self, *kinds):
        for kind in kinds:
            self.copy(kind).wait_recv()

    def lines(self):
        return ["z%d" % slot for slot in self.slots]

    def stage0(self):
        self.start(*self.lines())
        if self.held is not None:
            self.fetch().start()

    def stage1(self):
        if self.held is not None:
            self.fetch().wait()
            self.keep().start()
        self.arrived(*self.lines())
        self.start("x", "y", "c")

    def stage2(self):
        self.arrived("x")
        self.start("ya", "cx")
        self.arrived("y")
        self.start("xb", "cy")

    def stage3(self):
        self.arrived("ya", "xb")
        self.start("cd")

    def stage4(self):
        self.arrived("c", "cx", "cy", "cd")

    def finish(self):
        if self.held is not None:
            self.keep().wait()
        for kind in self.lines() + ["x", "y", "c", "ya", "xb", "cx", "cy", "cd"]:
            self.copy(kind).wait_send()

    stages = property(lambda s: [s.stage0, s.stage1, s.stage2, s.stage3, s.stage4])


REDUCE_COPIES = 18


def add_into(target, source):
    for index in range(4):
        target[index] = (target[index].astype(F32) + source[index].astype(F32)).astype(BF)


class Reduce:
    @staticmethod
    def scratch(rows, columns):
        r = rows // 16
        shapes = [
            (4, 2, 2, 2, r, columns),
            (4, 2, r, columns),
            (4, 2, r, columns),
            (4, r, columns),
            (4, r, columns),
            (3, 2, r, columns),
            (2, r, columns),
        ]
        return [
            pltpu.SemaphoreType.DMA((REDUCE_COPIES,)),
            pltpu.SemaphoreType.DMA((REDUCE_COPIES,)),
        ] + [pltpu.VMEM(shape, BF) for shape in shapes]

    def __init__(self, place, grads, out, scratch, buffer=None, absolute=False):
        self.p, self.grads, self.out, self.buffer = place, grads, out, buffer
        self.sems = scratch[:2]
        self.rc, self.rx, self.ry, self.ra, self.rb, self.rz, self.fin = scratch[2:9]
        self.acc = grads.at[:, place.core] if buffer is None else self.rc
        self.first = place.tp if absolute else 0

    def slot(self, step):
        return (self.first + step) % 4

    def copy(self, kind):
        p, acc, out, fin = self.p, self.acc, self.out, self.fin
        c, x, y = p.core, p.x, p.y
        if kind in ("z1", "z2", "z3"):
            step = int(kind[1])
            return remote(
                acc.at[self.slot(step), x, y], self.rz.at[step - 1], self.sems, 4 + step, p.ahead(step)
            )
        table = {
            "c": (lambda: self.grads.at[:, 1 - c], lambda: self.rc, 1, 0),
            "x": (lambda: acc.at[:, 1 - x, :, 0], lambda: self.rx, 2, 1),
            "y": (lambda: acc.at[:, :, 1 - y, 1], lambda: self.ry, 4, 2),
            "ya": (lambda: acc.at[:, x, 1 - y, 0], lambda: self.ra, 4, 3),
            "xb": (lambda: acc.at[:, 1 - x, y, 1], lambda: self.rb, 2, 4),
            "gx": (lambda: fin, lambda: out.at[c, x, y], 2, 8),
            "gy": (lambda: fin, lambda: out.at[c, x, y], 4, 9),
            "gc": (lambda: fin, lambda: out.at[c, x, y], 1, 10),
            "gya": (lambda: out.at[c, 1 - x, y, 0], lambda: out.at[c, 1 - x, y, 0], 4, 11),
            "gxb": (lambda: out.at[c, x, 1 - y, 1], lambda: out.at[c, x, 1 - y, 1], 2, 12),
            "gcx": (lambda: out.at[c, 1 - x, y], lambda: out.at[c, 1 - x, y], 1, 13),
            "gcy": (lambda: out.at[c, x, 1 - y], lambda: out.at[c, x, 1 - y], 1, 14),
            "gcd": (lambda: out.at[c, 1 - x, 1 - y], lambda: out.at[c, 1 - x, 1 - y], 1, 15),
        }
        source, target, bit, index = table[kind]
        return remote(source(), target(), self.sems, index, p.plane(bit))

    def load(self):
        return pltpu.make_async_copy(self.grads.at[:, self.p.core], self.buffer, self.sems[0].at[16])

    def keep(self):
        p = self.p
        return pltpu.make_async_copy(self.fin, self.out.at[p.core, p.x, p.y], self.sems[0].at[17])

    def start(self, *kinds):
        for kind in kinds:
            self.copy(kind).start()

    def arrived(self, *kinds):
        for kind in kinds:
            self.copy(kind).wait_recv()

    def stage0(self):
        self.start("c")
        if self.buffer is not None:
            self.load().start()

    def stage1(self):
        self.arrived("c")
        if self.buffer is None:
            add_into(self.acc, self.rc)
        else:
            self.load().wait()
            add_into(self.rc, self.buffer)
        self.start("x", "y")

    def stage2(self):
        p = self.p
        self.arrived("x")
        add_into(self.acc.at[:, p.x, :, 0], self.rx)
        self.start("ya")
        self.arrived("y")
        add_into(self.acc.at[:, :, p.y, 1], self.ry)
        self.start("xb")

    def stage3(self):
        p = self.p
        self.arrived("ya")
        add_into(self.acc.at[:, p.x, p.y, 0], self.ra)
        self.arrived("xb")
        add_into(self.acc.at[:, p.x, p.y, 1], self.rb)
        self.start("z1", "z2", "z3")

    def stage4(self):
        p = self.p
        self.arrived("z1", "z2", "z3")
        total = self.acc[self.slot(0), p.x, p.y].astype(F32)
        for step in range(3):
            total += self.rz[step].astype(F32)
        self.fin[...] = total.astype(BF)
        self.keep().start()
        self.start("gx", "gy", "gc")

    def stage5(self):
        self.arrived("gx")
        self.start("gya", "gcx")
        self.arrived("gy")
        self.start("gxb", "gcy")

    def stage6(self):
        self.arrived("gya", "gxb")
        self.start("gcd")

    def stage7(self):
        self.arrived("gc", "gcx", "gcy", "gcd")
        self.keep().wait()
        for kind in (
            "c", "x", "y", "ya", "xb", "z1", "z2", "z3", "gx", "gy", "gc", "gya", "gxb", "gcx", "gcy", "gcd",
        ):
            self.copy(kind).wait_send()

    stages = property(
        lambda s: [s.stage0, s.stage1, s.stage2, s.stage3, s.stage4, s.stage5, s.stage6, s.stage7]
    )


def pipeline(items, first=0):
    stages = [item.stages[first:] for item in items]
    depth = max(len(held) for held in stages)
    beats = []
    for beat in range(len(items) + depth - 1):
        beats.append(
            [held[beat - j] for j, held in enumerate(stages) if 0 <= beat - j < len(held)][::-1]
        )
    return beats


LAGS = (0, 1, 4, 7, 9, 12, 14, 15)
JOINS = (0, 1, 3, 5, 7)


class Flow:
    def __init__(self):
        self.items = []
        self.now = 0

    def add(self, item):
        self.items.append([(self.now + lag, stage) for lag, stage in zip(LAGS, item.stages)])

    def take(self):
        due = [held.pop(0)[1] for held in self.items[::-1] if held and held[0][0] <= self.now]
        self.now += 1
        return due

    def beat(self):
        for stage in self.take():
            stage()
        return any(self.items)


def plane_and_line(place):
    return [place.plane(bit) for bit in (1, 2, 4)] + [place.ahead(step) for step in (1, 2, 3)]


def flip3(index, mask):
    for bit in (1, 2, 4):
        if mask & bit:
            index = flip(index, bit)
    return index


def comm_params(collective_id):
    return pltpu.CompilerParams(
        vmem_limit_bytes=VMEM_LIMIT, collective_id=collective_id, has_side_effects=True
    )


def pieces(shape):
    return tuple(shape[:-2]) + (8, 2, shape[-2] // 16, shape[-1])


def blocks(shape):
    return tuple(shape[:-2]) + (2, 2, 2, 2, shape[-2] // 16, shape[-1])


def head_masks(rows):
    lane = lax.broadcasted_iota(jnp.int32, (rows, 2 * HEAD_DIM), 1)
    return [lane < HEAD_DIM, lane >= HEAD_DIM]


def key_bias(length, start, rows):
    position = lax.broadcasted_iota(jnp.int32, (rows, 1), 0) + start
    return jnp.where(position < length, 0.0, -1e30)


def attend_pair(bias0, bias1, q_ref, k0_ref, v0_ref, k1_ref, v1_ref):
    rows = q_ref.shape[0]
    query = q_ref[...] * jnp.asarray(1.0 / math.sqrt(HEAD_DIM), BF)
    masks = head_masks(rows)
    vt0 = v0_ref[...].T
    vt1 = v1_ref[...].T
    parts, totals = [], []
    for head in range(2):
        masked = jnp.where(masks[head], query, jnp.zeros_like(query))
        s0 = dot(k0_ref[...], masked, 1, 1) + bias0
        s1 = dot(k1_ref[...], masked, 1, 1) + bias1
        peak = jnp.maximum(
            jnp.max(s0, axis=0, keepdims=True), jnp.max(s1, axis=0, keepdims=True)
        )
        e0 = jnp.exp(s0 - peak)
        e1 = jnp.exp(s1 - peak)
        total = jnp.sum(e0, axis=0, keepdims=True) + jnp.sum(e1, axis=0, keepdims=True)
        side = slice(head * HEAD_DIM, (head + 1) * HEAD_DIM)
        acc = dot(vt0[side], e0.astype(BF)) + dot(vt1[side], e1.astype(BF))
        parts.append(acc / total)
        totals.append(peak + jnp.log(total))
    return jnp.concatenate(parts, axis=0).T.astype(BF), totals


def attend_back_pair(biases, q_ref, k0_ref, v0_ref, k1_ref, v1_ref, do_ref, o_ref, lse_ref):
    rows = q_ref.shape[0]
    keys = k0_ref.shape[0]
    width = 2 * HEAD_DIM
    scale = 1.0 / math.sqrt(HEAD_DIM)
    query = q_ref[...] * jnp.asarray(scale, BF)
    grads = do_ref[...]
    product = (grads.astype(F32) * o_ref[...].astype(F32)).T
    sides = ((k0_ref, v0_ref), (k1_ref, v1_ref))
    turned = [k_ref[...].T for k_ref, _ in sides]

    def one_head(head, carry):
        dq, sums = carry[0], list(carry[1:])
        lane = lax.broadcasted_iota(jnp.int32, (rows, width), 1) // HEAD_DIM
        line = lax.broadcasted_iota(jnp.int32, (width, 1), 0) // HEAD_DIM
        masked = jnp.where(lane == head, query, jnp.zeros_like(query))
        gmask = jnp.where(lane == head, grads, jnp.zeros_like(grads))
        delta = jnp.sum(jnp.where(line == head, product, 0.0), axis=0, keepdims=True)
        total = lse_ref[head]
        for which, (k_ref, v_ref) in enumerate(sides):
            scores = dot(k_ref[...], masked, 1, 1) + biases[which]
            probs = jnp.exp(scores - total)
            prob_grad = dot(v_ref[...], gmask, 1, 1)
            score_grad = (probs * (prob_grad - delta)).astype(BF)
            sums[2 * which] += dot(score_grad, masked)
            sums[2 * which + 1] += dot(probs.astype(BF), gmask)
            kt = jnp.where(line == head, turned[which].astype(F32), 0.0).astype(BF)
            dq += dot(kt, score_grad)
        return (dq, *sums)

    start = (jnp.zeros((width, rows), F32),) + (jnp.zeros((keys, width), F32),) * 4
    dq, *sums = lax.fori_loop(0, 2, one_head, start)
    return dq.T * scale, [sums[:2], sums[2:]]


def turn(values, cosine, sine):
    lane = lax.broadcasted_iota(jnp.int32, values.shape, 1)
    width = values.shape[1]
    other = jnp.where(
        lane % 2 == 0, pltpu.roll(values, width - 1, 1), pltpu.roll(values, 1, 1)
    )
    return values * cosine + other * sine


def attend_kernel(info_ref, q, k0, v0, k1, v1, o_ref, lse_ref):
    keys = k0.shape[0]
    biases = [key_bias(info_ref[0], info_ref[1 + which], keys) for which in range(2)]
    o_ref[...], (lse_ref[0], lse_ref[1]) = attend_pair(*biases, q, k0, v0, k1, v1)


def attend(info, query, own, other):
    rows = query.shape[0]
    pairs = WIDTH // (2 * HEAD_DIM)
    tile = pl.BlockSpec((rows, 2 * HEAD_DIM), lambda i: (0, i))
    return pl.pallas_call(
        attend_kernel,
        grid=(pairs,),
        in_specs=[pl.BlockSpec(memory_space=pltpu.SMEM)] + [tile] * 5,
        out_specs=[tile, pl.BlockSpec((2, 1, rows), lambda i: (i, 0, 0))],
        out_shape=[
            jax.ShapeDtypeStruct((rows, WIDTH), BF),
            jax.ShapeDtypeStruct((2 * pairs, 1, rows), F32),
        ],
        compiler_params=pltpu.CompilerParams(vmem_limit_bytes=VMEM_LIMIT),
        name="attend",
    )(info, query, *own, *other)


def sibling_copies(sent, targets, sems, index, width, slots):
    columns = pl.ds(pl.multiple_of(index * width, width), width)
    return [
        pltpu.make_async_remote_copy(
            src_ref=sent.at[kind, index % slots],
            dst_ref=target.at[:, columns],
            send_sem=sems[0].at[kind, index],
            recv_sem=sems[1].at[kind, index],
            device_id=(flip(lax.axis_index("dp"), 1), lax.axis_index("tp")),
            device_id_type=MESH,
        )
        for kind, target in enumerate(targets)
    ]


def attend_back_kernel(
    info_ref, q, k0, v0, k1, v1, do, o, lse, cos, sin,
    dq_ref, dk_ref, dv_ref, dk_in, dv_in, sent, *sems
):
    step = pl.program_id(0)
    last = pl.num_programs(0) - 1
    width = 2 * HEAD_DIM
    steps = WIDTH // width
    copies = lambda index: sibling_copies(sent, (dk_in, dv_in), sems, index, width, steps)

    @pl.when(step == 0)
    def _():
        greet([(flip(lax.axis_index("dp"), 1), lax.axis_index("tp"))])

    keys = k0.shape[0]
    biases = [key_bias(info_ref[0], info_ref[1 + which], keys) for which in range(2)]
    dq, results = attend_back_pair(biases, q, k0, v0, k1, v1, do, o, lse)
    dq_ref[...] = turn(dq, cos[...], -sin[...]).astype(BF)
    dk_ref[...], dv_ref[...] = results[0]
    sent[0, step] = results[1][0].astype(BF)
    sent[1, step] = results[1][1].astype(BF)
    for copy in copies(step):
        copy.start()

    @pl.when(step == last)
    def _():
        for index in range(steps):
            for copy in copies(index):
                copy.wait()


def attend_back(info, query, own, other, heads_grad, outputs, lse, cosine, sine):
    rows = query.shape[0]
    pairs = WIDTH // (2 * HEAD_DIM)
    width = 2 * HEAD_DIM
    tile = pl.BlockSpec((rows, width), lambda i: (0, i))
    fixed = pl.BlockSpec((rows, width), lambda i: (0, 0))
    dma = pltpu.SemaphoreType.DMA
    return pl.pallas_call(
        attend_back_kernel,
        grid=(pairs,),
        in_specs=[pl.BlockSpec(memory_space=pltpu.SMEM)]
        + [tile] * 7
        + [pl.BlockSpec((2, 1, rows), lambda i: (i, 0, 0)), fixed, fixed],
        out_specs=[tile] * 3 + [ANY] * 2,
        out_shape=[
            jax.ShapeDtypeStruct((rows, WIDTH), BF),
            jax.ShapeDtypeStruct((rows, WIDTH), F32),
            jax.ShapeDtypeStruct((rows, WIDTH), F32),
            jax.ShapeDtypeStruct((rows, WIDTH), BF),
            jax.ShapeDtypeStruct((rows, WIDTH), BF),
        ],
        scratch_shapes=[
            pltpu.VMEM((2, pairs, rows, width), BF),
            dma((2, pairs)),
            dma((2, pairs)),
        ],
        compiler_params=comm_params(3),
        name="attend_back",
    )(info, query, *own, *other, heads_grad, outputs, lse, cosine, sine)


def forward_kernel(
    mel, noise, extra, facts, mods, cot, qkv, out_w, up_w, down_w, table, mel_w, text_w, cos, sin,
    facts_all, mod_row, mine_out, extra_out, cot_in, qkv_full, out_full, up_full, down_full,
    sum_out, mid_out, normed_out, feats_out, text_out, hidden_out, x_out, q_out, k_out, v_out, ki_out, vi_out, heads_out, lse_out,
    mel_in, noise_in, extra_in, facts_v, mods_v, table_v, mel_wv, text_wv, cos_v, sin_v,
    feats_v, text_v, hidden_v, x_v, q_v, k_v, v_v, ki_v, vi_v, heads_v, lse_v, full_v, outw_v, sum_v, mid_v, normed_v, rows_v, mine_v,
    load_sems, save_sems, fact_sends, fact_recvs, mod_sends, mod_recvs, swap_sends, swap_recvs,
    kv_sends, kv_recvs, *scratch
):
    step = pl.program_id(0)
    last = pl.num_programs(0) - 1
    place = Place()
    dp, tp = place.dp, place.tp
    rows = x_v.shape[0]
    width = full_v.shape[-1]
    partner = (flip(dp, 1), flip(tp, 1))
    sibling = place.plane(1)
    moves = place.core != tp % 2
    stays = jnp.logical_not(moves)
    gathers = [
        Gather(place, qkv, full_v, scratch[2 * j : 2 * j + 2], (j + 1,)) for j in range(3)
    ] + [Gather(place, out_w, outw_v, scratch[6:8])] + [
        Gather(place, shard, full, scratch[8 + 3 * j : 11 + 3 * j], part=j % 2)
        for j, (shard, full) in enumerate(
            ((up_w, up_full), (up_w, up_full), (down_w, down_full), (down_w, down_full))
        )
    ]
    swaps = [
        remote(source, target, (swap_sends, swap_recvs), index, partner)
        for index, (source, target) in enumerate(
            ((mel, mel_in), (noise, noise_in), (extra, extra_in), (cot, cot_in))
        )
    ]
    own_qkv = pltpu.make_async_copy(qkv, full_v.at[0], load_sems.at[0])
    own_out = pltpu.make_async_copy(out_w, outw_v.at[0], load_sems.at[11])
    loads = [
        pltpu.make_async_copy(source, target, load_sems.at[index + 1])
        for index, (source, target) in enumerate(
            (
                (facts, facts_v.at[dp]),
                (mods, mods_v.at[place.core, tp]),
                (table, table_v),
                (mel_w, mel_wv),
                (text_w, text_wv),
                (cos, cos_v),
                (sin, sin_v),
            )
        )
    ]
    frames_own = [
        pltpu.make_async_copy(source, target, load_sems.at[8 + index])
        for index, (source, target) in enumerate(((mel, mel_in), (noise, noise_in), (extra, extra_in)))
    ]
    early_saves = [(feats_v, feats_out), (text_v, text_out), (hidden_v, hidden_out), (x_v, x_out)]
    early_saves += [(facts_v, facts_all), (rows_v, mod_row), (mine_v, mine_out), (extra_in, extra_out)]
    late_saves = [(q_v, q_out), (k_v, k_out), (v_v, v_out), (ki_v, ki_out), (vi_v, vi_out)]
    late_saves += [(full_v, qkv_full), (outw_v, out_full)]
    final_saves = [(heads_v, heads_out), (lse_v, lse_out)]
    final_saves += [(sum_v, sum_out), (mid_v, mid_out), (normed_v, normed_out)]
    saves = [
        pltpu.make_async_copy(source, target, save_sems.at[index])
        for index, (source, target) in enumerate(early_saves + late_saves + final_saves)
    ]
    n_early, n_late = len(early_saves), len(late_saves)

    def kv_copies(rank):
        columns = pl.ds(pl.multiple_of(rank * width, width), width)
        return [
            remote(
                source.at[:, columns], target.at[:, columns],
                (kv_sends.at[kind], kv_recvs.at[kind]), rank, sibling,
            )
            for kind, (source, target) in enumerate(((k_v, ki_v), (v_v, vi_v)))
        ]

    @pl.when(step == 0)
    def _():
        for copy in loads:
            copy.start()
        own_qkv.start()
        own_out.start()
        greet(
            [(flip3(dp, k), tp) for k in range(1, 8)]
            + [place.ahead(step) for step in (1, 2, 3)]
            + [(flip(dp, 1), (tp + step) % 4) for step in (1, 2, 3)]
        )
        fact_copies = [
            remote(facts, facts_v.at[dp], (fact_sends, fact_recvs), k - 1, (flip3(dp, k), tp))
            for k in range(1, 8)
        ]
        mod_copies = []
        for index in range(1, 8):
            target = (flip(dp, 1) if index >= 4 else dp, (tp + index) % 4)
            mod_copies.append(
                remote(mods, mods_v.at[place.core, tp], (mod_sends, mod_recvs), index - 1, target)
            )
        @pl.when(moves)
        def _():
            for copy in swaps[:3]:
                copy.start()

        @pl.when(stays)
        def _():
            for copy in frames_own:
                copy.start()

        for copy in fact_copies + mod_copies:
            copy.start()
        gathers[0].stage0()

        @pl.when(moves)
        def _():
            for copy in swaps[:3]:
                copy.wait()

        @pl.when(stays)
        def _():
            for copy in frames_own:
                copy.wait()

        gathers[1].stage0()
        gathers[0].stage1()
        for copy in loads[:2] + fact_copies + mod_copies:
            copy.wait()
        gathers[2].stage0()
        pick = lambda pair: jnp.where(tp // 2 == 0, pair[0:1], pair[1:2])
        source = dp - place.core + tp % 2
        mine = pick(facts_v[source, 0:8, TIME_DIM : TIME_DIM + 128])
        mine_v[...] = jnp.broadcast_to(mine, mine_v.shape)
        time_here, keep_audio, keep_text = mine[:, 0:1], mine[:, 2:3], mine[:, 3:4]
        chunk = WIDTH // 2
        per_rank = mods_v.shape[-1] // chunk
        for index in range(12):
            lane = index % per_rank * chunk
            rows_v[index // 2 : index // 2 + 1, index % 2 * chunk : (index % 2 + 1) * chunk] = pick(
                mods_v[tp % 2, index // per_rank, 0:8, lane : lane + chunk]
            )
        bins = mel_wv.shape[0] // 2
        extras = extra_in[...].astype(F32)
        mel_f = mel_in[...].astype(F32)
        keep_cond = (1.0 - extras[0:1]) * keep_audio
        feats_v[0:bins] = ((1.0 - time_here) * noise_in[...].astype(F32) + time_here * mel_f).astype(BF)
        feats_v[bins : 2 * bins] = (mel_f * keep_cond).astype(BF)
        ids = (extras[1:2] * 256.0 + extras[2:3]).astype(jnp.int32)
        ids = jnp.broadcast_to(ids, (8, rows)).T[:, 0:1]
        for copy in loads[2:]:
            copy.wait()
        vocabulary = table_v.shape[0]
        span = 512
        for first in range(0, vocabulary, span):
            lane = lax.broadcasted_iota(jnp.int32, (rows, span), 1) + first
            one_hot = (lane == ids).astype(F32).astype(BF)
            term = dot(one_hot, table_v[first : first + span])
            if first == 0:
                hidden_v[:, :TEXT_DIM] = term
            else:
                hidden_v[:, :TEXT_DIM] += term
        text_v[...] = (hidden_v[:, :TEXT_DIM] * keep_text).astype(BF)
        gathers[1].stage1()
        gathers[3].stage0()
        hidden_v[...] = dot(text_v[...], text_wv[...]) + dot(feats_v[...], mel_wv[...], 0, 0)
        gathers[0].stage2()
        block = 128
        for first in range(0, rows, block):
            values = hidden_v[first : first + block]
            normed, _ = norm_parts(values)
            x_v[first : first + block] = (normed * (1.0 + rows_v[1:2]) + rows_v[0:1]).astype(BF)
        gathers[2].stage1()
        gathers[4].stage0()
        gathers[5].stage0()
        for copy in saves[:n_early]:
            copy.start()
        own_qkv.wait()

    g = gathers
    schedule = {
        1: [g[0].stage3, g[1].stage2, g[3].stage1, g[6].stage0, g[7].stage0],
        2: [g[0].stage4, g[2].stage2, g[1].stage3],
        3: [g[3].stage2, g[2].stage3, g[4].stage1],
        4: [g[1].stage4, g[5].stage1, g[3].stage3],
        5: [g[2].stage4, g[4].stage2],
        6: [g[3].stage4, g[6].stage1, g[4].stage3, g[5].stage2],
        7: [g[7].stage1, g[5].stage3],
    }
    for index, stages in schedule.items():

        @pl.when(step == index)
        def _(stages=stages):
            for stage in stages:
                stage()

    @pl.when(step % 2 == 0)
    def _():
        rank = step // 2
        columns = pl.ds(pl.multiple_of(rank * width, width), width)
        x = x_v[...]
        wide = lambda v: jnp.concatenate([v, v], axis=1)
        cosine, sine = wide(cos_v[...]), wide(sin_v[...])
        weight = lambda part: full_v[rank, part].reshape(WIDTH, width)
        k_v[:, columns] = turn(dot(x, weight(1)), cosine, sine).astype(BF)
        v_v[:, columns] = dot(x, weight(2)).astype(BF)
        for copy in kv_copies(rank):
            copy.start()
        q_v[:, columns] = turn(dot(x, weight(0)), cosine, sine).astype(BF)

        @pl.when(jnp.logical_and(step == 4, moves))
        def _():
            swaps[3].start()

        for copy in kv_copies(rank):
            copy.wait()

    @pl.when(step == last - 1)
    def _():
        own_out.wait()
        for copy in saves[n_early : n_early + n_late]:
            copy.start()

    length = mine_v[0:1, 1:2].astype(jnp.int32)
    biases = [
        key_bias(length, place.core * rows, rows),
        key_bias(length, (1 - place.core) * rows, rows),
    ]
    columns = pl.ds(pl.multiple_of(step * 2 * HEAD_DIM, 2 * HEAD_DIM), 2 * HEAD_DIM)
    output, totals = attend_pair(
        *biases, *[ref.at[:, columns] for ref in (q_v, k_v, v_v, ki_v, vi_v)]
    )
    heads_v[:, columns] = output
    lse_v[2 * step], lse_v[2 * step + 1] = totals

    @pl.when(step == last)
    def _():
        g[6].stage2()
        sum_v[...] = dot(heads_v[...], outw_v[...].reshape(WIDTH, WIDTH))
        g[7].stage2()
        block = 128
        for first in range(0, rows, block):
            here = slice(first, first + block)
            values = hidden_v[here] + rows_v[2:3] * sum_v[here]
            mid_v[here] = values
            normed, _ = norm_parts(values)
            normed_v[here] = (normed * (1.0 + rows_v[4:5]) + rows_v[3:4]).astype(BF)
        for copy in saves[n_early + n_late :]:
            copy.start()
        g[6].stage3()
        g[7].stage3()
        g[4].stage4()
        g[5].stage4()
        g[6].stage4()
        g[7].stage4()

        @pl.when(moves)
        def _():
            swaps[3].wait()

        for gather in gathers:
            gather.finish()
        for copy in saves:
            copy.wait()


def forward(mel, noise, extra, facts, mods, cot, qkv, out_w, up_w, down_w, table, mel_w, text_w, cosine, sine):
    rows = cot.shape[0]
    width = qkv.shape[2]
    dma = pltpu.SemaphoreType.DMA
    shape = lambda s, t=BF: jax.ShapeDtypeStruct(s, t)
    full = (4, 3) + pieces(qkv.shape)[1:]
    parted = [
        out_w.reshape((1,) + pieces(out_w.shape)),
        up_w.reshape((2,) + pieces((up_w.shape[0] // 2, up_w.shape[1]))),
        down_w.reshape((2,) + pieces((down_w.shape[0] // 2, down_w.shape[1]))),
    ]
    head_count = WIDTH // HEAD_DIM
    frames = (rows, WIDTH)
    feats = (mel_w.shape[0], rows)
    text = (rows, TEXT_DIM)
    all_facts = (8,) + facts.shape
    lse = (head_count, 1, rows)
    scratch = Gather.scratch() * 4
    for w in parted[1:]:
        scratch += Gather.scratch(w.shape[1:]) * 2
    outs = pl.pallas_call(
        forward_kernel,
        grid=(WIDTH // (2 * HEAD_DIM),),
        in_specs=[ANY] * 15,
        out_specs=[ANY] * 23,
        out_shape=[
            shape(all_facts, F32), shape((8, WIDTH), F32), shape((8, 128), F32), shape(extra.shape),
            shape(cot.shape), shape(full),
        ]
        + [shape((4,) + w.shape) for w in parted]
        + [shape(frames, F32), shape(frames, F32), shape(frames)]
        + [shape(feats), shape(text), shape(frames, F32), shape(frames)]
        + [shape(frames)] * 6
        + [shape(lse, F32)],
        scratch_shapes=[
            *[pltpu.VMEM(v.shape, BF) for v in (mel, noise, extra)], pltpu.VMEM(all_facts, F32),
            pltpu.VMEM((2, 4) + mods.shape, F32), pltpu.VMEM(table.shape, BF),
            pltpu.VMEM(mel_w.shape, BF), pltpu.VMEM(text_w.shape, BF),
            pltpu.VMEM(cosine.shape, F32), pltpu.VMEM(sine.shape, F32),
            pltpu.VMEM(feats, BF), pltpu.VMEM(text, BF), pltpu.VMEM(frames, F32), pltpu.VMEM(frames, BF),
        ]
        + [pltpu.VMEM(frames, BF)] * 6
        + [
            pltpu.VMEM(lse, F32), pltpu.VMEM(full, BF), pltpu.VMEM((4,) + parted[0].shape, BF),
            pltpu.VMEM(frames, F32), pltpu.VMEM(frames, F32), pltpu.VMEM(frames, BF),
            pltpu.VMEM((8, WIDTH), F32), pltpu.VMEM((8, 128), F32),
            dma((12,)), dma((20,)), dma((7,)), dma((7,)), dma((7,)), dma((7,)), dma((4,)), dma((4,)),
            dma((2, 4)), dma((2, 4)),
        ]
        + scratch,
        compiler_params=comm_params(0),
        name="forward",
    )(
        mel, noise, extra, facts, mods, cot, qkv.reshape(pieces(qkv.shape)), *parted, table, mel_w,
        text_w, cosine, sine,
    )
    outs = list(outs)
    outs[5] = outs[5].reshape(4, 3, WIDTH, width)
    outs[6:9] = [f.reshape((4,) + w.shape) for f, w in zip(outs[6:9], (out_w, up_w, down_w))]
    return outs


def qkv_kernel(x_ref, w_ref, cos_ref, sin_ref, q_ref, k_ref, v_ref, ko_ref, vo_ref, sent, send_sems, recv_sems):
    step = pl.program_id(0)
    last = pl.num_programs(0) - 1
    width = q_ref.shape[1]
    sibling = (flip(lax.axis_index("dp"), 1), lax.axis_index("tp"))

    def copies(index):
        columns = pl.ds(pl.multiple_of(index * width, width), width)
        return [
            pltpu.make_async_remote_copy(
                src_ref=sent.at[kind, index],
                dst_ref=target.at[:, columns],
                send_sem=send_sems.at[kind, index],
                recv_sem=recv_sems.at[kind, index],
                device_id=sibling,
                device_id_type=MESH,
            )
            for kind, target in ((0, ko_ref), (1, vo_ref))
        ]

    @pl.when(step == 0)
    def _():
        greet([sibling])

    x = x_ref[...]
    key = turn(dot(x, w_ref[0, 1]), cos_ref[...], sin_ref[...]).astype(BF)
    value = dot(x, w_ref[0, 2]).astype(BF)
    k_ref[...] = key
    v_ref[...] = value
    sent[0, step] = key
    sent[1, step] = value
    for copy in copies(step):
        copy.start()
    q_ref[...] = turn(dot(x, w_ref[0, 0]), cos_ref[...], sin_ref[...]).astype(BF)

    @pl.when(step == last)
    def _():
        for index in range(WIDTH // width):
            for copy in copies(index):
                copy.wait()


def project_qkv(x, weights, cosine, sine):
    rows = x.shape[0]
    ranks, width = weights.shape[0], weights.shape[3]
    tile = pl.BlockSpec((rows, width), lambda r: (0, r))
    whole = lambda shape: pl.BlockSpec(shape, lambda r: (0, 0))
    dma = pltpu.SemaphoreType.DMA
    return pl.pallas_call(
        qkv_kernel,
        grid=(ranks,),
        in_specs=[
            whole(x.shape),
            pl.BlockSpec((1, 3, WIDTH, width), lambda r: (r, 0, 0, 0)),
            whole((rows, width)),
            whole((rows, width)),
        ],
        out_specs=[tile] * 3 + [ANY] * 2,
        out_shape=[jax.ShapeDtypeStruct((rows, WIDTH), BF)] * 5,
        scratch_shapes=[pltpu.VMEM((2, ranks, rows, width), BF), dma((2, ranks)), dma((2, ranks))],
        compiler_params=comm_params(1),
        name="project_qkv",
    )(x, weights, cosine, sine)


def qkv_back_kernel(
    x_ref, w_ref, cos_ref, sin_ref, dq_ref, dk_ref, dv_ref, dki_ref, dvi_ref, grad_ref, dx_ref, xt
):
    step = pl.program_id(0)

    @pl.when(step == 0)
    def _():
        xt[...] = x_ref[...].T

    dq = dq_ref[...]
    dk = turn(dk_ref[...] + dki_ref[...].astype(F32), cos_ref[...], -sin_ref[...]).astype(BF)
    dv = (dv_ref[...] + dvi_ref[...].astype(F32)).astype(BF)
    total = None
    for part, grad in enumerate((dq, dk, dv)):
        grad_ref[0, part] = dot(xt[...], grad).astype(BF)
        term = dot(grad, w_ref[0, part], 1, 1)
        total = term if total is None else total + term

    @pl.when(step == 0)
    def _():
        dx_ref[...] = total

    @pl.when(step > 0)
    def _():
        dx_ref[...] += total


def project_qkv_back(x, weights, cosine, sine, dq, dk, dv, dk_in, dv_in):
    rows = x.shape[0]
    ranks, width = weights.shape[0], weights.shape[3]
    tile = pl.BlockSpec((rows, width), lambda r: (0, r))
    whole = lambda shape: pl.BlockSpec(shape, lambda r: (0, 0))
    wide = pl.BlockSpec((1, 3, WIDTH, width), lambda r: (r, 0, 0, 0))
    return pl.pallas_call(
        qkv_back_kernel,
        grid=(ranks,),
        in_specs=[whole(x.shape), wide, whole((rows, width)), whole((rows, width))] + [tile] * 5,
        out_specs=[wide, whole((rows, WIDTH))],
        out_shape=[
            jax.ShapeDtypeStruct(weights.shape, BF),
            jax.ShapeDtypeStruct((rows, WIDTH), F32),
        ],
        scratch_shapes=[pltpu.VMEM((WIDTH, rows), BF)],
        compiler_params=pltpu.CompilerParams(vmem_limit_bytes=VMEM_LIMIT),
        name="project_qkv_back",
    )(x, weights, cosine, sine, dq, dk, dv, dk_in, dv_in)


def mlp_kernel(
    x_ref, cot_ref, row_ref, mid_ref, sum_ref, heads_ref, out_w_ref, wu_ref, wd_ref,
    layer_ref, mid_grad_ref, heads_grad_ref, out_grad_ref, sums_ref, du_ref, dd_ref,
    xt, grad_ref, y_ref, dx_ref, attn_ref
):
    step = pl.program_id(0)
    last = pl.num_programs(0) - 1

    @pl.when(step == 0)
    def _():
        xt[...] = x_ref[...].T
        grad_ref[...] = (row_ref[5:6] * cot_ref[...].astype(F32)).astype(BF)

    up = dot(x_ref[...], wu_ref[0])
    root = math.sqrt(2.0 / math.pi)
    square = up * up
    bent = jnp.tanh(root * (up + 0.044715 * up * square))
    half = 0.5 * (1.0 + bent)
    slope = half + 0.5 * up * (1.0 - bent * bent) * root * (1.0 + 3 * 0.044715 * square)
    act = (up * half).astype(BF)
    grad = grad_ref[...]
    up_grad = (dot(grad, wd_ref[0], 1, 1) * slope).astype(BF)
    dd_ref[0] = dot(act, grad, 0, 0).astype(BF)
    du_ref[0] = dot(xt[...], up_grad).astype(BF)
    y = dot(act, wd_ref[0])
    dx = dot(up_grad, wu_ref[0], 1, 1)

    @pl.when(step == 0)
    def _():
        y_ref[...] = y
        dx_ref[...] = dx

    @pl.when(step > 0)
    def _():
        y_ref[...] += y
        dx_ref[...] += dx

    @pl.when(step == last)
    def _():
        block = 128
        totals = [jnp.zeros((1, WIDTH), F32) for _ in range(4)]
        for first in range(0, x_ref.shape[0], block):
            here = slice(first, first + block)
            values, dx, y = mid_ref[here], dx_ref[here], y_ref[here]
            out_grad = cot_ref[here].astype(F32)
            layer_ref[here] = (values + row_ref[5:6] * y).astype(BF)
            normed, inverse = norm_parts(values)
            mid_grad = out_grad + norm_back(normed, inverse, row_ref[4:5], dx)
            mid_grad_ref[here] = mid_grad
            attn_ref[here] = (row_ref[2:3] * mid_grad).astype(BF)
            for index, term in enumerate(
                (sum_ref[here] * mid_grad, dx, dx * normed, out_grad * y)
            ):
                totals[index] += jnp.sum(term, axis=0, keepdims=True)
        for index in range(4):
            sums_ref[index : index + 1] = totals[index]
        sums_ref[4:8] = jnp.zeros((4, WIDTH), F32)
        heads_grad_ref[...] = dot(attn_ref[...], out_w_ref[...], 1, 1).astype(BF)
        out_grad_ref[...] = dot(heads_ref[...], attn_ref[...], 0, 0).astype(BF)


def mlp(x, cot, mod_rows, hidden_mid, attn_sum, heads_out, out_full, up_full, down_full):
    rows = x.shape[0]
    ranks, _, units = up_full.shape
    one = lambda shape: pl.BlockSpec(shape, lambda r: (0, 0), pipeline_mode=pl.Buffered(1))
    whole, square, row = one((rows, WIDTH)), one((WIDTH, WIDTH)), one((8, WIDTH))
    up_spec = pl.BlockSpec((1, WIDTH, units), lambda r: (r, 0, 0))
    down_spec = pl.BlockSpec((1, units, WIDTH), lambda r: (r, 0, 0))
    frames = (rows, WIDTH)
    return pl.pallas_call(
        mlp_kernel,
        grid=(ranks,),
        in_specs=[whole, whole, row, whole, whole, whole, square, up_spec, down_spec],
        out_specs=[whole, whole, whole, square, row, up_spec, down_spec],
        out_shape=[
            jax.ShapeDtypeStruct(frames, BF),
            jax.ShapeDtypeStruct(frames, F32),
            jax.ShapeDtypeStruct(frames, BF),
            jax.ShapeDtypeStruct((WIDTH, WIDTH), BF),
            jax.ShapeDtypeStruct((8, WIDTH), F32),
            jax.ShapeDtypeStruct(up_full.shape, BF),
            jax.ShapeDtypeStruct(down_full.shape, BF),
        ],
        scratch_shapes=[
            pltpu.VMEM((WIDTH, rows), BF),
            pltpu.VMEM(frames, BF),
            pltpu.VMEM(frames, F32),
            pltpu.VMEM(frames, F32),
            pltpu.VMEM(frames, BF),
        ],
        compiler_params=pltpu.CompilerParams(vmem_limit_bytes=VMEM_LIMIT),
        name="mlp",
    )(x, cot, mod_rows, hidden_mid, attn_sum, heads_out, out_full, up_full, down_full)


def backward_kernel(
    q, k0, v0, k1, v1, do, o, lse, cos, sin, mine_ref, row_ref, extra_ref, mod_in_ref,
    x_ref, w_ref, value_ref, mid_ref, feat_ref, mel_w_ref, text_w_ref, proj_ref, layer_ref, down_grads, up_grads, out_grads,
    sums_ref, act_ref, mel_out, layer_out, qkv_out, misc_out, down_out, up_out, out_out,
    dq_v, dk_v, dv_v, dki_v, dvi_v, sent, xt, tiles, total_ref, hidden_ref, text_ref, blocks_v,
    feat_v, mel_wv, text_wv, qkv_grads, misc_grads, mel_v,
    mod_ref, line, every, part_ref, acts, down_buffer, up_buffer, out_buffer,
    kv_sends, kv_recvs, load_sems, tile_sems, block_sems, line_sends, line_recvs, every_sends,
    every_recvs, act_sends, act_recvs, end_sends, end_recvs, *scratch
):
    step = pl.program_id(0)
    last = pl.num_programs(0) - 1
    place = Place()
    dp, tp = place.dp, place.tp
    partner = (flip(dp, 1), flip(tp, 1))
    moves = place.core != tp % 2
    stays = jnp.logical_not(moves)
    rows = dq_v.shape[0]
    ranks, width = w_ref.shape[0], w_ref.shape[3]
    pair_width = 2 * HEAD_DIM
    steps = WIDTH // pair_width
    size = 9
    early = [
        Reduce(place, grads.at[:, h], out.at[h], scratch[size * j : size * (j + 1)], buffer)
        for j, (grads, out, h, buffer) in enumerate(
            (
                (down_grads, down_out, 0, down_buffer),
                (up_grads, up_out, 0, up_buffer),
                (down_grads, down_out, 1, down_buffer),
                (up_grads, up_out, 1, up_buffer),
                (out_grads, out_out, 0, out_buffer),
            )
        )
    ]
    late = [
        Reduce(place, qkv_grads.at[part], qkv_out.at[part], scratch[size * (5 + part) : size * (6 + part)])
        for part in range(3)
    ] + [
        Reduce(
            place, misc_grads.at[h], misc_out.at[h], scratch[size * (8 + h) : size * (9 + h)],
            absolute=True,
        )
        for h in range(2)
    ]
    loads = [
        pltpu.make_async_copy(source, target, load_sems.at[index])
        for index, (source, target) in enumerate(
            (
                (x_ref, hidden_ref),
                (feat_ref, feat_v),
                (mel_w_ref, mel_wv),
                (text_w_ref, text_wv),
            )
        )
    ]
    def tile_load(part, rank):
        number = part * ranks + rank
        return pltpu.make_async_copy(
            w_ref.at[rank, part], tiles.at[number % 2], tile_sems.at[number]
        )

    span = tiles.shape[2]
    proj_loads = [
        pltpu.make_async_copy(
            proj_ref.at[:, pl.ds(index * span, span)], tiles.at[index % 2], tile_sems.at[3 * ranks + index]
        )
        for index in range(proj_ref.shape[1] // span)
    ]
    block = blocks_v.shape[2]
    block_loads = [
        [
            pltpu.make_async_copy(
                source.at[pl.ds(index * block, block)], blocks_v.at[index % 2, kind], block_sems.at[index, kind]
            )
            for kind, source in enumerate((value_ref, mid_ref))
        ]
        for index in range(rows // block)
    ]

    def outward(index, source, target):
        away = remote(source, target, (end_sends, end_recvs), index, partner)
        here = pltpu.make_async_copy(source, target, end_sends.at[2 + index])
        return away, here

    layer_load = pltpu.make_async_copy(layer_ref, dq_v, load_sems.at[4])
    ends = [outward(0, dq_v, layer_out), outward(1, mel_v, mel_out)]
    kv_copies = lambda index: sibling_copies(
        sent, (dki_v, dvi_v), (kv_sends, kv_recvs), index, pair_width, sent.shape[1]
    )

    def send_outward(index):
        @pl.when(moves)
        def _():
            ends[index][0].start()

        @pl.when(stays)
        def _():
            ends[index][1].start()

    @pl.when(step == 0)
    def _():
        for copy in loads:
            copy.start()
        for copy in [tile_load(0, 0), tile_load(0, 1)] + block_loads[0] + block_loads[1]:
            copy.start()
        greet(
            [(flip3(dp, k), tp) for k in range(1, 8)]
            + [place.ahead(step) for step in (1, 2, 3)]
            + [partner]
        )

    flow = Flow()
    for index in range(steps):
        if index in JOINS:
            flow.add(early[JOINS.index(index)])
        stages = flow.take()

        @pl.when(step == index)
        def _(stages=stages):
            for stage in stages:
                stage()

    columns = pl.ds(pl.multiple_of(step * pair_width, pair_width), pair_width)
    slots = sent.shape[1]
    length = mine_ref[0:1, 1:2].astype(jnp.int32)
    biases = [
        key_bias(length, place.core * rows, rows),
        key_bias(length, (1 - place.core) * rows, rows),
    ]
    dq, results = attend_back_pair(biases, q, k0, v0, k1, v1, do, o, lse)
    dq_v[:, columns] = turn(dq, cos[...], -sin[...]).astype(BF)
    dk_v[:, columns] = results[0][0].astype(dk_v.dtype)
    dv_v[:, columns] = results[0][1].astype(dv_v.dtype)

    @pl.when(step >= slots)
    def _():
        for copy in kv_copies(step - slots):
            copy.wait_send()

    sent[0, step % slots] = results[1][0].astype(BF)
    sent[1, step % slots] = results[1][1].astype(BF)
    for copy in kv_copies(step):
        copy.start()

    @pl.when(step == last)
    def _():
        for copy in loads:
            copy.wait()
        flow.beat()
        xt[...] = hidden_ref[...].T
        total_ref[...] = jnp.zeros_like(total_ref)
        cosine = jnp.concatenate([cos[...]] * (width // pair_width), axis=1)
        sine = -jnp.concatenate([sin[...]] * (width // pair_width), axis=1)
        extras = extra_ref[...].astype(F32)
        ids = (extras[1:2] * 256.0 + extras[2:3]).astype(jnp.int32)
        keep_cond = (1.0 - extras[0:1]) * mine_ref[0:1, 2:3]
        for part in range(3):
            if part == 1:

                @pl.loop(0, steps)
                def _(index):
                    for copy in kv_copies(index):
                        copy.wait_recv()

                @pl.loop(steps - slots, steps)
                def _(index):
                    for copy in kv_copies(index):
                        copy.wait_send()

            def one_rank(rank, part=part):
                side = pl.ds(pl.multiple_of(rank * width, width), width)
                if part == 0:
                    grad = dq_v[:, side]
                elif part == 1:
                    grad = turn(
                        dk_v[:, side].astype(F32) + dki_v[:, side].astype(F32), cosine, sine
                    ).astype(BF)
                else:
                    grad = (dv_v[:, side].astype(F32) + dvi_v[:, side].astype(F32)).astype(BF)
                number = part * ranks + rank
                tile_load(part, rank).wait()
                qkv_grads[part, rank] = (
                    dot(xt[...], grad).astype(BF).reshape(qkv_grads.shape[2:])
                )
                total_ref[...] += dot(grad, tiles[number % 2], 1, 1)

                @pl.when(number + 2 < 3 * ranks)
                def _():
                    tile_load((number + 2) // ranks, (number + 2) % ranks).start()

            pl.loop(0, ranks // 2)(one_rank)
            flow.beat()
            pl.loop(ranks // 2, ranks)(one_rank)
            if part == 0:
                layer_load.start()
            if part == 2:
                layer_load.wait()
                send_outward(0)
            flow.add(late[part])
            flow.beat()

        chunks = mod_ref.shape[1]
        lanes = mod_ref.shape[2]
        totals = [jnp.zeros((1, WIDTH), F32) for _ in range(2)]
        for index in range(rows // block):
            here = slice(index * block, (index + 1) * block)
            for copy in block_loads[index]:
                copy.wait()
            grad = total_ref[here]
            normed, inverse = norm_parts(blocks_v[index % 2, 0])
            hidden_ref[here] = (
                blocks_v[index % 2, 1] + norm_back(normed, inverse, row_ref[1:2], grad)
            ).astype(BF)
            totals[0] += jnp.sum(grad, axis=0, keepdims=True)
            totals[1] += jnp.sum(grad * normed, axis=0, keepdims=True)
            if index + 2 < rows // block:
                for copy in block_loads[index + 2]:
                    copy.start()
        for index in range(4):
            totals.append(mod_in_ref[index : index + 1])
        for index in range(6):
            for chunk in range(WIDTH // lanes):
                row = index * (WIDTH // lanes) + chunk
                mod_ref[row // chunks, row % chunks : row % chunks + 1, :] = totals[index][
                    :, chunk * lanes : (chunk + 1) * lanes
                ]
        line_copies = [
            remote(
                mod_ref.at[(tp + step) % 4], line.at[tp], (line_sends, line_recvs), step - 1, place.ahead(step)
            )
            for step in (1, 2, 3)
        ]
        every_copies = [
            remote(line, every.at[dp], (every_sends, every_recvs), k - 1, (flip3(dp, k), tp))
            for k in range(1, 8)
        ]
        act_copies = [
            remote(part_ref, acts.at[tp], (act_sends, act_recvs), step - 1, place.ahead(step))
            for step in (1, 2, 3)
        ]
        for copy in line_copies:
            copy.start()
        line[tp] = mod_ref[tp]
        flow.beat()

        text_ref[...] = dot(hidden_ref[...], text_wv[...], 1, 1).astype(BF) * mine_ref[0:1, 3:4].astype(BF)
        table_rows = VOCABULARY // ranks
        split = misc_grads.shape[-2] * 16
        shape = misc_grads.shape[2:]

        @pl.loop(0, ranks)
        def _(rank):
            row = lax.broadcasted_iota(jnp.int32, (split, rows), 0) + rank * table_rows
            one_hot = (row == ids).astype(F32).astype(BF)
            misc_grads[0, rank] = dot(one_hot, text_ref[...]).astype(BF).reshape(shape)

        flow.add(late[3])
        flow.beat()
        for copy in line_copies:
            copy.wait()
        every[dp] = line[...]
        for copy in every_copies:
            copy.start()
        feat_rows = feat_v.shape[1] // ranks
        rest = table_rows - split

        def rest_of(rank, share):
            row = lax.broadcasted_iota(jnp.int32, (rest, rows), 0) + (rank * table_rows + split)
            one_hot = (row == ids).astype(F32).astype(BF)
            table = dot(one_hot, text_ref[...]).astype(BF)
            misc_grads[1, rank] = jnp.concatenate(
                [table, share[:, :TEXT_DIM], share[:, TEXT_DIM:]], axis=0
            ).reshape(shape)

        for rank in range(ranks):
            side = slice(rank * feat_rows, (rank + 1) * feat_rows)
            rest_of(rank, dot(feat_v[:, side], hidden_ref[...], 0, 0).astype(BF))
        flow.add(late[4])
        flow.beat()
        for copy in proj_loads[:2]:
            copy.start()
        mel_part = dot(mel_wv[...], hidden_ref[...], 1, 1)
        bins = mel_part.shape[0] // 2
        mel_v[...] = mine_ref[0:1, 0:1] * mel_part[:bins] + keep_cond * mel_part[bins:]
        send_outward(1)
        flow.beat()
        for copy in every_copies:
            copy.wait()
        for pair in range(4):
            sums_ref[pair] = every[2 * pair] + every[2 * pair + 1]
        total = None
        for index, copy in enumerate(proj_loads):
            copy.wait()
            for lane in range(0, span, lanes):
                chunk = (index * span + lane) // lanes
                held = sums_ref[:, :, chunk, :].reshape(16, lanes).astype(BF)
                term = dot(held, tiles[index % 2, :, lane : lane + lanes], 1, 1)
                total = term if total is None else total + term
            if index + 2 < len(proj_loads):
                proj_loads[index + 2].start()
        part_ref[...] = total
        acts[tp] = total
        for copy in act_copies:
            copy.start()
        while flow.beat():
            pass
        for copy in act_copies:
            copy.wait()
        act_ref[...] = acts[...]

        @pl.when(moves)
        def _():
            for away, _ in ends:
                away.wait()

        @pl.when(stays)
        def _():
            for _, here in ends:
                here.wait()


def backward(
    query, own, other, heads_grad, heads_out, lse, cosine, sine, mine, mod_rows, extra, mod_part,
    x, weights, values, mid_grad, feats, mel_w, text_w, mod_proj, layer, down_grad, up_grad, out_grad,
):
    rows = x.shape[0]
    ranks, width = weights.shape[0], weights.shape[3]
    table_rows = VOCABULARY // ranks
    misc_rows = table_rows + 2 * (feats.shape[1] // ranks)
    chunks = mod_proj.shape[1] // 128
    pairs = WIDTH // (2 * HEAD_DIM)
    qkv_block = blocks((WIDTH, width))
    misc_block = blocks((misc_rows // 2, TEXT_DIM))
    dma = pltpu.SemaphoreType.DMA
    vmem = lambda shape, t=BF: pltpu.VMEM(shape, t)
    tile = pl.BlockSpec((rows, 2 * HEAD_DIM), lambda i: (0, i))
    one = lambda v: pl.BlockSpec(v.shape, lambda i: (0,) * v.ndim, pipeline_mode=pl.Buffered(1))
    parts = lambda v, count: v.reshape(
        (ranks, count) + blocks((v.shape[1] // count, v.shape[2]))
    )
    early = (parts(down_grad, 2), parts(up_grad, 2), parts(out_grad, 1))
    scratch = []
    for index in (0, 1, 0, 1, 2):
        block = early[index].shape
        scratch += Reduce.scratch(block[-2] * 16, block[-1])
    for _ in range(3):
        scratch += Reduce.scratch(WIDTH, width)
    for _ in range(2):
        scratch += Reduce.scratch(misc_rows // 2, TEXT_DIM)
    frames = (rows, WIDTH)
    mel_shape = (mel_w.shape[0] // 2, rows)
    sums_shape = jax.ShapeDtypeStruct((4, 4, chunks, 128), F32)
    act_shape = jax.ShapeDtypeStruct((4, 16, WIDTH), F32)
    outs = pl.pallas_call(
        backward_kernel,
        grid=(pairs,),
        in_specs=[tile] * 7
        + [pl.BlockSpec((2, 1, rows), lambda i: (i, 0, 0))]
        + [one(v) for v in (cosine, sine, mine, mod_rows, extra, mod_part)]
        + [ANY] * 12,
        out_specs=[one(sums_shape), one(act_shape)] + [ANY] * 7,
        out_shape=[
            sums_shape,
            act_shape,
            jax.ShapeDtypeStruct(mel_shape, F32),
            jax.ShapeDtypeStruct(frames, BF),
            jax.ShapeDtypeStruct((3,) + qkv_block, BF),
            jax.ShapeDtypeStruct((2,) + misc_block, BF),
        ]
        + [jax.ShapeDtypeStruct(v.shape[1:], BF) for v in early],
        scratch_shapes=[
            vmem(frames), vmem(frames), vmem(frames), vmem(frames), vmem(frames),
            vmem((2, 4, rows, 2 * HEAD_DIM)), vmem((WIDTH, rows)), vmem((2, WIDTH, width)),
            vmem(frames, F32), vmem(frames), vmem((rows, TEXT_DIM)), vmem((2, 2, 64, WIDTH), F32),
            vmem(feats.shape), vmem(mel_w.shape), vmem(text_w.shape),
            vmem((3, ranks) + qkv_block), vmem((2, ranks) + misc_block), vmem(mel_shape, F32),
            vmem((4, chunks, 128), F32), vmem((4, chunks, 128), F32), vmem((8, 4, chunks, 128), F32),
            vmem((16, WIDTH), F32), vmem((4, 16, WIDTH), F32),
        ]
        + [vmem((ranks,) + v.shape[3:]) for v in early]
        + [
            dma((2, pairs)), dma((2, pairs)), dma((5,)), dma((3 * ranks + mod_proj.shape[1] // width,)),
            dma((rows // 64, 2)),
            dma((3,)), dma((3,)), dma((7,)), dma((7,)), dma((3,)), dma((3,)), dma((4,)), dma((2,)),
        ]
        + scratch,
        compiler_params=comm_params(4),
        name="backward",
    )(
        query, *own, *other, heads_grad, heads_out, lse, cosine, sine, mine, mod_rows, extra, mod_part,
        x, weights, values, mid_grad, feats, mel_w, text_w, mod_proj, layer, *early,
    )
    outs = list(outs)
    outs[4] = outs[4].reshape(3, WIDTH, width)
    outs[5] = outs[5].reshape(misc_rows, TEXT_DIM)
    outs[6:] = [o.reshape(v.shape[1:]) for o, v in zip(outs[6:], (down_grad, up_grad, out_grad))]
    return outs


def time_features(flow_times, width):
    half_dim = width // 2
    frequency = jnp.exp(
        jnp.arange(half_dim, dtype=F32) * (-math.log(10000.0) / (half_dim - 1))
    )
    angles = 1000.0 * flow_times[:, None] * frequency[None, :]
    return jnp.concatenate([jnp.sin(angles), jnp.cos(angles)], axis=1)


def rope_tables(positions, width):
    lane = jnp.arange(width, dtype=jnp.int32)
    pair = ((lane % HEAD_DIM) // 2).astype(F32)
    inverse = jnp.exp(pair * (-2.0 * math.log(10000.0) / HEAD_DIM))
    angles = positions.astype(F32)[:, None] * inverse[None, :]
    sign = jnp.where(lane % 2 == 0, -1.0, 1.0)
    return jnp.cos(angles), jnp.sin(angles) * sign[None, :]


def norm_parts(values):
    average = jnp.mean(values, axis=-1, keepdims=True)
    centered = values - average
    spread = jnp.mean(centered * centered, axis=-1, keepdims=True)
    inverse = lax.rsqrt(spread + 1e-06)
    return centered * inverse, inverse


def norm_back(normed, inverse, scale_part, grad):
    inner = grad * (1.0 + scale_part)
    first = jnp.mean(inner, axis=-1, keepdims=True)
    second = jnp.mean(inner * normed, axis=-1, keepdims=True)
    return inverse * (inner - first - normed * second)


def body(
    mel_frames, noise_frames, text_ids, span_mask, lengths, audio_drop, text_drop, flow_times,
    in_proj, text_table, time_proj, mod_proj, qkv_proj, out_proj, up_proj, down_proj, cotangent,
):
    dp_size = lax.axis_size("dp")
    tp_size = lax.axis_size("tp")
    dp_rank = lax.axis_index("dp")
    tp_rank = lax.axis_index("tp")
    local_rows = mel_frames.shape[0]
    per_group = flow_times.shape[0]
    utt_total = per_group * dp_size
    dp_low = dp_rank % 2
    tp_low = tp_rank % 2
    stay = dp_low == tp_low
    direct = dp_size == 8 and tp_size == 4
    pairs = []
    for d in range(dp_size):
        for t in range(tp_size):
            if d % 2 != t % 2:
                pairs.append((d * tp_size + t, (d ^ 1) * tp_size + (t ^ 1)))

    def swap(values):
        return jnp.where(stay, values, lax.ppermute(values, AXES, pairs))

    source_dp = dp_rank - dp_low + tp_low
    utterance = source_dp * per_group + tp_rank // 2
    half = dp_low

    def relative(values):
        return jnp.roll(values, -tp_rank, axis=0)

    def gather(shard):
        return relative(lax.all_gather(shard, "tp", axis=0))

    lane = jnp.arange(TIME_DIM + 128, dtype=jnp.int32)[None, :]
    half_dim = TIME_DIM // 2
    frequency = jnp.exp((lane % half_dim).astype(F32) * (-math.log(10000.0) / (half_dim - 1)))
    column = lambda v: v[:, None]
    angles = 1000.0 * column(flow_times) * frequency
    facts = jnp.where(lane < half_dim, jnp.sin(angles), jnp.cos(angles))
    for index, fact in enumerate((flow_times, lengths, 1 - audio_drop, 1 - text_drop)):
        facts = jnp.where(lane == TIME_DIM + index, column(fact).astype(F32), facts)
    sinus_own = facts[:, :TIME_DIM]
    act_own = jax.nn.silu(dot(sinus_own.astype(BF), time_proj)).astype(BF)
    mod_cols = dot(act_own, mod_proj)
    spare = -MEL_BINS % 16
    bins = MEL_BINS + spare
    line = jnp.arange(16, dtype=jnp.int32)[:, None]
    extra = jnp.where(
        line == 0,
        span_mask[None, :],
        jnp.where(line == 1, text_ids[None, :] // 256, jnp.where(line == 2, text_ids[None, :] % 256, 0)),
    ).astype(BF)
    padded = lambda v: jnp.pad(v, ((0, spare), (0, 0)))
    mel, noise = padded(mel_frames.T), padded(noise_frames.T)
    mel_w = jnp.concatenate(
        [padded(in_proj[:MEL_BINS]), padded(in_proj[MEL_BINS : 2 * MEL_BINS])], axis=0
    )
    text_w = in_proj[2 * MEL_BINS :]
    qkv_shard = qkv_proj.transpose(1, 0, 2)
    positions = half * local_rows + jnp.arange(local_rows, dtype=jnp.int32)
    cosine, sine = rope_tables(positions, 2 * HEAD_DIM)
    wide = lambda table: jnp.tile(table, (1, WIDTH // tp_size // (2 * HEAD_DIM)))
    if direct:
        pad = ((0, 8 - per_group), (0, 0))
        (
            facts_all, mod_rows, mine, extra, cot, qkv_full, out_full, up_full, down_full,
            attn_sum, hidden_mid, normed_mlp, feats, text_emb, hidden, normed_attn, query, key, value, key_in, value_in, heads_out, lse,
        ) = forward(
            mel, noise, extra, jnp.pad(facts, pad), jnp.pad(mod_cols, pad), cotangent, qkv_shard, out_proj, up_proj,
            down_proj, text_table, mel_w, text_w, cosine, sine,
        )
        cot = jnp.where(stay, cotangent, cot)
        facts_all = facts_all[:, :per_group].reshape(utt_total, -1)
    else:
        facts_all = lax.all_gather(facts, "dp", axis=0, tiled=True)
        near = lax.all_gather(lax.all_gather(mod_cols, "tp", axis=1, tiled=True), "dp", axis=0, tiled=True)
        mod_row = lax.dynamic_slice_in_dim(near, utterance, 1, 0)
        mel, noise, extra, cot = swap(mel), swap(noise), swap(extra), swap(cotangent)
        mine = lax.dynamic_slice_in_dim(facts_all, utterance, 1, 0)[:, TIME_DIM:]
    if not direct:
        shift_attn, scale_attn, gate_attn, shift_mlp, scale_mlp, gate_mlp = jnp.split(mod_row, 6, axis=1)
        time_here, length, keep_audio, keep_text = (mine[0, i] for i in range(4))
        length = length.astype(jnp.int32)
        extra = extra[:3].astype(jnp.int32)
        ids = extra[1] * 256 + extra[2]
        keep_cond = (1.0 - extra[0].astype(F32))[None, :] * keep_audio
        info = jnp.stack([length, half * local_rows, (1 - half) * local_rows])
        mel, noise = mel.astype(F32), noise.astype(F32)
        noisy = (1.0 - time_here) * noise + time_here * mel
        feats = jnp.concatenate([noisy, mel * keep_cond], axis=0).astype(BF)
        text_emb = (jnp.take(text_table, ids, axis=0).astype(F32) * keep_text).astype(BF)
    features = jnp.concatenate([feats[:MEL_BINS].T, feats[bins : bins + MEL_BINS].T, text_emb], axis=1)
    if not direct:
        qkv_full = gather(qkv_shard)
        hidden = dot(features, in_proj)
        norm_a, inv_a = norm_parts(hidden)
        normed_attn = (norm_a * (1.0 + scale_attn) + shift_attn).astype(BF)
        query, key, value, key_in, value_in = project_qkv(normed_attn, qkv_full, wide(cosine), wide(sine))
        heads_out, lse = attend(info, query, (key, value), (key_in, value_in))
        out_full, up_full, down_full = (gather(shard) for shard in (out_proj, up_proj, down_proj))
    own, other = (key, value), (key_in, value_in)
    out_full = out_full.reshape(WIDTH, WIDTH)
    if not direct:
        attn_sum = dot(heads_out, out_full)
        hidden_mid = hidden + gate_attn * attn_sum
        normed, _ = norm_parts(hidden_mid)
        normed_mlp = (normed * (1.0 + scale_mlp) + shift_mlp).astype(BF)
        mod_rows = jnp.pad(mod_row.reshape(6, WIDTH), ((0, 2), (0, 0)))
    layer, mid_grad, heads_grad, out_grad_w, mlp_sums, up_grad, down_grad = mlp(
        normed_mlp, cot, mod_rows, hidden_mid, attn_sum, heads_out, out_full, up_full, down_full
    )
    out_grad_w = out_grad_w.reshape(tp_size, -1, WIDTH)
    sinus = facts_all[:, :TIME_DIM].astype(BF)
    time_embed = dot(sinus, time_proj)
    time_act = jax.nn.silu(time_embed).astype(BF)
    in_rows = in_proj.shape[0] // tp_size
    in_pad = -in_rows % 64
    table_rows = VOCABULARY // tp_size
    spaced = lambda v, axis: jnp.concatenate(
        [
            jnp.pad(
                lax.slice_in_dim(v, i * in_rows, (i + 1) * in_rows, axis=axis),
                [(0, in_pad if d == axis else 0) for d in range(2)],
            )
            for i in range(tp_size)
        ],
        axis=axis,
    )
    if direct:
        sums, act_parts, mel_grad, layer_out, qkv_out, misc_out, *early_out = backward(
            query, own, other, heads_grad, heads_out, lse, cosine, sine, mine, mod_rows, extra, mlp_sums,
            normed_attn, qkv_full, hidden, mid_grad, spaced(features, 1), mel_w, text_w, mod_proj,
            layer, down_grad, up_grad, out_grad_w,
        )
        mel_grad = mel_grad[:MEL_BINS].T
        order = lambda v: v.reshape((4, 2, 2) + v.shape[2:]).swapaxes(1, 2)
        mod_sums = order(sums).reshape(utt_total, -1).astype(BF)
        act_grad = jnp.sum(act_parts, axis=0)
        act_grad = order(act_grad.reshape(4, 4, WIDTH)).reshape(utt_total, WIDTH)
    else:
        layer_out = swap(layer)
        mod_rest = mlp_sums[:4].reshape(1, 4 * WIDTH)
        column_sum = lambda values: jnp.sum(values, axis=0, keepdims=True)
        dq, dk, dv, dk_in, dv_in = attend_back(
            info, query, own, other, heads_grad, heads_out, lse, cosine, sine
        )
        qkv_grad, normed_attn_grad = project_qkv_back(
            normed_attn, qkv_full, wide(cosine), wide(sine), dq, dk, dv, dk_in, dv_in
        )
        hidden_grad = (mid_grad + norm_back(norm_a, inv_a, scale_attn, normed_attn_grad)).astype(BF)
        in_grad = dot(features, hidden_grad, 0, 0).astype(BF)
        mel_part = dot(in_proj[: 2 * MEL_BINS], hidden_grad, 1, 1)
        mel_grad = swap(
            (time_here * mel_part[:MEL_BINS] + keep_cond * mel_part[MEL_BINS:]).T
        )
        text_grad = dot(hidden_grad, in_proj[2 * MEL_BINS :], 1, 1).astype(BF) * keep_text.astype(BF)
        one_hot = (ids[None, :] == jnp.arange(VOCABULARY, dtype=jnp.int32)[:, None]).astype(BF)
        table_grad = dot(one_hot, text_grad).astype(BF).reshape(tp_size, table_rows, TEXT_DIM)
        in_grad = spaced(in_grad, 0).reshape(tp_size, in_rows + in_pad, WIDTH)
        misc = jnp.concatenate(
            [table_grad, in_grad[:, :, :TEXT_DIM], in_grad[:, :, TEXT_DIM:]], axis=1
        )
        mod_part = jnp.concatenate(
            [column_sum(normed_attn_grad), column_sum(normed_attn_grad * norm_a), mod_rest], axis=1
        )
        slot = (jnp.arange(utt_total, dtype=jnp.int32) == utterance).astype(F32)[:, None]
        mod_sums = lax.psum(
            lax.psum_scatter(slot * mod_part, "tp", scatter_dimension=1, tiled=True), "dp"
        ).astype(BF)
        act_grad = lax.psum(dot(mod_sums, mod_proj, 1, 1), "tp")

        def reduce(values):
            return lax.psum(
                lax.psum_scatter(values, "tp", scatter_dimension=0, tiled=True)[0], "dp"
            )

        absolute = lambda values: jnp.roll(values, tp_rank, axis=0)
        early_out = [reduce(absolute(values)) for values in (down_grad, up_grad, out_grad_w)]
        qkv_out = reduce(absolute(qkv_grad))
        misc_out = reduce(misc)
    mod_grad = dot(time_act, mod_sums, 0, 0)
    embed_grad = jax.vjp(jax.nn.silu, time_embed)[1](act_grad)[0].astype(BF)
    time_rows = TIME_DIM // tp_size
    sinus_share = lax.dynamic_slice_in_dim(sinus, tp_rank * time_rows, time_rows, 1)
    time_grad = dot(sinus_share, embed_grad, 0, 0)
    down_out, up_out, out_out = (values.astype(F32) for values in early_out)
    misc_out = misc_out.astype(F32)
    right = table_rows + in_rows + in_pad
    in_out = jnp.concatenate(
        [misc_out[table_rows : table_rows + in_rows], misc_out[right : right + in_rows]], axis=1
    )
    return (
        layer_out, mel_grad, in_out, misc_out[:table_rows], time_grad, mod_grad,
        qkv_out.astype(F32).transpose(1, 0, 2), out_out, up_out, down_out,
    )


def solution(mesh):
    frames = P(("dp", "tp"), None)
    frame = P(("dp", "tp"))
    return jax.shard_map(
        body,
        mesh=mesh,
        in_specs=(
            frames, frames, frame, frame, P("dp"), P("dp"), P("dp"), P("dp"),
            P(), P(), P(), P(None, "tp"), P(None, None, "tp"), P("tp", None), P(None, "tp"),
            P("tp", None), frames,
        ),
        out_specs=(
            frames, frames, P("tp", None), P("tp", None), P("tp", None), P(None, "tp"),
            P(None, None, "tp"), P("tp", None), P(None, "tp"), P("tp", None),
        ),
        check_vma=False,
    )
```

```python
import functools
import math

import jax
import jax.numpy as jnp
from jax import lax
from jax.experimental import pallas as pl
from jax.experimental.pallas import tpu as pltpu
from jax.sharding import PartitionSpec as P

WIDTH = 1024
HEAD_DIM = 64
MEL_BINS = 100
TEXT_DIM = 512
TIME_DIM = 256
VOCABULARY = 2560
FFN_DIM = 2048
AXES = ("dp", "tp")
BF = jnp.bfloat16
F32 = jnp.float32
MESH = pl.DeviceIdType.MESH
VMEM_LIMIT = 60 * 1024 * 1024
ANY = pl.BlockSpec(memory_space=pl.ANY)


def dot(left, right, left_dim=1, right_dim=0):
    return lax.dot_general(
        left, right, (((left_dim,), (right_dim,)), ((), ())), preferred_element_type=F32
    )


def flip(index, bit):
    return index + bit - 2 * bit * ((index // bit) % 2)


class Place:
    def __init__(self):
        self.dp = lax.axis_index("dp")
        self.tp = lax.axis_index("tp")
        self.core = self.dp % 2
        self.x = (self.dp // 2) % 2
        self.y = self.dp // 4

    def plane(self, bit):
        return (flip(self.dp, bit), self.tp)

    def ahead(self, step):
        return (self.dp, (self.tp + step) % 4)


def greet(devices):
    barrier = pltpu.get_barrier_semaphore()
    for device in devices:
        pl.semaphore_signal(barrier, inc=1, device_id=device, device_id_type=MESH)
    pl.semaphore_wait(barrier, len(devices))


def remote(source, target, sems, index, device):
    return pltpu.make_async_remote_copy(
        src_ref=source,
        dst_ref=target,
        send_sem=sems[0].at[index],
        recv_sem=sems[1].at[index],
        device_id=device,
        device_id_type=MESH,
    )


GATHER_COPIES = 13


class Gather:
    def __init__(self, place, shard, full, scratch, slots=(1, 2, 3), part=slice(None)):
        self.p, self.shard, self.full = place, shard, full
        self.sems, self.held = scratch[:2], (scratch[2:] or [None])[0]
        self.slots, self.part = slots, part

    @staticmethod
    def scratch(shape=None):
        dma = pltpu.SemaphoreType.DMA
        held = [] if shape is None else [pltpu.VMEM(shape, BF)]
        return [dma((GATHER_COPIES,)), dma((GATHER_COPIES,))] + held

    def view(self, *index):
        return self.full.at[(slice(self.slots[0], self.slots[-1] + 1), self.part) + index]

    def copy(self, kind):
        p = self.p
        dp = p.dp
        beside, above = flip(dp, 2), flip(dp, 4)
        across = flip(above, 2)
        if kind[0] == "z":
            step = int(kind[1])
            return remote(
                self.shard.at[self.part, dp],
                self.full.at[step, self.part, dp],
                self.sems,
                step - 1,
                p.ahead(4 - step),
            )
        index, bit, sem = {
            "x": ((dp,), 2, 3),
            "y": ((dp,), 4, 4),
            "c": ((dp,), 1, 5),
            "ya": ((beside, 0), 4, 6),
            "xb": ((above, 1), 2, 7),
            "cx": ((beside,), 1, 8),
            "cy": ((above,), 1, 9),
            "cd": ((across,), 1, 10),
        }[kind]
        return remote(self.view(*index), self.view(*index), self.sems, sem, p.plane(bit))

    def fetch(self):
        return pltpu.make_async_copy(self.shard.at[self.part], self.held, self.sems[0].at[11])

    def keep(self):
        return pltpu.make_async_copy(self.held, self.full.at[0, self.part], self.sems[0].at[12])

    def start(self, *kinds):
        for kind in kinds:
            self.copy(kind).start()

    def arrived(self, *kinds):
        for kind in kinds:
            self.copy(kind).wait_recv()

    def lines(self):
        return ["z%d" % slot for slot in self.slots]

    def stage0(self):
        self.start(*self.lines())
        if self.held is not None:
            self.fetch().start()

    def stage1(self):
        if self.held is not None:
            self.fetch().wait()
            self.keep().start()
        self.arrived(*self.lines())
        self.start("x", "y", "c")

    def stage2(self):
        self.arrived("x")
        self.start("ya", "cx")
        self.arrived("y")
        self.start("xb", "cy")

    def stage3(self):
        self.arrived("ya", "xb")
        self.start("cd")

    def stage4(self):
        self.arrived("c", "cx", "cy", "cd")

    def finish(self):
        if self.held is not None:
            self.keep().wait()
        for kind in self.lines() + ["x", "y", "c", "ya", "xb", "cx", "cy", "cd"]:
            self.copy(kind).wait_send()

    stages = property(lambda s: [s.stage0, s.stage1, s.stage2, s.stage3, s.stage4])


REDUCE_COPIES = 18


def add_into(target, source):
    for index in range(4):
        target[index] = (target[index].astype(F32) + source[index].astype(F32)).astype(BF)


class Reduce:
    @staticmethod
    def scratch(rows, columns):
        r = rows // 16
        shapes = [
            (4, 2, 2, 2, r, columns),
            (4, 2, r, columns),
            (4, 2, r, columns),
            (4, r, columns),
            (4, r, columns),
            (3, 2, r, columns),
            (2, r, columns),
        ]
        return [
            pltpu.SemaphoreType.DMA((REDUCE_COPIES,)),
            pltpu.SemaphoreType.DMA((REDUCE_COPIES,)),
        ] + [pltpu.VMEM(shape, BF) for shape in shapes]

    def __init__(self, place, grads, out, scratch, buffer=None, absolute=False):
        self.p, self.grads, self.out, self.buffer = place, grads, out, buffer
        self.sems = scratch[:2]
        self.rc, self.rx, self.ry, self.ra, self.rb, self.rz, self.fin = scratch[2:9]
        self.acc = grads.at[:, place.core] if buffer is None else self.rc
        self.first = place.tp if absolute else 0

    def slot(self, step):
        return (self.first + step) % 4

    def copy(self, kind):
        p, acc, out, fin = self.p, self.acc, self.out, self.fin
        c, x, y = p.core, p.x, p.y
        if kind in ("z1", "z2", "z3"):
            step = int(kind[1])
            return remote(
                acc.at[self.slot(step), x, y], self.rz.at[step - 1], self.sems, 4 + step, p.ahead(step)
            )
        table = {
            "c": (lambda: self.grads.at[:, 1 - c], lambda: self.rc, 1, 0),
            "x": (lambda: acc.at[:, 1 - x, :, 0], lambda: self.rx, 2, 1),
            "y": (lambda: acc.at[:, :, 1 - y, 1], lambda: self.ry, 4, 2),
            "ya": (lambda: acc.at[:, x, 1 - y, 0], lambda: self.ra, 4, 3),
            "xb": (lambda: acc.at[:, 1 - x, y, 1], lambda: self.rb, 2, 4),
            "gx": (lambda: fin, lambda: out.at[c, x, y], 2, 8),
            "gy": (lambda: fin, lambda: out.at[c, x, y], 4, 9),
            "gc": (lambda: fin, lambda: out.at[c, x, y], 1, 10),
            "gya": (lambda: out.at[c, 1 - x, y, 0], lambda: out.at[c, 1 - x, y, 0], 4, 11),
            "gxb": (lambda: out.at[c, x, 1 - y, 1], lambda: out.at[c, x, 1 - y, 1], 2, 12),
            "gcx": (lambda: out.at[c, 1 - x, y], lambda: out.at[c, 1 - x, y], 1, 13),
            "gcy": (lambda: out.at[c, x, 1 - y], lambda: out.at[c, x, 1 - y], 1, 14),
            "gcd": (lambda: out.at[c, 1 - x, 1 - y], lambda: out.at[c, 1 - x, 1 - y], 1, 15),
        }
        source, target, bit, index = table[kind]
        return remote(source(), target(), self.sems, index, p.plane(bit))

    def load(self):
        return pltpu.make_async_copy(self.grads.at[:, self.p.core], self.buffer, self.sems[0].at[16])

    def keep(self):
        p = self.p
        return pltpu.make_async_copy(self.fin, self.out.at[p.core, p.x, p.y], self.sems[0].at[17])

    def start(self, *kinds):
        for kind in kinds:
            self.copy(kind).start()

    def arrived(self, *kinds):
        for kind in kinds:
            self.copy(kind).wait_recv()

    def stage0(self):
        self.start("c")
        if self.buffer is not None:
            self.load().start()

    def stage1(self):
        self.arrived("c")
        if self.buffer is None:
            add_into(self.acc, self.rc)
        else:
            self.load().wait()
            add_into(self.rc, self.buffer)
        self.start("x", "y")

    def stage2(self):
        p = self.p
        self.arrived("x")
        add_into(self.acc.at[:, p.x, :, 0], self.rx)
        self.start("ya")
        self.arrived("y")
        add_into(self.acc.at[:, :, p.y, 1], self.ry)
        self.start("xb")

    def stage3(self):
        p = self.p
        self.arrived("ya")
        add_into(self.acc.at[:, p.x, p.y, 0], self.ra)
        self.arrived("xb")
        add_into(self.acc.at[:, p.x, p.y, 1], self.rb)
        self.start("z1", "z2", "z3")

    def stage4(self):
        p = self.p
        self.arrived("z1", "z2", "z3")
        total = self.acc[self.slot(0), p.x, p.y].astype(F32)
        for step in range(3):
            total += self.rz[step].astype(F32)
        self.fin[...] = total.astype(BF)
        self.keep().start()
        self.start("gx", "gy", "gc")

    def stage5(self):
        self.arrived("gx")
        self.start("gya", "gcx")
        self.arrived("gy")
        self.start("gxb", "gcy")

    def stage6(self):
        self.arrived("gya", "gxb")
        self.start("gcd")

    def stage7(self):
        self.arrived("gc", "gcx", "gcy", "gcd")
        self.keep().wait()
        for kind in (
            "c", "x", "y", "ya", "xb", "z1", "z2", "z3", "gx", "gy", "gc", "gya", "gxb", "gcx", "gcy", "gcd",
        ):
            self.copy(kind).wait_send()

    stages = property(
        lambda s: [s.stage0, s.stage1, s.stage2, s.stage3, s.stage4, s.stage5, s.stage6, s.stage7]
    )


def pipeline(items, first=0):
    stages = [item.stages[first:] for item in items]
    depth = max(len(held) for held in stages)
    beats = []
    for beat in range(len(items) + depth - 1):
        beats.append(
            [held[beat - j] for j, held in enumerate(stages) if 0 <= beat - j < len(held)][::-1]
        )
    return beats


LAGS = (0, 1, 4, 7, 9, 12, 14, 15)
JOINS = (0, 1, 3, 5, 7)


class Flow:
    def __init__(self):
        self.items = []
        self.now = 0

    def add(self, item):
        self.items.append([(self.now + lag, stage) for lag, stage in zip(LAGS, item.stages)])

    def take(self):
        due = [held.pop(0)[1] for held in self.items[::-1] if held and held[0][0] <= self.now]
        self.now += 1
        return due

    def beat(self):
        for stage in self.take():
            stage()
        return any(self.items)


def plane_and_line(place):
    return [place.plane(bit) for bit in (1, 2, 4)] + [place.ahead(step) for step in (1, 2, 3)]


def flip3(index, mask):
    for bit in (1, 2, 4):
        if mask & bit:
            index = flip(index, bit)
    return index


def comm_params(collective_id):
    return pltpu.CompilerParams(
        vmem_limit_bytes=VMEM_LIMIT, collective_id=collective_id, has_side_effects=True
    )


def pieces(shape):
    return tuple(shape[:-2]) + (8, 2, shape[-2] // 16, shape[-1])


def blocks(shape):
    return tuple(shape[:-2]) + (2, 2, 2, 2, shape[-2] // 16, shape[-1])


def head_masks(rows):
    lane = lax.broadcasted_iota(jnp.int32, (rows, 2 * HEAD_DIM), 1)
    return [lane < HEAD_DIM, lane >= HEAD_DIM]


def key_bias(length, start, rows):
    position = lax.broadcasted_iota(jnp.int32, (rows, 1), 0) + start
    return jnp.where(position < length, 0.0, -1e30)


def attend_pair(bias0, bias1, q_ref, k0_ref, v0_ref, k1_ref, v1_ref):
    rows = q_ref.shape[0]
    query = q_ref[...] * jnp.asarray(1.0 / math.sqrt(HEAD_DIM), BF)
    masks = head_masks(rows)
    vt0 = v0_ref[...].T
    vt1 = v1_ref[...].T
    parts, totals = [], []
    for head in range(2):
        masked = jnp.where(masks[head], query, jnp.zeros_like(query))
        s0 = dot(k0_ref[...], masked, 1, 1) + bias0
        s1 = dot(k1_ref[...], masked, 1, 1) + bias1
        peak = jnp.maximum(
            jnp.max(s0, axis=0, keepdims=True), jnp.max(s1, axis=0, keepdims=True)
        )
        e0 = jnp.exp(s0 - peak)
        e1 = jnp.exp(s1 - peak)
        total = jnp.sum(e0, axis=0, keepdims=True) + jnp.sum(e1, axis=0, keepdims=True)
        side = slice(head * HEAD_DIM, (head + 1) * HEAD_DIM)
        acc = dot(vt0[side], e0.astype(BF)) + dot(vt1[side], e1.astype(BF))
        parts.append(acc / total)
        totals.append(peak + jnp.log(total))
    return jnp.concatenate(parts, axis=0).T.astype(BF), totals


def attend_back_pair(biases, q_ref, k0_ref, v0_ref, k1_ref, v1_ref, do_ref, o_ref, lse_ref):
    rows = q_ref.shape[0]
    keys = k0_ref.shape[0]
    width = 2 * HEAD_DIM
    scale = 1.0 / math.sqrt(HEAD_DIM)
    query = q_ref[...] * jnp.asarray(scale, BF)
    grads = do_ref[...]
    product = (grads.astype(F32) * o_ref[...].astype(F32)).T
    sides = ((k0_ref, v0_ref), (k1_ref, v1_ref))
    turned = [k_ref[...].T for k_ref, _ in sides]

    def one_head(head, carry):
        dq, sums = carry[0], list(carry[1:])
        lane = lax.broadcasted_iota(jnp.int32, (rows, width), 1) // HEAD_DIM
        line = lax.broadcasted_iota(jnp.int32, (width, 1), 0) // HEAD_DIM
        masked = jnp.where(lane == head, query, jnp.zeros_like(query))
        gmask = jnp.where(lane == head, grads, jnp.zeros_like(grads))
        delta = jnp.sum(jnp.where(line == head, product, 0.0), axis=0, keepdims=True)
        total = lse_ref[head]
        for which, (k_ref, v_ref) in enumerate(sides):
            scores = dot(k_ref[...], masked, 1, 1) + biases[which]
            probs = jnp.exp(scores - total)
            prob_grad = dot(v_ref[...], gmask, 1, 1)
            score_grad = (probs * (prob_grad - delta)).astype(BF)
            sums[2 * which] += dot(score_grad, masked)
            sums[2 * which + 1] += dot(probs.astype(BF), gmask)
            kt = jnp.where(line == head, turned[which].astype(F32), 0.0).astype(BF)
            dq += dot(kt, score_grad)
        return (dq, *sums)

    start = (jnp.zeros((width, rows), F32),) + (jnp.zeros((keys, width), F32),) * 4
    dq, *sums = lax.fori_loop(0, 2, one_head, start)
    return dq.T * scale, [sums[:2], sums[2:]]


def turn(values, cosine, sine):
    lane = lax.broadcasted_iota(jnp.int32, values.shape, 1)
    width = values.shape[1]
    other = jnp.where(
        lane % 2 == 0, pltpu.roll(values, width - 1, 1), pltpu.roll(values, 1, 1)
    )
    return values * cosine + other * sine


def attend_kernel(info_ref, q, k0, v0, k1, v1, o_ref, lse_ref):
    keys = k0.shape[0]
    biases = [key_bias(info_ref[0], info_ref[1 + which], keys) for which in range(2)]
    o_ref[...], (lse_ref[0], lse_ref[1]) = attend_pair(*biases, q, k0, v0, k1, v1)


def attend(info, query, own, other):
    rows = query.shape[0]
    pairs = WIDTH // (2 * HEAD_DIM)
    tile = pl.BlockSpec((rows, 2 * HEAD_DIM), lambda i: (0, i))
    return pl.pallas_call(
        attend_kernel,
        grid=(pairs,),
        in_specs=[pl.BlockSpec(memory_space=pltpu.SMEM)] + [tile] * 5,
        out_specs=[tile, pl.BlockSpec((2, 1, rows), lambda i: (i, 0, 0))],
        out_shape=[
            jax.ShapeDtypeStruct((rows, WIDTH), BF),
            jax.ShapeDtypeStruct((2 * pairs, 1, rows), F32),
        ],
        compiler_params=pltpu.CompilerParams(vmem_limit_bytes=VMEM_LIMIT),
        name="attend",
    )(info, query, *own, *other)


def sibling_copies(sent, targets, sems, index, width, slots):
    columns = pl.ds(pl.multiple_of(index * width, width), width)
    return [
        pltpu.make_async_remote_copy(
            src_ref=sent.at[kind, index % slots],
            dst_ref=target.at[:, columns],
            send_sem=sems[0].at[kind, index],
            recv_sem=sems[1].at[kind, index],
            device_id=(flip(lax.axis_index("dp"), 1), lax.axis_index("tp")),
            device_id_type=MESH,
        )
        for kind, target in enumerate(targets)
    ]


def attend_back_kernel(
    info_ref, q, k0, v0, k1, v1, do, o, lse, cos, sin,
    dq_ref, dk_ref, dv_ref, dk_in, dv_in, sent, *sems
):
    step = pl.program_id(0)
    last = pl.num_programs(0) - 1
    width = 2 * HEAD_DIM
    steps = WIDTH // width
    copies = lambda index: sibling_copies(sent, (dk_in, dv_in), sems, index, width, steps)

    @pl.when(step == 0)
    def _():
        greet([(flip(lax.axis_index("dp"), 1), lax.axis_index("tp"))])

    keys = k0.shape[0]
    biases = [key_bias(info_ref[0], info_ref[1 + which], keys) for which in range(2)]
    dq, results = attend_back_pair(biases, q, k0, v0, k1, v1, do, o, lse)
    dq_ref[...] = turn(dq, cos[...], -sin[...]).astype(BF)
    dk_ref[...], dv_ref[...] = results[0]
    sent[0, step] = results[1][0].astype(BF)
    sent[1, step] = results[1][1].astype(BF)
    for copy in copies(step):
        copy.start()

    @pl.when(step == last)
    def _():
        for index in range(steps):
            for copy in copies(index):
                copy.wait()


def attend_back(info, query, own, other, heads_grad, outputs, lse, cosine, sine):
    rows = query.shape[0]
    pairs = WIDTH // (2 * HEAD_DIM)
    width = 2 * HEAD_DIM
    tile = pl.BlockSpec((rows, width), lambda i: (0, i))
    fixed = pl.BlockSpec((rows, width), lambda i: (0, 0))
    dma = pltpu.SemaphoreType.DMA
    return pl.pallas_call(
        attend_back_kernel,
        grid=(pairs,),
        in_specs=[pl.BlockSpec(memory_space=pltpu.SMEM)]
        + [tile] * 7
        + [pl.BlockSpec((2, 1, rows), lambda i: (i, 0, 0)), fixed, fixed],
        out_specs=[tile] * 3 + [ANY] * 2,
        out_shape=[
            jax.ShapeDtypeStruct((rows, WIDTH), BF),
            jax.ShapeDtypeStruct((rows, WIDTH), F32),
            jax.ShapeDtypeStruct((rows, WIDTH), F32),
            jax.ShapeDtypeStruct((rows, WIDTH), BF),
            jax.ShapeDtypeStruct((rows, WIDTH), BF),
        ],
        scratch_shapes=[
            pltpu.VMEM((2, pairs, rows, width), BF),
            dma((2, pairs)),
            dma((2, pairs)),
        ],
        compiler_params=comm_params(3),
        name="attend_back",
    )(info, query, *own, *other, heads_grad, outputs, lse, cosine, sine)


def forward_kernel(
    mel, noise, extra, facts, mods, cot, qkv, out_w, up_w, down_w, table, mel_w, text_w, cos, sin,
    facts_all, mod_row, mine_out, extra_out, qkv_full, feats_out, text_out, hidden_out, x_out,
    q_out, k_out, v_out, ki_out, vi_out, heads_out, lse_out,
    layer_out, mid_out, heads_grad_out, out_grad_out, sums_out, up_out, down_out,
    mel_in, noise_in, extra_in, facts_v, mods_v, table_v, mel_wv, text_wv, cos_v, sin_v,
    feats_v, text_v, hidden_v, x_v, q_v, k_v, v_v, ki_v, vi_v, heads_v, lse_v, full_v, outw_v,
    up_v, down_v, cot_v, sum_v, mid_v, normed_v, y_v, xt, up_ring, down_ring, rows_v, mine_v, sums_v,
    load_sems, save_sems, ring_sems, fact_sends, fact_recvs, mod_sends, mod_recvs, swap_sends, swap_recvs,
    kv_sends, kv_recvs, *scratch
):
    step = pl.program_id(0)
    steps = WIDTH // (2 * HEAD_DIM)
    last = steps - 1
    place = Place()
    dp, tp = place.dp, place.tp
    rows = x_v.shape[0]
    width = full_v.shape[-1]
    partner = (flip(dp, 1), flip(tp, 1))
    sibling = place.plane(1)
    moves = place.core != tp % 2
    stays = jnp.logical_not(moves)
    gathers = [
        Gather(place, qkv, full_v, scratch[2 * j : 2 * j + 2], (j + 1,)) for j in range(3)
    ] + [Gather(place, out_w, outw_v, scratch[6:8])] + [
        Gather(place, shard, full, scratch[8 + 2 * j : 10 + 2 * j], (j // 2 + 1,))
        for j, (shard, full) in enumerate(((up_w, up_v), (down_w, down_v)) * 3)
    ]
    swaps = [
        remote(source, target, (swap_sends, swap_recvs), index, partner)
        for index, (source, target) in enumerate(
            ((mel, mel_in), (noise, noise_in), (extra, extra_in), (cot, cot_v))
        )
    ]
    own_qkv = pltpu.make_async_copy(qkv, full_v.at[0], load_sems.at[0])
    own_rest = [
        pltpu.make_async_copy(shard, full.at[0], load_sems.at[11 + index])
        for index, (shard, full) in enumerate(((out_w, outw_v), (up_w, up_v), (down_w, down_v)))
    ]
    own_cot = pltpu.make_async_copy(cot, cot_v, load_sems.at[14])
    loads = [
        pltpu.make_async_copy(source, target, load_sems.at[index + 1])
        for index, (source, target) in enumerate(
            (
                (facts, facts_v.at[dp]),
                (mods, mods_v.at[place.core, tp]),
                (table, table_v),
                (mel_w, mel_wv),
                (text_w, text_wv),
                (cos, cos_v),
                (sin, sin_v),
            )
        )
    ]
    frames_own = [
        pltpu.make_async_copy(source, target, load_sems.at[8 + index])
        for index, (source, target) in enumerate(((mel, mel_in), (noise, noise_in), (extra, extra_in)))
    ]
    early_saves = [(feats_v, feats_out), (text_v, text_out), (hidden_v, hidden_out), (x_v, x_out)]
    early_saves += [(facts_v, facts_all), (rows_v, mod_row), (mine_v, mine_out), (extra_in, extra_out)]
    late_saves = [(q_v, q_out), (k_v, k_out), (v_v, v_out), (ki_v, ki_out), (vi_v, vi_out)]
    late_saves += [(full_v, qkv_full)]
    final_saves = [(heads_v, heads_out), (lse_v, lse_out)]
    end_saves = [(k_v, layer_out), (mid_v, mid_out), (v_v, heads_grad_out), (outw_v, out_grad_out)]
    end_saves += [(sums_v, sums_out)]
    saves = [
        pltpu.make_async_copy(source, target, save_sems.at[index])
        for index, (source, target) in enumerate(early_saves + late_saves + final_saves + end_saves)
    ]
    n_early, n_late = len(early_saves), len(late_saves)
    n_final = n_early + n_late + len(final_saves)

    def ring_copies(rank):
        return [
            pltpu.make_async_copy(ring.at[rank % 2], target.at[rank], ring_sems.at[kind, rank])
            for kind, (ring, target) in enumerate(((up_ring, up_out), (down_ring, down_out)))
        ]

    def kv_copies(rank):
        columns = pl.ds(pl.multiple_of(rank * width, width), width)
        return [
            remote(
                source.at[:, columns], target.at[:, columns],
                (kv_sends.at[kind], kv_recvs.at[kind]), rank, sibling,
            )
            for kind, (source, target) in enumerate(((k_v, ki_v), (v_v, vi_v)))
        ]

    @pl.when(step == 0)
    def _():
        for copy in loads:
            copy.start()
        own_qkv.start()
        for copy in own_rest:
            copy.start()
        greet(
            [(flip3(dp, k), tp) for k in range(1, 8)]
            + [place.ahead(step) for step in (1, 2, 3)]
            + [(flip(dp, 1), (tp + step) % 4) for step in (1, 2, 3)]
        )
        fact_copies = [
            remote(facts, facts_v.at[dp], (fact_sends, fact_recvs), k - 1, (flip3(dp, k), tp))
            for k in range(1, 8)
        ]
        mod_copies = []
        for index in range(1, 8):
            target = (flip(dp, 1) if index >= 4 else dp, (tp + index) % 4)
            mod_copies.append(
                remote(mods, mods_v.at[place.core, tp], (mod_sends, mod_recvs), index - 1, target)
            )
        @pl.when(moves)
        def _():
            for copy in swaps[:3]:
                copy.start()

        @pl.when(stays)
        def _():
            for copy in frames_own:
                copy.start()

        for copy in fact_copies + mod_copies:
            copy.start()
        gathers[0].stage0()

        @pl.when(moves)
        def _():
            for copy in swaps[:3]:
                copy.wait()

        @pl.when(stays)
        def _():
            for copy in frames_own:
                copy.wait()

        gathers[1].stage0()
        gathers[0].stage1()
        for copy in loads[:2] + fact_copies + mod_copies:
            copy.wait()
        gathers[2].stage0()
        pick = lambda pair: jnp.where(tp // 2 == 0, pair[0:1], pair[1:2])
        source = dp - place.core + tp % 2
        mine = pick(facts_v[source, 0:8, TIME_DIM : TIME_DIM + 128])
        mine_v[...] = jnp.broadcast_to(mine, mine_v.shape)
        time_here, keep_audio, keep_text = mine[:, 0:1], mine[:, 2:3], mine[:, 3:4]
        chunk = WIDTH // 2
        per_rank = mods_v.shape[-1] // chunk
        for index in range(12):
            lane = index % per_rank * chunk
            rows_v[index // 2 : index // 2 + 1, index % 2 * chunk : (index % 2 + 1) * chunk] = pick(
                mods_v[tp % 2, index // per_rank, 0:8, lane : lane + chunk]
            )
        bins = mel_wv.shape[0] // 2
        extras = extra_in[...].astype(F32)
        mel_f = mel_in[...].astype(F32)
        keep_cond = (1.0 - extras[0:1]) * keep_audio
        feats_v[0:bins] = ((1.0 - time_here) * noise_in[...].astype(F32) + time_here * mel_f).astype(BF)
        feats_v[bins : 2 * bins] = (mel_f * keep_cond).astype(BF)
        ids = (extras[1:2] * 256.0 + extras[2:3]).astype(jnp.int32)
        ids = jnp.broadcast_to(ids, (8, rows)).T[:, 0:1]
        for copy in loads[2:]:
            copy.wait()
        vocabulary = table_v.shape[0]
        span = 512
        for first in range(0, vocabulary, span):
            lane = lax.broadcasted_iota(jnp.int32, (rows, span), 1) + first
            one_hot = (lane == ids).astype(F32).astype(BF)
            term = dot(one_hot, table_v[first : first + span])
            if first == 0:
                hidden_v[:, :TEXT_DIM] = term
            else:
                hidden_v[:, :TEXT_DIM] += term
        text_v[...] = (hidden_v[:, :TEXT_DIM] * keep_text).astype(BF)
        gathers[1].stage1()
        gathers[3].stage0()
        hidden_v[...] = dot(text_v[...], text_wv[...]) + dot(feats_v[...], mel_wv[...], 0, 0)
        gathers[0].stage2()
        block = 128
        for first in range(0, rows, block):
            values = hidden_v[first : first + block]
            normed, _ = norm_parts(values)
            x_v[first : first + block] = (normed * (1.0 + rows_v[1:2]) + rows_v[0:1]).astype(BF)
        gathers[2].stage1()
        gathers[4].stage0()
        gathers[5].stage0()
        for copy in saves[:n_early]:
            copy.start()
        own_qkv.wait()

    g = gathers
    schedule = {
        1: [g[0].stage3, g[1].stage2, g[3].stage1, g[6].stage0, g[7].stage0],
        2: [g[0].stage4, g[2].stage2, g[1].stage3, g[4].stage1],
        3: [g[3].stage2, g[2].stage3, g[5].stage1, g[8].stage0, g[9].stage0],
        4: [g[1].stage4, g[4].stage2, g[3].stage3],
        5: [g[2].stage4, g[5].stage2, g[6].stage1],
        6: [g[4].stage3, g[7].stage1, g[3].stage4],
        7: [g[5].stage3, g[6].stage2, g[8].stage1],
        8: [g[9].stage1, g[7].stage2, g[6].stage3],
        9: [g[8].stage2, g[7].stage3, g[4].stage4, g[5].stage4],
        10: [g[9].stage2, g[8].stage3, g[6].stage4, g[7].stage4],
        11: [g[9].stage3, g[8].stage4, g[9].stage4],
    }
    for index, stages in schedule.items():

        @pl.when(step == index)
        def _(stages=stages):
            for stage in stages:
                stage()

    @pl.when(jnp.logical_and(step % 2 == 0, step < steps))
    def _():
        rank = step // 2
        columns = pl.ds(pl.multiple_of(rank * width, width), width)
        x = x_v[...]
        wide = lambda v: jnp.concatenate([v, v], axis=1)
        cosine, sine = wide(cos_v[...]), wide(sin_v[...])
        weight = lambda part: full_v[rank, part].reshape(WIDTH, width)
        k_v[:, columns] = turn(dot(x, weight(1)), cosine, sine).astype(BF)
        v_v[:, columns] = dot(x, weight(2)).astype(BF)
        for copy in kv_copies(rank):
            copy.start()
        q_v[:, columns] = turn(dot(x, weight(0)), cosine, sine).astype(BF)

        @pl.when(jnp.logical_and(step == 4, moves))
        def _():
            swaps[3].start()

        @pl.when(jnp.logical_and(step == 4, stays))
        def _():
            own_cot.start()

        for copy in kv_copies(rank):
            copy.wait()

    @pl.when(step == last - 1)
    def _():
        for copy in saves[n_early : n_early + n_late]:
            copy.start()

    @pl.when(step < steps)
    def _():
        length = mine_v[0:1, 1:2].astype(jnp.int32)
        biases = [
            key_bias(length, place.core * rows, rows),
            key_bias(length, (1 - place.core) * rows, rows),
        ]
        columns = pl.ds(pl.multiple_of(step * 2 * HEAD_DIM, 2 * HEAD_DIM), 2 * HEAD_DIM)
        output, totals = attend_pair(
            *biases, *[ref.at[:, columns] for ref in (q_v, k_v, v_v, ki_v, vi_v)]
        )
        heads_v[:, columns] = output
        lse_v[2 * step], lse_v[2 * step + 1] = totals

    block = 128

    @pl.when(step == last)
    def _():
        for copy in saves[n_early + n_late : n_final]:
            copy.start()
        for copy in own_rest:
            copy.wait()
        sum_v[...] = dot(heads_v[...], outw_v[...].reshape(WIDTH, WIDTH))
        for first in range(0, rows, block):
            here = slice(first, first + block)
            values = hidden_v[here] + rows_v[2:3] * sum_v[here]
            mid_v[here] = values
            normed, _ = norm_parts(values)
            normed_v[here] = (normed * (1.0 + rows_v[4:5]) + rows_v[3:4]).astype(BF)
        for copy in saves[: n_early + n_late]:
            copy.wait()

        @pl.when(moves)
        def _():
            swaps[3].wait()

        @pl.when(stays)
        def _():
            own_cot.wait()

        xt[...] = normed_v[...].T
        ki_v[...] = (rows_v[5:6] * cot_v[...].astype(F32)).astype(BF)
        y_v[...] = jnp.zeros_like(y_v)
        hidden_v[...] = jnp.zeros_like(hidden_v)

    @pl.when(step >= steps)
    def _():
        rank = step - steps

        @pl.when(rank >= 2)
        def _():
            for copy in ring_copies(rank - 2):
                copy.wait()

        units = down_v.shape[2] * down_v.shape[3] * down_v.shape[4]
        up_weight = up_v[rank, 0].reshape(WIDTH, units)
        down_weight = down_v[rank, 0].reshape(units, WIDTH)
        act, slope = gelu_parts(dot(normed_v[...], up_weight))
        grad = ki_v[...]
        up_grad = (dot(grad, down_weight, 1, 1) * slope).astype(BF)
        down_ring[rank % 2] = dot(act, grad, 0, 0).astype(BF)
        up_ring[rank % 2] = dot(xt[...], up_grad).astype(BF)
        for copy in ring_copies(rank):
            copy.start()
        y_v[...] += dot(act, down_weight)
        hidden_v[...] += dot(up_grad, up_weight, 1, 1)

    @pl.when(step == pl.num_programs(0) - 1)
    def _():
        totals = [jnp.zeros((1, WIDTH), F32) for _ in range(4)]
        for first in range(0, rows, block):
            here = slice(first, first + block)
            values, dx, y = mid_v[here], hidden_v[here], y_v[here]
            out_grad = cot_v[here].astype(F32)
            k_v[here] = (values + rows_v[5:6] * y).astype(BF)
            normed, inverse = norm_parts(values)
            mid_grad = out_grad + norm_back(normed, inverse, rows_v[4:5], dx)
            mid_v[here] = mid_grad
            q_v[here] = (rows_v[2:3] * mid_grad).astype(BF)
            for index, term in enumerate(
                (sum_v[here] * mid_grad, dx, dx * normed, out_grad * y)
            ):
                totals[index] += jnp.sum(term, axis=0, keepdims=True)
        for index in range(4):
            sums_v[index : index + 1] = totals[index]
        sums_v[4:8] = jnp.zeros((4, WIDTH), F32)
        for copy in saves[n_final : n_final + 2] + saves[n_final + 4 :]:
            copy.start()
        v_v[...] = dot(q_v[...], outw_v[...].reshape(WIDTH, WIDTH), 1, 1).astype(BF)
        saves[n_final + 2].start()
        for gather in gathers:
            gather.finish()
        outw_v[...] = dot(heads_v[...], q_v[...], 0, 0).astype(BF).reshape(outw_v.shape)
        saves[n_final + 3].start()
        for rank in (2, 3):
            for copy in ring_copies(rank):
                copy.wait()
        for copy in saves[n_early + n_late :]:
            copy.wait()


def forward(mel, noise, extra, facts, mods, cot, qkv, out_w, up_w, down_w, table, mel_w, text_w, cosine, sine):
    rows = cot.shape[0]
    width = qkv.shape[2]
    dma = pltpu.SemaphoreType.DMA
    shape = lambda s, t=BF: jax.ShapeDtypeStruct(s, t)
    full = (4, 3) + pieces(qkv.shape)[1:]
    parted = [w.reshape((1,) + pieces(w.shape)) for w in (out_w, up_w, down_w)]
    head_count = WIDTH // HEAD_DIM
    frames = (rows, WIDTH)
    feats = (mel_w.shape[0], rows)
    text = (rows, TEXT_DIM)
    all_facts = (8,) + facts.shape
    lse = (head_count, 1, rows)
    outs = pl.pallas_call(
        forward_kernel,
        grid=(WIDTH // (2 * HEAD_DIM) + 4,),
        in_specs=[ANY] * 15,
        out_specs=[ANY] * 23,
        out_shape=[
            shape(all_facts, F32), shape((8, WIDTH), F32), shape((8, 128), F32), shape(extra.shape),
            shape(full), shape(feats), shape(text), shape(frames, F32), shape(frames),
        ]
        + [shape(frames)] * 6
        + [shape(lse, F32)]
        + [shape(frames), shape(frames, F32), shape(frames), shape((4,) + parted[0].shape)]
        + [shape((8, WIDTH), F32), shape((4,) + up_w.shape), shape((4,) + down_w.shape)],
        scratch_shapes=[
            *[pltpu.VMEM(v.shape, BF) for v in (mel, noise, extra)], pltpu.VMEM(all_facts, F32),
            pltpu.VMEM((2, 4) + mods.shape, F32), pltpu.VMEM(table.shape, BF),
            pltpu.VMEM(mel_w.shape, BF), pltpu.VMEM(text_w.shape, BF),
            pltpu.VMEM(cosine.shape, F32), pltpu.VMEM(sine.shape, F32),
            pltpu.VMEM(feats, BF), pltpu.VMEM(text, BF), pltpu.VMEM(frames, F32), pltpu.VMEM(frames, BF),
        ]
        + [pltpu.VMEM(frames, BF)] * 6
        + [pltpu.VMEM(lse, F32), pltpu.VMEM(full, BF)]
        + [pltpu.VMEM((4,) + w.shape, BF) for w in parted]
        + [
            pltpu.VMEM(frames, BF), pltpu.VMEM(frames, F32), pltpu.VMEM(frames, F32),
            pltpu.VMEM(frames, BF), pltpu.VMEM(frames, F32), pltpu.VMEM((WIDTH, rows), BF),
            pltpu.VMEM((2,) + up_w.shape, BF), pltpu.VMEM((2,) + down_w.shape, BF),
            pltpu.VMEM((8, WIDTH), F32), pltpu.VMEM((8, 128), F32), pltpu.VMEM((8, WIDTH), F32),
            dma((15,)), dma((24,)), dma((2, 4)), dma((7,)), dma((7,)), dma((7,)), dma((7,)), dma((4,)),
            dma((4,)), dma((2, 4)), dma((2, 4)),
        ]
        + Gather.scratch() * 10,
        compiler_params=comm_params(0),
        name="forward",
    )(
        mel, noise, extra, facts, mods, cot, qkv.reshape(pieces(qkv.shape)), *parted, table, mel_w,
        text_w, cosine, sine,
    )
    outs = list(outs)
    outs[4] = outs[4].reshape(4, 3, WIDTH, width)
    outs[19] = outs[19].reshape((4,) + out_w.shape)
    return outs


def qkv_kernel(x_ref, w_ref, cos_ref, sin_ref, q_ref, k_ref, v_ref, ko_ref, vo_ref, sent, send_sems, recv_sems):
    step = pl.program_id(0)
    last = pl.num_programs(0) - 1
    width = q_ref.shape[1]
    sibling = (flip(lax.axis_index("dp"), 1), lax.axis_index("tp"))

    def copies(index):
        columns = pl.ds(pl.multiple_of(index * width, width), width)
        return [
            pltpu.make_async_remote_copy(
                src_ref=sent.at[kind, index],
                dst_ref=target.at[:, columns],
                send_sem=send_sems.at[kind, index],
                recv_sem=recv_sems.at[kind, index],
                device_id=sibling,
                device_id_type=MESH,
            )
            for kind, target in ((0, ko_ref), (1, vo_ref))
        ]

    @pl.when(step == 0)
    def _():
        greet([sibling])

    x = x_ref[...]
    key = turn(dot(x, w_ref[0, 1]), cos_ref[...], sin_ref[...]).astype(BF)
    value = dot(x, w_ref[0, 2]).astype(BF)
    k_ref[...] = key
    v_ref[...] = value
    sent[0, step] = key
    sent[1, step] = value
    for copy in copies(step):
        copy.start()
    q_ref[...] = turn(dot(x, w_ref[0, 0]), cos_ref[...], sin_ref[...]).astype(BF)

    @pl.when(step == last)
    def _():
        for index in range(WIDTH // width):
            for copy in copies(index):
                copy.wait()


def project_qkv(x, weights, cosine, sine):
    rows = x.shape[0]
    ranks, width = weights.shape[0], weights.shape[3]
    tile = pl.BlockSpec((rows, width), lambda r: (0, r))
    whole = lambda shape: pl.BlockSpec(shape, lambda r: (0, 0))
    dma = pltpu.SemaphoreType.DMA
    return pl.pallas_call(
        qkv_kernel,
        grid=(ranks,),
        in_specs=[
            whole(x.shape),
            pl.BlockSpec((1, 3, WIDTH, width), lambda r: (r, 0, 0, 0)),
            whole((rows, width)),
            whole((rows, width)),
        ],
        out_specs=[tile] * 3 + [ANY] * 2,
        out_shape=[jax.ShapeDtypeStruct((rows, WIDTH), BF)] * 5,
        scratch_shapes=[pltpu.VMEM((2, ranks, rows, width), BF), dma((2, ranks)), dma((2, ranks))],
        compiler_params=comm_params(1),
        name="project_qkv",
    )(x, weights, cosine, sine)


def qkv_back_kernel(
    x_ref, w_ref, cos_ref, sin_ref, dq_ref, dk_ref, dv_ref, dki_ref, dvi_ref, grad_ref, dx_ref, xt
):
    step = pl.program_id(0)

    @pl.when(step == 0)
    def _():
        xt[...] = x_ref[...].T

    dq = dq_ref[...]
    dk = turn(dk_ref[...] + dki_ref[...].astype(F32), cos_ref[...], -sin_ref[...]).astype(BF)
    dv = (dv_ref[...] + dvi_ref[...].astype(F32)).astype(BF)
    total = None
    for part, grad in enumerate((dq, dk, dv)):
        grad_ref[0, part] = dot(xt[...], grad).astype(BF)
        term = dot(grad, w_ref[0, part], 1, 1)
        total = term if total is None else total + term

    @pl.when(step == 0)
    def _():
        dx_ref[...] = total

    @pl.when(step > 0)
    def _():
        dx_ref[...] += total


def project_qkv_back(x, weights, cosine, sine, dq, dk, dv, dk_in, dv_in):
    rows = x.shape[0]
    ranks, width = weights.shape[0], weights.shape[3]
    tile = pl.BlockSpec((rows, width), lambda r: (0, r))
    whole = lambda shape: pl.BlockSpec(shape, lambda r: (0, 0))
    wide = pl.BlockSpec((1, 3, WIDTH, width), lambda r: (r, 0, 0, 0))
    return pl.pallas_call(
        qkv_back_kernel,
        grid=(ranks,),
        in_specs=[whole(x.shape), wide, whole((rows, width)), whole((rows, width))] + [tile] * 5,
        out_specs=[wide, whole((rows, WIDTH))],
        out_shape=[
            jax.ShapeDtypeStruct(weights.shape, BF),
            jax.ShapeDtypeStruct((rows, WIDTH), F32),
        ],
        scratch_shapes=[pltpu.VMEM((WIDTH, rows), BF)],
        compiler_params=pltpu.CompilerParams(vmem_limit_bytes=VMEM_LIMIT),
        name="project_qkv_back",
    )(x, weights, cosine, sine, dq, dk, dv, dk_in, dv_in)


def gelu_parts(up):
    root = math.sqrt(2.0 / math.pi)
    square = up * up
    bent = jnp.tanh(root * (up + 0.044715 * up * square))
    half = 0.5 * (1.0 + bent)
    slope = half + 0.5 * up * (1.0 - bent * bent) * root * (1.0 + 3 * 0.044715 * square)
    return (up * half).astype(BF), slope


def mlp_kernel(
    x_ref, cot_ref, row_ref, mid_ref, sum_ref, heads_ref, out_w_ref, wu_ref, wd_ref,
    layer_ref, mid_grad_ref, heads_grad_ref, out_grad_ref, sums_ref, du_ref, dd_ref,
    xt, grad_ref, y_ref, dx_ref, attn_ref
):
    step = pl.program_id(0)
    last = pl.num_programs(0) - 1

    @pl.when(step == 0)
    def _():
        xt[...] = x_ref[...].T
        grad_ref[...] = (row_ref[5:6] * cot_ref[...].astype(F32)).astype(BF)

    act, slope = gelu_parts(dot(x_ref[...], wu_ref[0]))
    grad = grad_ref[...]
    up_grad = (dot(grad, wd_ref[0], 1, 1) * slope).astype(BF)
    dd_ref[0] = dot(act, grad, 0, 0).astype(BF)
    du_ref[0] = dot(xt[...], up_grad).astype(BF)
    y = dot(act, wd_ref[0])
    dx = dot(up_grad, wu_ref[0], 1, 1)

    @pl.when(step == 0)
    def _():
        y_ref[...] = y
        dx_ref[...] = dx

    @pl.when(step > 0)
    def _():
        y_ref[...] += y
        dx_ref[...] += dx

    @pl.when(step == last)
    def _():
        block = 128
        totals = [jnp.zeros((1, WIDTH), F32) for _ in range(4)]
        for first in range(0, x_ref.shape[0], block):
            here = slice(first, first + block)
            values, dx, y = mid_ref[here], dx_ref[here], y_ref[here]
            out_grad = cot_ref[here].astype(F32)
            layer_ref[here] = (values + row_ref[5:6] * y).astype(BF)
            normed, inverse = norm_parts(values)
            mid_grad = out_grad + norm_back(normed, inverse, row_ref[4:5], dx)
            mid_grad_ref[here] = mid_grad
            attn_ref[here] = (row_ref[2:3] * mid_grad).astype(BF)
            for index, term in enumerate(
                (sum_ref[here] * mid_grad, dx, dx * normed, out_grad * y)
            ):
                totals[index] += jnp.sum(term, axis=0, keepdims=True)
        for index in range(4):
            sums_ref[index : index + 1] = totals[index]
        sums_ref[4:8] = jnp.zeros((4, WIDTH), F32)
        heads_grad_ref[...] = dot(attn_ref[...], out_w_ref[...], 1, 1).astype(BF)
        out_grad_ref[...] = dot(heads_ref[...], attn_ref[...], 0, 0).astype(BF)


def mlp(x, cot, mod_rows, hidden_mid, attn_sum, heads_out, out_full, up_full, down_full):
    rows = x.shape[0]
    ranks, _, units = up_full.shape
    one = lambda shape: pl.BlockSpec(shape, lambda r: (0, 0), pipeline_mode=pl.Buffered(1))
    whole, square, row = one((rows, WIDTH)), one((WIDTH, WIDTH)), one((8, WIDTH))
    up_spec = pl.BlockSpec((1, WIDTH, units), lambda r: (r, 0, 0))
    down_spec = pl.BlockSpec((1, units, WIDTH), lambda r: (r, 0, 0))
    frames = (rows, WIDTH)
    return pl.pallas_call(
        mlp_kernel,
        grid=(ranks,),
        in_specs=[whole, whole, row, whole, whole, whole, square, up_spec, down_spec],
        out_specs=[whole, whole, whole, square, row, up_spec, down_spec],
        out_shape=[
            jax.ShapeDtypeStruct(frames, BF),
            jax.ShapeDtypeStruct(frames, F32),
            jax.ShapeDtypeStruct(frames, BF),
            jax.ShapeDtypeStruct((WIDTH, WIDTH), BF),
            jax.ShapeDtypeStruct((8, WIDTH), F32),
            jax.ShapeDtypeStruct(up_full.shape, BF),
            jax.ShapeDtypeStruct(down_full.shape, BF),
        ],
        scratch_shapes=[
            pltpu.VMEM((WIDTH, rows), BF),
            pltpu.VMEM(frames, BF),
            pltpu.VMEM(frames, F32),
            pltpu.VMEM(frames, F32),
            pltpu.VMEM(frames, BF),
        ],
        compiler_params=pltpu.CompilerParams(vmem_limit_bytes=VMEM_LIMIT),
        name="mlp",
    )(x, cot, mod_rows, hidden_mid, attn_sum, heads_out, out_full, up_full, down_full)


def backward_kernel(
    q, k0, v0, k1, v1, do, o, lse, cos, sin, mine_ref, row_ref, extra_ref, mod_in_ref,
    x_ref, w_ref, value_ref, mid_ref, feat_ref, mel_w_ref, text_w_ref, proj_ref, layer_ref, down_grads, up_grads, out_grads,
    sums_ref, act_ref, mel_out, layer_out, qkv_out, misc_out, down_out, up_out, out_out,
    dq_v, dk_v, dv_v, dki_v, dvi_v, sent, xt, tiles, total_ref, hidden_ref, text_ref, blocks_v,
    feat_v, mel_wv, text_wv, qkv_grads, misc_grads, mel_v,
    mod_ref, line, every, part_ref, acts, down_buffer, up_buffer, out_buffer,
    kv_sends, kv_recvs, load_sems, tile_sems, block_sems, line_sends, line_recvs, every_sends,
    every_recvs, act_sends, act_recvs, end_sends, end_recvs, *scratch
):
    step = pl.program_id(0)
    last = pl.num_programs(0) - 1
    place = Place()
    dp, tp = place.dp, place.tp
    partner = (flip(dp, 1), flip(tp, 1))
    moves = place.core != tp % 2
    stays = jnp.logical_not(moves)
    rows = dq_v.shape[0]
    ranks, width = w_ref.shape[0], w_ref.shape[3]
    pair_width = 2 * HEAD_DIM
    steps = WIDTH // pair_width
    size = 9
    early = [
        Reduce(place, grads.at[:, h], out.at[h], scratch[size * j : size * (j + 1)], buffer)
        for j, (grads, out, h, buffer) in enumerate(
            (
                (down_grads, down_out, 0, down_buffer),
                (up_grads, up_out, 0, up_buffer),
                (down_grads, down_out, 1, down_buffer),
                (up_grads, up_out, 1, up_buffer),
                (out_grads, out_out, 0, out_buffer),
            )
        )
    ]
    late = [
        Reduce(place, qkv_grads.at[part], qkv_out.at[part], scratch[size * (5 + part) : size * (6 + part)])
        for part in range(3)
    ] + [
        Reduce(
            place, misc_grads.at[h], misc_out.at[h], scratch[size * (8 + h) : size * (9 + h)],
            absolute=True,
        )
        for h in range(2)
    ]
    loads = [
        pltpu.make_async_copy(source, target, load_sems.at[index])
        for index, (source, target) in enumerate(
            (
                (x_ref, hidden_ref),
                (feat_ref, feat_v),
                (mel_w_ref, mel_wv),
                (text_w_ref, text_wv),
            )
        )
    ]
    def tile_load(part, rank):
        number = part * ranks + rank
        return pltpu.make_async_copy(
            w_ref.at[rank, part], tiles.at[number % 2], tile_sems.at[number]
        )

    span = tiles.shape[2]
    proj_loads = [
        pltpu.make_async_copy(
            proj_ref.at[:, pl.ds(index * span, span)], tiles.at[index % 2], tile_sems.at[3 * ranks + index]
        )
        for index in range(proj_ref.shape[1] // span)
    ]
    block = blocks_v.shape[2]
    block_loads = [
        [
            pltpu.make_async_copy(
                source.at[pl.ds(index * block, block)], blocks_v.at[index % 2, kind], block_sems.at[index, kind]
            )
            for kind, source in enumerate((value_ref, mid_ref))
        ]
        for index in range(rows // block)
    ]

    def outward(index, source, target):
        away = remote(source, target, (end_sends, end_recvs), index, partner)
        here = pltpu.make_async_copy(source, target, end_sends.at[2 + index])
        return away, here

    layer_load = pltpu.make_async_copy(layer_ref, dq_v, load_sems.at[4])
    ends = [outward(0, dq_v, layer_out), outward(1, mel_v, mel_out)]
    kv_copies = lambda index: sibling_copies(
        sent, (dki_v, dvi_v), (kv_sends, kv_recvs), index, pair_width, sent.shape[1]
    )

    def send_outward(index):
        @pl.when(moves)
        def _():
            ends[index][0].start()

        @pl.when(stays)
        def _():
            ends[index][1].start()

    @pl.when(step == 0)
    def _():
        for copy in loads:
            copy.start()
        for copy in [tile_load(0, 0), tile_load(0, 1)] + block_loads[0] + block_loads[1]:
            copy.start()
        greet(
            [(flip3(dp, k), tp) for k in range(1, 8)]
            + [place.ahead(step) for step in (1, 2, 3)]
            + [partner]
        )

    flow = Flow()
    for index in range(steps):
        if index in JOINS:
            flow.add(early[JOINS.index(index)])
        stages = flow.take()

        @pl.when(step == index)
        def _(stages=stages):
            for stage in stages:
                stage()

    columns = pl.ds(pl.multiple_of(step * pair_width, pair_width), pair_width)
    slots = sent.shape[1]
    length = mine_ref[0:1, 1:2].astype(jnp.int32)
    biases = [
        key_bias(length, place.core * rows, rows),
        key_bias(length, (1 - place.core) * rows, rows),
    ]
    dq, results = attend_back_pair(biases, q, k0, v0, k1, v1, do, o, lse)
    dq_v[:, columns] = turn(dq, cos[...], -sin[...]).astype(BF)
    dk_v[:, columns] = results[0][0].astype(dk_v.dtype)
    dv_v[:, columns] = results[0][1].astype(dv_v.dtype)

    @pl.when(step >= slots)
    def _():
        for copy in kv_copies(step - slots):
            copy.wait_send()

    sent[0, step % slots] = results[1][0].astype(BF)
    sent[1, step % slots] = results[1][1].astype(BF)
    for copy in kv_copies(step):
        copy.start()

    @pl.when(step == last)
    def _():
        for copy in loads:
            copy.wait()
        flow.beat()
        xt[...] = hidden_ref[...].T
        total_ref[...] = jnp.zeros_like(total_ref)
        cosine = jnp.concatenate([cos[...]] * (width // pair_width), axis=1)
        sine = -jnp.concatenate([sin[...]] * (width // pair_width), axis=1)
        extras = extra_ref[...].astype(F32)
        ids = (extras[1:2] * 256.0 + extras[2:3]).astype(jnp.int32)
        keep_cond = (1.0 - extras[0:1]) * mine_ref[0:1, 2:3]
        for part in range(3):
            if part == 1:

                @pl.loop(0, steps)
                def _(index):
                    for copy in kv_copies(index):
                        copy.wait_recv()

                @pl.loop(steps - slots, steps)
                def _(index):
                    for copy in kv_copies(index):
                        copy.wait_send()

            def one_rank(rank, part=part):
                side = pl.ds(pl.multiple_of(rank * width, width), width)
                if part == 0:
                    grad = dq_v[:, side]
                elif part == 1:
                    grad = turn(
                        dk_v[:, side].astype(F32) + dki_v[:, side].astype(F32), cosine, sine
                    ).astype(BF)
                else:
                    grad = (dv_v[:, side].astype(F32) + dvi_v[:, side].astype(F32)).astype(BF)
                number = part * ranks + rank
                tile_load(part, rank).wait()
                qkv_grads[part, rank] = (
                    dot(xt[...], grad).astype(BF).reshape(qkv_grads.shape[2:])
                )
                total_ref[...] += dot(grad, tiles[number % 2], 1, 1)

                @pl.when(number + 2 < 3 * ranks)
                def _():
                    tile_load((number + 2) // ranks, (number + 2) % ranks).start()

            pl.loop(0, ranks // 2)(one_rank)
            flow.beat()
            pl.loop(ranks // 2, ranks)(one_rank)
            if part == 0:
                layer_load.start()
            if part == 2:
                layer_load.wait()
                send_outward(0)
            flow.add(late[part])
            flow.beat()

        chunks = mod_ref.shape[1]
        lanes = mod_ref.shape[2]
        totals = [jnp.zeros((1, WIDTH), F32) for _ in range(2)]
        for index in range(rows // block):
            here = slice(index * block, (index + 1) * block)
            for copy in block_loads[index]:
                copy.wait()
            grad = total_ref[here]
            normed, inverse = norm_parts(blocks_v[index % 2, 0])
            hidden_ref[here] = (
                blocks_v[index % 2, 1] + norm_back(normed, inverse, row_ref[1:2], grad)
            ).astype(BF)
            totals[0] += jnp.sum(grad, axis=0, keepdims=True)
            totals[1] += jnp.sum(grad * normed, axis=0, keepdims=True)
            if index + 2 < rows // block:
                for copy in block_loads[index + 2]:
                    copy.start()
        for index in range(4):
            totals.append(mod_in_ref[index : index + 1])
        for index in range(6):
            for chunk in range(WIDTH // lanes):
                row = index * (WIDTH // lanes) + chunk
                mod_ref[row // chunks, row % chunks : row % chunks + 1, :] = totals[index][
                    :, chunk * lanes : (chunk + 1) * lanes
                ]
        line_copies = [
            remote(
                mod_ref.at[(tp + step) % 4], line.at[tp], (line_sends, line_recvs), step - 1, place.ahead(step)
            )
            for step in (1, 2, 3)
        ]
        every_copies = [
            remote(line, every.at[dp], (every_sends, every_recvs), k - 1, (flip3(dp, k), tp))
            for k in range(1, 8)
        ]
        act_copies = [
            remote(part_ref, acts.at[tp], (act_sends, act_recvs), step - 1, place.ahead(step))
            for step in (1, 2, 3)
        ]
        for copy in line_copies:
            copy.start()
        line[tp] = mod_ref[tp]
        flow.beat()

        text_ref[...] = dot(hidden_ref[...], text_wv[...], 1, 1).astype(BF) * mine_ref[0:1, 3:4].astype(BF)
        table_rows = VOCABULARY // ranks
        split = misc_grads.shape[-2] * 16
        shape = misc_grads.shape[2:]

        @pl.loop(0, ranks)
        def _(rank):
            row = lax.broadcasted_iota(jnp.int32, (split, rows), 0) + rank * table_rows
            one_hot = (row == ids).astype(F32).astype(BF)
            misc_grads[0, rank] = dot(one_hot, text_ref[...]).astype(BF).reshape(shape)

        flow.add(late[3])
        flow.beat()
        for copy in line_copies:
            copy.wait()
        every[dp] = line[...]
        for copy in every_copies:
            copy.start()
        feat_rows = feat_v.shape[1] // ranks
        rest = table_rows - split

        def rest_of(rank, share):
            row = lax.broadcasted_iota(jnp.int32, (rest, rows), 0) + (rank * table_rows + split)
            one_hot = (row == ids).astype(F32).astype(BF)
            table = dot(one_hot, text_ref[...]).astype(BF)
            misc_grads[1, rank] = jnp.concatenate(
                [table, share[:, :TEXT_DIM], share[:, TEXT_DIM:]], axis=0
            ).reshape(shape)

        for rank in range(ranks):
            side = slice(rank * feat_rows, (rank + 1) * feat_rows)
            rest_of(rank, dot(feat_v[:, side], hidden_ref[...], 0, 0).astype(BF))
        flow.add(late[4])
        flow.beat()
        for copy in proj_loads[:2]:
            copy.start()
        mel_part = dot(mel_wv[...], hidden_ref[...], 1, 1)
        bins = mel_part.shape[0] // 2
        mel_v[...] = mine_ref[0:1, 0:1] * mel_part[:bins] + keep_cond * mel_part[bins:]
        send_outward(1)
        flow.beat()
        for copy in every_copies:
            copy.wait()
        for pair in range(4):
            sums_ref[pair] = every[2 * pair] + every[2 * pair + 1]
        total = None
        for index, copy in enumerate(proj_loads):
            copy.wait()
            for lane in range(0, span, lanes):
                chunk = (index * span + lane) // lanes
                held = sums_ref[:, :, chunk, :].reshape(16, lanes).astype(BF)
                term = dot(held, tiles[index % 2, :, lane : lane + lanes], 1, 1)
                total = term if total is None else total + term
            if index + 2 < len(proj_loads):
                proj_loads[index + 2].start()
        part_ref[...] = total
        acts[tp] = total
        for copy in act_copies:
            copy.start()
        while flow.beat():
            pass
        for copy in act_copies:
            copy.wait()
        act_ref[...] = acts[...]

        @pl.when(moves)
        def _():
            for away, _ in ends:
                away.wait()

        @pl.when(stays)
        def _():
            for _, here in ends:
                here.wait()


def backward(
    query, own, other, heads_grad, heads_out, lse, cosine, sine, mine, mod_rows, extra, mod_part,
    x, weights, values, mid_grad, feats, mel_w, text_w, mod_proj, layer, down_grad, up_grad, out_grad,
):
    rows = x.shape[0]
    ranks, width = weights.shape[0], weights.shape[3]
    table_rows = VOCABULARY // ranks
    misc_rows = table_rows + 2 * (feats.shape[1] // ranks)
    chunks = mod_proj.shape[1] // 128
    pairs = WIDTH // (2 * HEAD_DIM)
    qkv_block = blocks((WIDTH, width))
    misc_block = blocks((misc_rows // 2, TEXT_DIM))
    dma = pltpu.SemaphoreType.DMA
    vmem = lambda shape, t=BF: pltpu.VMEM(shape, t)
    tile = pl.BlockSpec((rows, 2 * HEAD_DIM), lambda i: (0, i))
    one = lambda v: pl.BlockSpec(v.shape, lambda i: (0,) * v.ndim, pipeline_mode=pl.Buffered(1))
    parts = lambda v, count: v.reshape(
        (ranks, count) + blocks((v.shape[1] // count, v.shape[2]))
    )
    early = (parts(down_grad, 2), parts(up_grad, 2), parts(out_grad, 1))
    scratch = []
    for index in (0, 1, 0, 1, 2):
        block = early[index].shape
        scratch += Reduce.scratch(block[-2] * 16, block[-1])
    for _ in range(3):
        scratch += Reduce.scratch(WIDTH, width)
    for _ in range(2):
        scratch += Reduce.scratch(misc_rows // 2, TEXT_DIM)
    frames = (rows, WIDTH)
    mel_shape = (mel_w.shape[0] // 2, rows)
    sums_shape = jax.ShapeDtypeStruct((4, 4, chunks, 128), F32)
    act_shape = jax.ShapeDtypeStruct((4, 16, WIDTH), F32)
    outs = pl.pallas_call(
        backward_kernel,
        grid=(pairs,),
        in_specs=[tile] * 7
        + [pl.BlockSpec((2, 1, rows), lambda i: (i, 0, 0))]
        + [one(v) for v in (cosine, sine, mine, mod_rows, extra, mod_part)]
        + [ANY] * 12,
        out_specs=[one(sums_shape), one(act_shape)] + [ANY] * 7,
        out_shape=[
            sums_shape,
            act_shape,
            jax.ShapeDtypeStruct(mel_shape, F32),
            jax.ShapeDtypeStruct(frames, BF),
            jax.ShapeDtypeStruct((3,) + qkv_block, BF),
            jax.ShapeDtypeStruct((2,) + misc_block, BF),
        ]
        + [jax.ShapeDtypeStruct(v.shape[1:], BF) for v in early],
        scratch_shapes=[
            vmem(frames), vmem(frames), vmem(frames), vmem(frames), vmem(frames),
            vmem((2, 4, rows, 2 * HEAD_DIM)), vmem((WIDTH, rows)), vmem((2, WIDTH, width)),
            vmem(frames, F32), vmem(frames), vmem((rows, TEXT_DIM)), vmem((2, 2, 64, WIDTH), F32),
            vmem(feats.shape), vmem(mel_w.shape), vmem(text_w.shape),
            vmem((3, ranks) + qkv_block), vmem((2, ranks) + misc_block), vmem(mel_shape, F32),
            vmem((4, chunks, 128), F32), vmem((4, chunks, 128), F32), vmem((8, 4, chunks, 128), F32),
            vmem((16, WIDTH), F32), vmem((4, 16, WIDTH), F32),
        ]
        + [vmem((ranks,) + v.shape[3:]) for v in early]
        + [
            dma((2, pairs)), dma((2, pairs)), dma((5,)), dma((3 * ranks + mod_proj.shape[1] // width,)),
            dma((rows // 64, 2)),
            dma((3,)), dma((3,)), dma((7,)), dma((7,)), dma((3,)), dma((3,)), dma((4,)), dma((2,)),
        ]
        + scratch,
        compiler_params=comm_params(4),
        name="backward",
    )(
        query, *own, *other, heads_grad, heads_out, lse, cosine, sine, mine, mod_rows, extra, mod_part,
        x, weights, values, mid_grad, feats, mel_w, text_w, mod_proj, layer, *early,
    )
    outs = list(outs)
    outs[4] = outs[4].reshape(3, WIDTH, width)
    outs[5] = outs[5].reshape(misc_rows, TEXT_DIM)
    outs[6:] = [o.reshape(v.shape[1:]) for o, v in zip(outs[6:], (down_grad, up_grad, out_grad))]
    return outs


def time_features(flow_times, width):
    half_dim = width // 2
    frequency = jnp.exp(
        jnp.arange(half_dim, dtype=F32) * (-math.log(10000.0) / (half_dim - 1))
    )
    angles = 1000.0 * flow_times[:, None] * frequency[None, :]
    return jnp.concatenate([jnp.sin(angles), jnp.cos(angles)], axis=1)


def rope_tables(positions, width):
    lane = jnp.arange(width, dtype=jnp.int32)
    pair = ((lane % HEAD_DIM) // 2).astype(F32)
    inverse = jnp.exp(pair * (-2.0 * math.log(10000.0) / HEAD_DIM))
    angles = positions.astype(F32)[:, None] * inverse[None, :]
    sign = jnp.where(lane % 2 == 0, -1.0, 1.0)
    return jnp.cos(angles), jnp.sin(angles) * sign[None, :]


def norm_parts(values):
    average = jnp.mean(values, axis=-1, keepdims=True)
    centered = values - average
    spread = jnp.mean(centered * centered, axis=-1, keepdims=True)
    inverse = lax.rsqrt(spread + 1e-06)
    return centered * inverse, inverse


def norm_back(normed, inverse, scale_part, grad):
    inner = grad * (1.0 + scale_part)
    first = jnp.mean(inner, axis=-1, keepdims=True)
    second = jnp.mean(inner * normed, axis=-1, keepdims=True)
    return inverse * (inner - first - normed * second)


def body(
    mel_frames, noise_frames, text_ids, span_mask, lengths, audio_drop, text_drop, flow_times,
    in_proj, text_table, time_proj, mod_proj, qkv_proj, out_proj, up_proj, down_proj, cotangent,
):
    dp_size = lax.axis_size("dp")
    tp_size = lax.axis_size("tp")
    dp_rank = lax.axis_index("dp")
    tp_rank = lax.axis_index("tp")
    local_rows = mel_frames.shape[0]
    per_group = flow_times.shape[0]
    utt_total = per_group * dp_size
    dp_low = dp_rank % 2
    tp_low = tp_rank % 2
    stay = dp_low == tp_low
    direct = dp_size == 8 and tp_size == 4
    pairs = []
    for d in range(dp_size):
        for t in range(tp_size):
            if d % 2 != t % 2:
                pairs.append((d * tp_size + t, (d ^ 1) * tp_size + (t ^ 1)))

    def swap(values):
        return jnp.where(stay, values, lax.ppermute(values, AXES, pairs))

    source_dp = dp_rank - dp_low + tp_low
    utterance = source_dp * per_group + tp_rank // 2
    half = dp_low

    def relative(values):
        return jnp.roll(values, -tp_rank, axis=0)

    def gather(shard):
        return relative(lax.all_gather(shard, "tp", axis=0))

    lane = jnp.arange(TIME_DIM + 128, dtype=jnp.int32)[None, :]
    half_dim = TIME_DIM // 2
    frequency = jnp.exp((lane % half_dim).astype(F32) * (-math.log(10000.0) / (half_dim - 1)))
    column = lambda v: v[:, None]
    angles = 1000.0 * column(flow_times) * frequency
    facts = jnp.where(lane < half_dim, jnp.sin(angles), jnp.cos(angles))
    for index, fact in enumerate((flow_times, lengths, 1 - audio_drop, 1 - text_drop)):
        facts = jnp.where(lane == TIME_DIM + index, column(fact).astype(F32), facts)
    sinus_own = facts[:, :TIME_DIM]
    act_own = jax.nn.silu(dot(sinus_own.astype(BF), time_proj)).astype(BF)
    mod_cols = dot(act_own, mod_proj)
    spare = -MEL_BINS % 16
    bins = MEL_BINS + spare
    line = jnp.arange(16, dtype=jnp.int32)[:, None]
    extra = jnp.where(
        line == 0,
        span_mask[None, :],
        jnp.where(line == 1, text_ids[None, :] // 256, jnp.where(line == 2, text_ids[None, :] % 256, 0)),
    ).astype(BF)
    padded = lambda v: jnp.pad(v, ((0, spare), (0, 0)))
    mel, noise = padded(mel_frames.T), padded(noise_frames.T)
    mel_w = jnp.concatenate(
        [padded(in_proj[:MEL_BINS]), padded(in_proj[MEL_BINS : 2 * MEL_BINS])], axis=0
    )
    text_w = in_proj[2 * MEL_BINS :]
    qkv_shard = qkv_proj.transpose(1, 0, 2)
    positions = half * local_rows + jnp.arange(local_rows, dtype=jnp.int32)
    cosine, sine = rope_tables(positions, 2 * HEAD_DIM)
    wide = lambda table: jnp.tile(table, (1, WIDTH // tp_size // (2 * HEAD_DIM)))
    if direct:
        pad = ((0, 8 - per_group), (0, 0))
        (
            facts_all, mod_rows, mine, extra, qkv_full, feats, text_emb, hidden, normed_attn,
            query, key, value, key_in, value_in, heads_out, lse,
            layer, mid_grad, heads_grad, out_grad_w, mlp_sums, up_grad, down_grad,
        ) = forward(
            mel, noise, extra, jnp.pad(facts, pad), jnp.pad(mod_cols, pad), cotangent, qkv_shard, out_proj, up_proj,
            down_proj, text_table, mel_w, text_w, cosine, sine,
        )
        facts_all = facts_all[:, :per_group].reshape(utt_total, -1)
    else:
        facts_all = lax.all_gather(facts, "dp", axis=0, tiled=True)
        near = lax.all_gather(lax.all_gather(mod_cols, "tp", axis=1, tiled=True), "dp", axis=0, tiled=True)
        mod_row = lax.dynamic_slice_in_dim(near, utterance, 1, 0)
        mel, noise, extra, cot = swap(mel), swap(noise), swap(extra), swap(cotangent)
        mine = lax.dynamic_slice_in_dim(facts_all, utterance, 1, 0)[:, TIME_DIM:]
    if not direct:
        shift_attn, scale_attn, gate_attn, shift_mlp, scale_mlp, gate_mlp = jnp.split(mod_row, 6, axis=1)
        time_here, length, keep_audio, keep_text = (mine[0, i] for i in range(4))
        length = length.astype(jnp.int32)
        extra = extra[:3].astype(jnp.int32)
        ids = extra[1] * 256 + extra[2]
        keep_cond = (1.0 - extra[0].astype(F32))[None, :] * keep_audio
        info = jnp.stack([length, half * local_rows, (1 - half) * local_rows])
        mel, noise = mel.astype(F32), noise.astype(F32)
        noisy = (1.0 - time_here) * noise + time_here * mel
        feats = jnp.concatenate([noisy, mel * keep_cond], axis=0).astype(BF)
        text_emb = (jnp.take(text_table, ids, axis=0).astype(F32) * keep_text).astype(BF)
    features = jnp.concatenate([feats[:MEL_BINS].T, feats[bins : bins + MEL_BINS].T, text_emb], axis=1)
    if not direct:
        qkv_full = gather(qkv_shard)
        hidden = dot(features, in_proj)
        norm_a, inv_a = norm_parts(hidden)
        normed_attn = (norm_a * (1.0 + scale_attn) + shift_attn).astype(BF)
        query, key, value, key_in, value_in = project_qkv(normed_attn, qkv_full, wide(cosine), wide(sine))
        heads_out, lse = attend(info, query, (key, value), (key_in, value_in))
        out_full, up_full, down_full = (gather(shard) for shard in (out_proj, up_proj, down_proj))
    own, other = (key, value), (key_in, value_in)
    if not direct:
        out_full = out_full.reshape(WIDTH, WIDTH)
        attn_sum = dot(heads_out, out_full)
        hidden_mid = hidden + gate_attn * attn_sum
        normed, _ = norm_parts(hidden_mid)
        normed_mlp = (normed * (1.0 + scale_mlp) + shift_mlp).astype(BF)
        mod_rows = jnp.pad(mod_row.reshape(6, WIDTH), ((0, 2), (0, 0)))
        layer, mid_grad, heads_grad, out_grad_w, mlp_sums, up_grad, down_grad = mlp(
            normed_mlp, cot, mod_rows, hidden_mid, attn_sum, heads_out, out_full, up_full, down_full
        )
        out_grad_w = out_grad_w.reshape(tp_size, -1, WIDTH)
    sinus = facts_all[:, :TIME_DIM].astype(BF)
    time_embed = dot(sinus, time_proj)
    time_act = jax.nn.silu(time_embed).astype(BF)
    in_rows = in_proj.shape[0] // tp_size
    in_pad = -in_rows % 64
    table_rows = VOCABULARY // tp_size
    spaced = lambda v, axis: jnp.concatenate(
        [
            jnp.pad(
                lax.slice_in_dim(v, i * in_rows, (i + 1) * in_rows, axis=axis),
                [(0, in_pad if d == axis else 0) for d in range(2)],
            )
            for i in range(tp_size)
        ],
        axis=axis,
    )
    if direct:
        sums, act_parts, mel_grad, layer_out, qkv_out, misc_out, *early_out = backward(
            query, own, other, heads_grad, heads_out, lse, cosine, sine, mine, mod_rows, extra, mlp_sums,
            normed_attn, qkv_full, hidden, mid_grad, spaced(features, 1), mel_w, text_w, mod_proj,
            layer, down_grad, up_grad, out_grad_w,
        )
        mel_grad = mel_grad[:MEL_BINS].T
        order = lambda v: v.reshape((4, 2, 2) + v.shape[2:]).swapaxes(1, 2)
        mod_sums = order(sums).reshape(utt_total, -1).astype(BF)
        act_grad = jnp.sum(act_parts, axis=0)
        act_grad = order(act_grad.reshape(4, 4, WIDTH)).reshape(utt_total, WIDTH)
    else:
        layer_out = swap(layer)
        mod_rest = mlp_sums[:4].reshape(1, 4 * WIDTH)
        column_sum = lambda values: jnp.sum(values, axis=0, keepdims=True)
        dq, dk, dv, dk_in, dv_in = attend_back(
            info, query, own, other, heads_grad, heads_out, lse, cosine, sine
        )
        qkv_grad, normed_attn_grad = project_qkv_back(
            normed_attn, qkv_full, wide(cosine), wide(sine), dq, dk, dv, dk_in, dv_in
        )
        hidden_grad = (mid_grad + norm_back(norm_a, inv_a, scale_attn, normed_attn_grad)).astype(BF)
        in_grad = dot(features, hidden_grad, 0, 0).astype(BF)
        mel_part = dot(in_proj[: 2 * MEL_BINS], hidden_grad, 1, 1)
        mel_grad = swap(
            (time_here * mel_part[:MEL_BINS] + keep_cond * mel_part[MEL_BINS:]).T
        )
        text_grad = dot(hidden_grad, in_proj[2 * MEL_BINS :], 1, 1).astype(BF) * keep_text.astype(BF)
        one_hot = (ids[None, :] == jnp.arange(VOCABULARY, dtype=jnp.int32)[:, None]).astype(BF)
        table_grad = dot(one_hot, text_grad).astype(BF).reshape(tp_size, table_rows, TEXT_DIM)
        in_grad = spaced(in_grad, 0).reshape(tp_size, in_rows + in_pad, WIDTH)
        misc = jnp.concatenate(
            [table_grad, in_grad[:, :, :TEXT_DIM], in_grad[:, :, TEXT_DIM:]], axis=1
        )
        mod_part = jnp.concatenate(
            [column_sum(normed_attn_grad), column_sum(normed_attn_grad * norm_a), mod_rest], axis=1
        )
        slot = (jnp.arange(utt_total, dtype=jnp.int32) == utterance).astype(F32)[:, None]
        mod_sums = lax.psum(
            lax.psum_scatter(slot * mod_part, "tp", scatter_dimension=1, tiled=True), "dp"
        ).astype(BF)
        act_grad = lax.psum(dot(mod_sums, mod_proj, 1, 1), "tp")

        def reduce(values):
            return lax.psum(
                lax.psum_scatter(values, "tp", scatter_dimension=0, tiled=True)[0], "dp"
            )

        absolute = lambda values: jnp.roll(values, tp_rank, axis=0)
        early_out = [reduce(absolute(values)) for values in (down_grad, up_grad, out_grad_w)]
        qkv_out = reduce(absolute(qkv_grad))
        misc_out = reduce(misc)
    mod_grad = dot(time_act, mod_sums, 0, 0)
    embed_grad = jax.vjp(jax.nn.silu, time_embed)[1](act_grad)[0].astype(BF)
    time_rows = TIME_DIM // tp_size
    sinus_share = lax.dynamic_slice_in_dim(sinus, tp_rank * time_rows, time_rows, 1)
    time_grad = dot(sinus_share, embed_grad, 0, 0)
    down_out, up_out, out_out = (values.astype(F32) for values in early_out)
    misc_out = misc_out.astype(F32)
    right = table_rows + in_rows + in_pad
    in_out = jnp.concatenate(
        [misc_out[table_rows : table_rows + in_rows], misc_out[right : right + in_rows]], axis=1
    )
    return (
        layer_out, mel_grad, in_out, misc_out[:table_rows], time_grad, mod_grad,
        qkv_out.astype(F32).transpose(1, 0, 2), out_out, up_out, down_out,
    )


def solution(mesh):
    frames = P(("dp", "tp"), None)
    frame = P(("dp", "tp"))
    return jax.shard_map(
        body,
        mesh=mesh,
        in_specs=(
            frames, frames, frame, frame, P("dp"), P("dp"), P("dp"), P("dp"),
            P(), P(), P(), P(None, "tp"), P(None, None, "tp"), P("tp", None), P(None, "tp"),
            P("tp", None), frames,
        ),
        out_specs=(
            frames, frames, P("tp", None), P("tp", None), P("tp", None), P(None, "tp"),
            P(None, None, "tp"), P("tp", None), P(None, "tp"), P("tp", None),
        ),
        check_vma=False,
    )
```

```python
import functools
import math

import jax
import jax.numpy as jnp
from jax import lax
from jax.experimental import pallas as pl
from jax.experimental.pallas import tpu as pltpu
from jax.sharding import PartitionSpec as P

WIDTH = 1024
HEAD_DIM = 64
MEL_BINS = 100
TEXT_DIM = 512
TIME_DIM = 256
VOCABULARY = 2560
FFN_DIM = 2048
AXES = ("dp", "tp")
BF = jnp.bfloat16
F32 = jnp.float32
MESH = pl.DeviceIdType.MESH
VMEM_LIMIT = 60 * 1024 * 1024
ANY = pl.BlockSpec(memory_space=pl.ANY)


def dot(left, right, left_dim=1, right_dim=0):
    return lax.dot_general(
        left, right, (((left_dim,), (right_dim,)), ((), ())), preferred_element_type=F32
    )


def flip(index, bit):
    return index + bit - 2 * bit * ((index // bit) % 2)


class Place:
    def __init__(self):
        self.dp = lax.axis_index("dp")
        self.tp = lax.axis_index("tp")
        self.core = self.dp % 2
        self.x = (self.dp // 2) % 2
        self.y = self.dp // 4

    def plane(self, bit):
        return (flip(self.dp, bit), self.tp)

    def ahead(self, step):
        return (self.dp, (self.tp + step) % 4)


def greet(devices):
    barrier = pltpu.get_barrier_semaphore()
    for device in devices:
        pl.semaphore_signal(barrier, inc=1, device_id=device, device_id_type=MESH)
    pl.semaphore_wait(barrier, len(devices))


def remote(source, target, sems, index, device):
    return pltpu.make_async_remote_copy(
        src_ref=source,
        dst_ref=target,
        send_sem=sems[0].at[index],
        recv_sem=sems[1].at[index],
        device_id=device,
        device_id_type=MESH,
    )


GATHER_COPIES = 13


class Gather:
    def __init__(self, place, shard, full, scratch, slots=(1, 2, 3), part=slice(None)):
        self.p, self.shard, self.full = place, shard, full
        self.sems, self.held = scratch[:2], (scratch[2:] or [None])[0]
        self.slots, self.part = slots, part

    @staticmethod
    def scratch(shape=None):
        dma = pltpu.SemaphoreType.DMA
        held = [] if shape is None else [pltpu.VMEM(shape, BF)]
        return [dma((GATHER_COPIES,)), dma((GATHER_COPIES,))] + held

    def view(self, *index):
        return self.full.at[(slice(self.slots[0], self.slots[-1] + 1), self.part) + index]

    def copy(self, kind):
        p = self.p
        dp = p.dp
        beside, above = flip(dp, 2), flip(dp, 4)
        across = flip(above, 2)
        if kind[0] == "z":
            step = int(kind[1])
            return remote(
                self.shard.at[self.part, dp],
                self.full.at[step, self.part, dp],
                self.sems,
                step - 1,
                p.ahead(4 - step),
            )
        index, bit, sem = {
            "x": ((dp,), 2, 3),
            "y": ((dp,), 4, 4),
            "c": ((dp,), 1, 5),
            "ya": ((beside, 0), 4, 6),
            "xb": ((above, 1), 2, 7),
            "cx": ((beside,), 1, 8),
            "cy": ((above,), 1, 9),
            "cd": ((across,), 1, 10),
        }[kind]
        return remote(self.view(*index), self.view(*index), self.sems, sem, p.plane(bit))

    def fetch(self):
        return pltpu.make_async_copy(self.shard.at[self.part], self.held, self.sems[0].at[11])

    def keep(self):
        return pltpu.make_async_copy(self.held, self.full.at[0, self.part], self.sems[0].at[12])

    def start(self, *kinds):
        for kind in kinds:
            self.copy(kind).start()

    def arrived(self, *kinds):
        for kind in kinds:
            self.copy(kind).wait_recv()

    def lines(self):
        return ["z%d" % slot for slot in self.slots]

    def stage0(self):
        self.start(*self.lines())
        if self.held is not None:
            self.fetch().start()

    def stage1(self):
        if self.held is not None:
            self.fetch().wait()
            self.keep().start()
        self.arrived(*self.lines())
        self.start("x", "y", "c")

    def stage2(self):
        self.arrived("x")
        self.start("ya", "cx")
        self.arrived("y")
        self.start("xb", "cy")

    def stage3(self):
        self.arrived("ya", "xb")
        self.start("cd")

    def stage4(self):
        self.arrived("c", "cx", "cy", "cd")

    def finish(self):
        if self.held is not None:
            self.keep().wait()
        for kind in self.lines() + ["x", "y", "c", "ya", "xb", "cx", "cy", "cd"]:
            self.copy(kind).wait_send()

    stages = property(lambda s: [s.stage0, s.stage1, s.stage2, s.stage3, s.stage4])


REDUCE_COPIES = 18


def add_into(target, source):
    for index in range(4):
        target[index] = (target[index].astype(F32) + source[index].astype(F32)).astype(BF)


class Reduce:
    @staticmethod
    def scratch(rows, columns):
        r = rows // 16
        shapes = [
            (4, 2, 2, 2, r, columns),
            (4, 2, r, columns),
            (4, 2, r, columns),
            (4, r, columns),
            (4, r, columns),
            (3, 2, r, columns),
        ]
        return [
            pltpu.SemaphoreType.DMA((REDUCE_COPIES,)),
            pltpu.SemaphoreType.DMA((REDUCE_COPIES,)),
        ] + [pltpu.VMEM(shape, BF) for shape in shapes]

    def __init__(self, place, grads, out, target, scratch, buffer=None, absolute=False):
        self.p, self.grads, self.out, self.target, self.buffer = place, grads, out, target, buffer
        self.sems = scratch[:2]
        self.rc, self.rx, self.ry, self.ra, self.rb, self.rz = scratch[2:8]
        self.acc = grads.at[:, place.core] if buffer is None else self.rc
        self.first = place.tp if absolute else 0

    def slot(self, step):
        return (self.first + step) % 4

    def copy(self, kind):
        p, acc, out = self.p, self.acc, self.out
        c, x, y = p.core, p.x, p.y
        if kind in ("z1", "z2", "z3"):
            step = int(kind[1])
            return remote(
                acc.at[self.slot(step), x, y], self.rz.at[step - 1], self.sems, 4 + step, p.ahead(step)
            )
        table = {
            "c": (lambda: self.grads.at[:, 1 - c], lambda: self.rc, 1, 0),
            "x": (lambda: acc.at[:, 1 - x, :, 0], lambda: self.rx, 2, 1),
            "y": (lambda: acc.at[:, :, 1 - y, 1], lambda: self.ry, 4, 2),
            "ya": (lambda: acc.at[:, x, 1 - y, 0], lambda: self.ra, 4, 3),
            "xb": (lambda: acc.at[:, 1 - x, y, 1], lambda: self.rb, 2, 4),
            "gx": (lambda: out.at[c, x, y], lambda: out.at[c, x, y], 2, 8),
            "gy": (lambda: out.at[c, x, y], lambda: out.at[c, x, y], 4, 9),
            "gc": (lambda: out.at[c, x, y], lambda: out.at[c, x, y], 1, 10),
            "gya": (lambda: out.at[c, 1 - x, y, 0], lambda: out.at[c, 1 - x, y, 0], 4, 11),
            "gxb": (lambda: out.at[c, x, 1 - y, 1], lambda: out.at[c, x, 1 - y, 1], 2, 12),
            "gcx": (lambda: out.at[c, 1 - x, y], lambda: out.at[c, 1 - x, y], 1, 13),
            "gcy": (lambda: out.at[c, x, 1 - y], lambda: out.at[c, x, 1 - y], 1, 14),
            "gcd": (lambda: out.at[c, 1 - x, 1 - y], lambda: out.at[c, 1 - x, 1 - y], 1, 15),
        }
        source, target, bit, index = table[kind]
        return remote(source(), target(), self.sems, index, p.plane(bit))

    def load(self):
        return pltpu.make_async_copy(self.grads.at[:, self.p.core], self.buffer, self.sems[0].at[16])

    def save(self):
        return pltpu.make_async_copy(self.out, self.target, self.sems[0].at[17])

    def start(self, *kinds):
        for kind in kinds:
            self.copy(kind).start()

    def arrived(self, *kinds):
        for kind in kinds:
            self.copy(kind).wait_recv()

    def stage0(self):
        self.start("c")
        if self.buffer is not None:
            self.load().start()

    def stage1(self):
        self.arrived("c")
        if self.buffer is None:
            add_into(self.acc, self.rc)
        else:
            self.load().wait()
            add_into(self.rc, self.buffer)
        self.start("x", "y")

    def stage2(self):
        p = self.p
        self.arrived("x")
        add_into(self.acc.at[:, p.x, :, 0], self.rx)
        self.start("ya")
        self.arrived("y")
        add_into(self.acc.at[:, :, p.y, 1], self.ry)
        self.start("xb")

    def stage3(self):
        p = self.p
        self.arrived("ya")
        add_into(self.acc.at[:, p.x, p.y, 0], self.ra)
        self.arrived("xb")
        add_into(self.acc.at[:, p.x, p.y, 1], self.rb)
        self.start("z1", "z2", "z3")

    def stage4(self):
        p = self.p
        self.arrived("z1", "z2", "z3")
        total = self.acc[self.slot(0), p.x, p.y].astype(F32)
        for step in range(3):
            total += self.rz[step].astype(F32)
        self.out[p.core, p.x, p.y] = total.astype(BF)
        self.start("gx", "gy", "gc")

    def stage5(self):
        self.arrived("gx")
        self.start("gya", "gcx")
        self.arrived("gy")
        self.start("gxb", "gcy")

    def stage6(self):
        self.arrived("gya", "gxb")
        self.start("gcd")

    def stage7(self):
        self.arrived("gc", "gcx", "gcy", "gcd")
        self.save().start()
        for kind in (
            "c", "x", "y", "ya", "xb", "z1", "z2", "z3", "gx", "gy", "gc", "gya", "gxb", "gcx", "gcy", "gcd",
        ):
            self.copy(kind).wait_send()

    stages = property(
        lambda s: [s.stage0, s.stage1, s.stage2, s.stage3, s.stage4, s.stage5, s.stage6, s.stage7]
    )


def pipeline(items, first=0):
    stages = [item.stages[first:] for item in items]
    depth = max(len(held) for held in stages)
    beats = []
    for beat in range(len(items) + depth - 1):
        beats.append(
            [held[beat - j] for j, held in enumerate(stages) if 0 <= beat - j < len(held)][::-1]
        )
    return beats


LAGS = (0, 1, 4, 7, 9, 12, 14, 15)
JOINS = (0, 1, 3, 5, 7)


class Flow:
    def __init__(self):
        self.items = []
        self.now = 0

    def add(self, item):
        self.items.append([(self.now + lag, stage) for lag, stage in zip(LAGS, item.stages)])

    def take(self):
        due = [held.pop(0)[1] for held in self.items[::-1] if held and held[0][0] <= self.now]
        self.now += 1
        return due

    def beat(self):
        for stage in self.take():
            stage()
        return any(self.items)


def plane_and_line(place):
    return [place.plane(bit) for bit in (1, 2, 4)] + [place.ahead(step) for step in (1, 2, 3)]


def flip3(index, mask):
    for bit in (1, 2, 4):
        if mask & bit:
            index = flip(index, bit)
    return index


def comm_params(collective_id):
    return pltpu.CompilerParams(
        vmem_limit_bytes=VMEM_LIMIT, collective_id=collective_id, has_side_effects=True
    )


def pieces(shape):
    return tuple(shape[:-2]) + (8, 2, shape[-2] // 16, shape[-1])


def blocks(shape):
    return tuple(shape[:-2]) + (2, 2, 2, 2, shape[-2] // 16, shape[-1])


def head_masks(rows):
    lane = lax.broadcasted_iota(jnp.int32, (rows, 2 * HEAD_DIM), 1)
    return [lane < HEAD_DIM, lane >= HEAD_DIM]


def key_bias(length, start, rows):
    position = lax.broadcasted_iota(jnp.int32, (rows, 1), 0) + start
    return jnp.where(position < length, 0.0, -1e30)


def attend_pair(bias0, bias1, q_ref, k0_ref, v0_ref, k1_ref, v1_ref):
    rows = q_ref.shape[0]
    query = q_ref[...] * jnp.asarray(1.0 / math.sqrt(HEAD_DIM), BF)
    masks = head_masks(rows)
    vt0 = v0_ref[...].T
    vt1 = v1_ref[...].T
    parts, totals = [], []
    for head in range(2):
        masked = jnp.where(masks[head], query, jnp.zeros_like(query))
        s0 = dot(k0_ref[...], masked, 1, 1) + bias0
        s1 = dot(k1_ref[...], masked, 1, 1) + bias1
        peak = jnp.maximum(
            jnp.max(s0, axis=0, keepdims=True), jnp.max(s1, axis=0, keepdims=True)
        )
        e0 = jnp.exp(s0 - peak)
        e1 = jnp.exp(s1 - peak)
        total = jnp.sum(e0, axis=0, keepdims=True) + jnp.sum(e1, axis=0, keepdims=True)
        side = slice(head * HEAD_DIM, (head + 1) * HEAD_DIM)
        acc = dot(vt0[side], e0.astype(BF)) + dot(vt1[side], e1.astype(BF))
        parts.append(acc / total)
        totals.append(peak + jnp.log(total))
    return jnp.concatenate(parts, axis=0).T.astype(BF), totals


def attend_back_pair(biases, q_ref, k0_ref, v0_ref, k1_ref, v1_ref, do_ref, o_ref, lse_ref):
    rows = q_ref.shape[0]
    keys = k0_ref.shape[0]
    width = 2 * HEAD_DIM
    scale = 1.0 / math.sqrt(HEAD_DIM)
    query = q_ref[...] * jnp.asarray(scale, BF)
    grads = do_ref[...]
    product = (grads.astype(F32) * o_ref[...].astype(F32)).T
    sides = ((k0_ref, v0_ref), (k1_ref, v1_ref))
    turned = [k_ref[...].T for k_ref, _ in sides]

    def one_head(head, carry):
        dq, sums = carry[0], list(carry[1:])
        lane = lax.broadcasted_iota(jnp.int32, (rows, width), 1) // HEAD_DIM
        line = lax.broadcasted_iota(jnp.int32, (width, 1), 0) // HEAD_DIM
        masked = jnp.where(lane == head, query, jnp.zeros_like(query))
        gmask = jnp.where(lane == head, grads, jnp.zeros_like(grads))
        delta = jnp.sum(jnp.where(line == head, product, 0.0), axis=0, keepdims=True)
        total = lse_ref[head]
        for which, (k_ref, v_ref) in enumerate(sides):
            scores = dot(k_ref[...], masked, 1, 1) + biases[which]
            probs = jnp.exp(scores - total)
            prob_grad = dot(v_ref[...], gmask, 1, 1)
            score_grad = (probs * (prob_grad - delta)).astype(BF)
            sums[2 * which] += dot(score_grad, masked)
            sums[2 * which + 1] += dot(probs.astype(BF), gmask)
            kt = jnp.where(line == head, turned[which].astype(F32), 0.0).astype(BF)
            dq += dot(kt, score_grad)
        return (dq, *sums)

    start = (jnp.zeros((width, rows), F32),) + (jnp.zeros((keys, width), F32),) * 4
    dq, *sums = lax.fori_loop(0, 2, one_head, start)
    return dq.T * scale, [sums[:2], sums[2:]]


def turn(values, cosine, sine):
    lane = lax.broadcasted_iota(jnp.int32, values.shape, 1)
    width = values.shape[1]
    other = jnp.where(
        lane % 2 == 0, pltpu.roll(values, width - 1, 1), pltpu.roll(values, 1, 1)
    )
    return values * cosine + other * sine


def attend_kernel(info_ref, q, k0, v0, k1, v1, o_ref, lse_ref):
    keys = k0.shape[0]
    biases = [key_bias(info_ref[0], info_ref[1 + which], keys) for which in range(2)]
    o_ref[...], (lse_ref[0], lse_ref[1]) = attend_pair(*biases, q, k0, v0, k1, v1)


def attend(info, query, own, other):
    rows = query.shape[0]
    pairs = WIDTH // (2 * HEAD_DIM)
    tile = pl.BlockSpec((rows, 2 * HEAD_DIM), lambda i: (0, i))
    return pl.pallas_call(
        attend_kernel,
        grid=(pairs,),
        in_specs=[pl.BlockSpec(memory_space=pltpu.SMEM)] + [tile] * 5,
        out_specs=[tile, pl.BlockSpec((2, 1, rows), lambda i: (i, 0, 0))],
        out_shape=[
            jax.ShapeDtypeStruct((rows, WIDTH), BF),
            jax.ShapeDtypeStruct((2 * pairs, 1, rows), F32),
        ],
        compiler_params=pltpu.CompilerParams(vmem_limit_bytes=VMEM_LIMIT),
        name="attend",
    )(info, query, *own, *other)


def sibling_copies(sent, targets, sems, index, width, slots):
    columns = pl.ds(pl.multiple_of(index * width, width), width)
    return [
        pltpu.make_async_remote_copy(
            src_ref=sent.at[kind, index % slots],
            dst_ref=target.at[:, columns],
            send_sem=sems[0].at[kind, index],
            recv_sem=sems[1].at[kind, index],
            device_id=(flip(lax.axis_index("dp"), 1), lax.axis_index("tp")),
            device_id_type=MESH,
        )
        for kind, target in enumerate(targets)
    ]


def attend_back_kernel(
    info_ref, q, k0, v0, k1, v1, do, o, lse, cos, sin,
    dq_ref, dk_ref, dv_ref, dk_in, dv_in, sent, *sems
):
    step = pl.program_id(0)
    last = pl.num_programs(0) - 1
    width = 2 * HEAD_DIM
    steps = WIDTH // width
    copies = lambda index: sibling_copies(sent, (dk_in, dv_in), sems, index, width, steps)

    @pl.when(step == 0)
    def _():
        greet([(flip(lax.axis_index("dp"), 1), lax.axis_index("tp"))])

    keys = k0.shape[0]
    biases = [key_bias(info_ref[0], info_ref[1 + which], keys) for which in range(2)]
    dq, results = attend_back_pair(biases, q, k0, v0, k1, v1, do, o, lse)
    dq_ref[...] = turn(dq, cos[...], -sin[...]).astype(BF)
    dk_ref[...], dv_ref[...] = results[0]
    sent[0, step] = results[1][0].astype(BF)
    sent[1, step] = results[1][1].astype(BF)
    for copy in copies(step):
        copy.start()

    @pl.when(step == last)
    def _():
        for index in range(steps):
            for copy in copies(index):
                copy.wait()


def attend_back(info, query, own, other, heads_grad, outputs, lse, cosine, sine):
    rows = query.shape[0]
    pairs = WIDTH // (2 * HEAD_DIM)
    width = 2 * HEAD_DIM
    tile = pl.BlockSpec((rows, width), lambda i: (0, i))
    fixed = pl.BlockSpec((rows, width), lambda i: (0, 0))
    dma = pltpu.SemaphoreType.DMA
    return pl.pallas_call(
        attend_back_kernel,
        grid=(pairs,),
        in_specs=[pl.BlockSpec(memory_space=pltpu.SMEM)]
        + [tile] * 7
        + [pl.BlockSpec((2, 1, rows), lambda i: (i, 0, 0)), fixed, fixed],
        out_specs=[tile] * 3 + [ANY] * 2,
        out_shape=[
            jax.ShapeDtypeStruct((rows, WIDTH), BF),
            jax.ShapeDtypeStruct((rows, WIDTH), F32),
            jax.ShapeDtypeStruct((rows, WIDTH), F32),
            jax.ShapeDtypeStruct((rows, WIDTH), BF),
            jax.ShapeDtypeStruct((rows, WIDTH), BF),
        ],
        scratch_shapes=[
            pltpu.VMEM((2, pairs, rows, width), BF),
            dma((2, pairs)),
            dma((2, pairs)),
        ],
        compiler_params=comm_params(3),
        name="attend_back",
    )(info, query, *own, *other, heads_grad, outputs, lse, cosine, sine)


def forward_kernel(
    mel, noise, extra, facts, mods, cot, qkv, out_w, up_w, down_w, table, mel_w, text_w, cos, sin,
    facts_all, mod_row, mine_out, extra_out, qkv_full, feats_out, text_out, hidden_out, x_out,
    q_out, k_out, v_out, ki_out, vi_out, heads_out, lse_out,
    layer_out, mid_out, heads_grad_out, out_grad_out, sums_out, up_out, down_out,
    mel_in, noise_in, extra_in, facts_v, mods_v, table_v, mel_wv, text_wv, cos_v, sin_v,
    feats_v, text_v, hidden_v, x_v, q_v, k_v, v_v, ki_v, vi_v, heads_v, lse_v, full_v, outw_v,
    up_v, down_v, cot_v, sum_v, mid_v, normed_v, y_v, xt, up_ring, down_ring, rows_v, mine_v, sums_v,
    load_sems, save_sems, ring_sems, fact_sends, fact_recvs, mod_sends, mod_recvs, swap_sends, swap_recvs,
    kv_sends, kv_recvs, *scratch
):
    step = pl.program_id(0)
    steps = WIDTH // (2 * HEAD_DIM)
    last = steps - 1
    place = Place()
    dp, tp = place.dp, place.tp
    rows = x_v.shape[0]
    width = full_v.shape[-1]
    partner = (flip(dp, 1), flip(tp, 1))
    sibling = place.plane(1)
    moves = place.core != tp % 2
    stays = jnp.logical_not(moves)
    gathers = [
        Gather(place, qkv, full_v, scratch[2 * j : 2 * j + 2], (j + 1,)) for j in range(3)
    ] + [Gather(place, out_w, outw_v, scratch[6:8])] + [
        Gather(place, shard, full, scratch[8 + 2 * j : 10 + 2 * j], (j // 2 + 1,))
        for j, (shard, full) in enumerate(((up_w, up_v), (down_w, down_v)) * 3)
    ]
    swaps = [
        remote(source, target, (swap_sends, swap_recvs), index, partner)
        for index, (source, target) in enumerate(
            ((mel, mel_in), (noise, noise_in), (extra, extra_in), (cot, cot_v))
        )
    ]
    own_qkv = pltpu.make_async_copy(qkv, full_v.at[0], load_sems.at[0])
    own_rest = [
        pltpu.make_async_copy(shard, full.at[0], load_sems.at[11 + index])
        for index, (shard, full) in enumerate(((out_w, outw_v), (up_w, up_v), (down_w, down_v)))
    ]
    own_cot = pltpu.make_async_copy(cot, cot_v, load_sems.at[14])
    loads = [
        pltpu.make_async_copy(source, target, load_sems.at[index + 1])
        for index, (source, target) in enumerate(
            (
                (facts, facts_v.at[dp]),
                (mods, mods_v.at[place.core, tp]),
                (table, table_v),
                (mel_w, mel_wv),
                (text_w, text_wv),
                (cos, cos_v),
                (sin, sin_v),
            )
        )
    ]
    frames_own = [
        pltpu.make_async_copy(source, target, load_sems.at[8 + index])
        for index, (source, target) in enumerate(((mel, mel_in), (noise, noise_in), (extra, extra_in)))
    ]
    early_saves = [(feats_v, feats_out), (text_v, text_out), (hidden_v, hidden_out), (x_v, x_out)]
    early_saves += [(facts_v, facts_all), (rows_v, mod_row), (mine_v, mine_out), (extra_in, extra_out)]
    late_saves = [(q_v, q_out), (k_v, k_out), (v_v, v_out), (ki_v, ki_out), (vi_v, vi_out)]
    late_saves += [(full_v, qkv_full)]
    final_saves = [(heads_v, heads_out), (lse_v, lse_out)]
    end_saves = [(k_v, layer_out), (mid_v, mid_out), (v_v, heads_grad_out), (outw_v, out_grad_out)]
    end_saves += [(sums_v, sums_out)]
    saves = [
        pltpu.make_async_copy(source, target, save_sems.at[index])
        for index, (source, target) in enumerate(early_saves + late_saves + final_saves + end_saves)
    ]
    n_early, n_late = len(early_saves), len(late_saves)
    n_final = n_early + n_late + len(final_saves)

    def ring_copies(rank):
        return [
            pltpu.make_async_copy(ring.at[rank % 2], target.at[rank], ring_sems.at[kind, rank])
            for kind, (ring, target) in enumerate(((up_ring, up_out), (down_ring, down_out)))
        ]

    def kv_copies(rank):
        columns = pl.ds(pl.multiple_of(rank * width, width), width)
        return [
            remote(
                source.at[:, columns], target.at[:, columns],
                (kv_sends.at[kind], kv_recvs.at[kind]), rank, sibling,
            )
            for kind, (source, target) in enumerate(((k_v, ki_v), (v_v, vi_v)))
        ]

    @pl.when(step == 0)
    def _():
        for copy in loads:
            copy.start()
        own_qkv.start()
        for copy in own_rest:
            copy.start()
        greet(
            [(flip3(dp, k), tp) for k in range(1, 8)]
            + [place.ahead(step) for step in (1, 2, 3)]
            + [(flip(dp, 1), (tp + step) % 4) for step in (1, 2, 3)]
        )
        fact_copies = [
            remote(facts, facts_v.at[dp], (fact_sends, fact_recvs), k - 1, (flip3(dp, k), tp))
            for k in range(1, 8)
        ]
        mod_copies = []
        for index in range(1, 8):
            target = (flip(dp, 1) if index >= 4 else dp, (tp + index) % 4)
            mod_copies.append(
                remote(mods, mods_v.at[place.core, tp], (mod_sends, mod_recvs), index - 1, target)
            )
        @pl.when(moves)
        def _():
            for copy in swaps[:3]:
                copy.start()

        @pl.when(stays)
        def _():
            for copy in frames_own:
                copy.start()

        for copy in fact_copies + mod_copies:
            copy.start()
        gathers[0].stage0()

        @pl.when(moves)
        def _():
            for copy in swaps[:3]:
                copy.wait()

        @pl.when(stays)
        def _():
            for copy in frames_own:
                copy.wait()

        gathers[1].stage0()
        gathers[0].stage1()
        for copy in loads[:2] + fact_copies + mod_copies:
            copy.wait()
        gathers[2].stage0()
        pick = lambda pair: jnp.where(tp // 2 == 0, pair[0:1], pair[1:2])
        source = dp - place.core + tp % 2
        mine = pick(facts_v[source, 0:8, TIME_DIM : TIME_DIM + 128])
        mine_v[...] = jnp.broadcast_to(mine, mine_v.shape)
        time_here, keep_audio, keep_text = mine[:, 0:1], mine[:, 2:3], mine[:, 3:4]
        chunk = WIDTH // 2
        per_rank = mods_v.shape[-1] // chunk
        for index in range(12):
            lane = index % per_rank * chunk
            rows_v[index // 2 : index // 2 + 1, index % 2 * chunk : (index % 2 + 1) * chunk] = pick(
                mods_v[tp % 2, index // per_rank, 0:8, lane : lane + chunk]
            )
        bins = mel_wv.shape[0] // 2
        extras = extra_in[...].astype(F32)
        mel_f = mel_in[...].astype(F32)
        keep_cond = (1.0 - extras[0:1]) * keep_audio
        feats_v[0:bins] = ((1.0 - time_here) * noise_in[...].astype(F32) + time_here * mel_f).astype(BF)
        feats_v[bins : 2 * bins] = (mel_f * keep_cond).astype(BF)
        ids = (extras[1:2] * 256.0 + extras[2:3]).astype(jnp.int32)
        ids = jnp.broadcast_to(ids, (8, rows)).T[:, 0:1]
        for copy in loads[2:]:
            copy.wait()
        vocabulary = table_v.shape[0]
        span = 512
        for first in range(0, vocabulary, span):
            lane = lax.broadcasted_iota(jnp.int32, (rows, span), 1) + first
            one_hot = (lane == ids).astype(F32).astype(BF)
            term = dot(one_hot, table_v[first : first + span])
            if first == 0:
                hidden_v[:, :TEXT_DIM] = term
            else:
                hidden_v[:, :TEXT_DIM] += term
        text_v[...] = (hidden_v[:, :TEXT_DIM] * keep_text).astype(BF)
        gathers[1].stage1()
        gathers[3].stage0()
        hidden_v[...] = dot(text_v[...], text_wv[...]) + dot(feats_v[...], mel_wv[...], 0, 0)
        gathers[0].stage2()
        block = 128
        for first in range(0, rows, block):
            values = hidden_v[first : first + block]
            normed, _ = norm_parts(values)
            x_v[first : first + block] = (normed * (1.0 + rows_v[1:2]) + rows_v[0:1]).astype(BF)
        gathers[2].stage1()
        gathers[4].stage0()
        gathers[5].stage0()
        for copy in saves[:n_early]:
            copy.start()
        own_qkv.wait()

    g = gathers
    schedule = {
        1: [g[0].stage3, g[1].stage2, g[3].stage1, g[6].stage0, g[7].stage0],
        2: [g[0].stage4, g[2].stage2, g[1].stage3, g[4].stage1],
        3: [g[3].stage2, g[2].stage3, g[5].stage1, g[8].stage0, g[9].stage0],
        4: [g[1].stage4, g[4].stage2, g[3].stage3],
        5: [g[2].stage4, g[5].stage2, g[6].stage1],
        6: [g[4].stage3, g[7].stage1, g[3].stage4],
        7: [g[5].stage3, g[6].stage2, g[8].stage1],
        8: [g[9].stage1, g[7].stage2, g[6].stage3],
        9: [g[8].stage2, g[7].stage3, g[4].stage4, g[5].stage4],
        10: [g[9].stage2, g[8].stage3, g[6].stage4, g[7].stage4],
        11: [g[9].stage3, g[8].stage4, g[9].stage4],
    }
    for index, stages in schedule.items():

        @pl.when(step == index)
        def _(stages=stages):
            for stage in stages:
                stage()

    @pl.when(jnp.logical_and(step % 2 == 0, step < steps))
    def _():
        rank = step // 2
        columns = pl.ds(pl.multiple_of(rank * width, width), width)
        x = x_v[...]
        wide = lambda v: jnp.concatenate([v, v], axis=1)
        cosine, sine = wide(cos_v[...]), wide(sin_v[...])
        weight = lambda part: full_v[rank, part].reshape(WIDTH, width)
        k_v[:, columns] = turn(dot(x, weight(1)), cosine, sine).astype(BF)
        v_v[:, columns] = dot(x, weight(2)).astype(BF)
        for copy in kv_copies(rank):
            copy.start()
        q_v[:, columns] = turn(dot(x, weight(0)), cosine, sine).astype(BF)

        @pl.when(jnp.logical_and(step == 4, moves))
        def _():
            swaps[3].start()

        @pl.when(jnp.logical_and(step == 4, stays))
        def _():
            own_cot.start()

        for copy in kv_copies(rank):
            copy.wait()

    @pl.when(step == last - 1)
    def _():
        for copy in saves[n_early : n_early + n_late]:
            copy.start()

    @pl.when(step < steps)
    def _():
        length = mine_v[0:1, 1:2].astype(jnp.int32)
        biases = [
            key_bias(length, place.core * rows, rows),
            key_bias(length, (1 - place.core) * rows, rows),
        ]
        columns = pl.ds(pl.multiple_of(step * 2 * HEAD_DIM, 2 * HEAD_DIM), 2 * HEAD_DIM)
        output, totals = attend_pair(
            *biases, *[ref.at[:, columns] for ref in (q_v, k_v, v_v, ki_v, vi_v)]
        )
        heads_v[:, columns] = output
        lse_v[2 * step], lse_v[2 * step + 1] = totals

    block = 128

    @pl.when(step == last)
    def _():
        for copy in saves[n_early + n_late : n_final]:
            copy.start()
        for copy in own_rest:
            copy.wait()
        sum_v[...] = dot(heads_v[...], outw_v[...].reshape(WIDTH, WIDTH))
        for first in range(0, rows, block):
            here = slice(first, first + block)
            values = hidden_v[here] + rows_v[2:3] * sum_v[here]
            mid_v[here] = values
            normed, _ = norm_parts(values)
            normed_v[here] = (normed * (1.0 + rows_v[4:5]) + rows_v[3:4]).astype(BF)
        for copy in saves[: n_early + n_late]:
            copy.wait()

        @pl.when(moves)
        def _():
            swaps[3].wait()

        @pl.when(stays)
        def _():
            own_cot.wait()

        xt[...] = normed_v[...].T
        ki_v[...] = (rows_v[5:6] * cot_v[...].astype(F32)).astype(BF)
        y_v[...] = jnp.zeros_like(y_v)
        hidden_v[...] = jnp.zeros_like(hidden_v)

    @pl.when(step >= steps)
    def _():
        rank = step - steps

        @pl.when(rank >= 2)
        def _():
            for copy in ring_copies(rank - 2):
                copy.wait()

        units = down_v.shape[2] * down_v.shape[3] * down_v.shape[4]
        up_weight = up_v[rank, 0].reshape(WIDTH, units)
        down_weight = down_v[rank, 0].reshape(units, WIDTH)
        act, slope = gelu_parts(dot(normed_v[...], up_weight))
        grad = ki_v[...]
        up_grad = (dot(grad, down_weight, 1, 1) * slope).astype(BF)
        down_ring[rank % 2] = dot(act, grad, 0, 0).astype(BF)
        up_ring[rank % 2] = dot(xt[...], up_grad).astype(BF)
        for copy in ring_copies(rank):
            copy.start()
        y_v[...] += dot(act, down_weight)
        hidden_v[...] += dot(up_grad, up_weight, 1, 1)

    @pl.when(step == pl.num_programs(0) - 1)
    def _():
        totals = [jnp.zeros((1, WIDTH), F32) for _ in range(4)]
        for first in range(0, rows, block):
            here = slice(first, first + block)
            values, dx, y = mid_v[here], hidden_v[here], y_v[here]
            out_grad = cot_v[here].astype(F32)
            k_v[here] = (values + rows_v[5:6] * y).astype(BF)
            normed, inverse = norm_parts(values)
            mid_grad = out_grad + norm_back(normed, inverse, rows_v[4:5], dx)
            mid_v[here] = mid_grad
            q_v[here] = (rows_v[2:3] * mid_grad).astype(BF)
            for index, term in enumerate(
                (sum_v[here] * mid_grad, dx, dx * normed, out_grad * y)
            ):
                totals[index] += jnp.sum(term, axis=0, keepdims=True)
        for index in range(4):
            sums_v[index : index + 1] = totals[index]
        sums_v[4:8] = jnp.zeros((4, WIDTH), F32)
        for copy in saves[n_final : n_final + 2] + saves[n_final + 4 :]:
            copy.start()
        v_v[...] = dot(q_v[...], outw_v[...].reshape(WIDTH, WIDTH), 1, 1).astype(BF)
        saves[n_final + 2].start()
        for gather in gathers:
            gather.finish()
        outw_v[...] = dot(heads_v[...], q_v[...], 0, 0).astype(BF).reshape(outw_v.shape)
        saves[n_final + 3].start()
        for rank in (2, 3):
            for copy in ring_copies(rank):
                copy.wait()
        for copy in saves[n_early + n_late :]:
            copy.wait()


def forward(mel, noise, extra, facts, mods, cot, qkv, out_w, up_w, down_w, table, mel_w, text_w, cosine, sine):
    rows = cot.shape[0]
    width = qkv.shape[2]
    dma = pltpu.SemaphoreType.DMA
    shape = lambda s, t=BF: jax.ShapeDtypeStruct(s, t)
    full = (4, 3) + pieces(qkv.shape)[1:]
    parted = [w.reshape((1,) + pieces(w.shape)) for w in (out_w, up_w, down_w)]
    head_count = WIDTH // HEAD_DIM
    frames = (rows, WIDTH)
    feats = (mel_w.shape[0], rows)
    text = (rows, TEXT_DIM)
    all_facts = (8,) + facts.shape
    lse = (head_count, 1, rows)
    outs = pl.pallas_call(
        forward_kernel,
        grid=(WIDTH // (2 * HEAD_DIM) + 4,),
        in_specs=[ANY] * 15,
        out_specs=[ANY] * 23,
        out_shape=[
            shape(all_facts, F32), shape((8, WIDTH), F32), shape((8, 128), F32), shape(extra.shape),
            shape(full), shape(feats), shape(text), shape(frames, F32), shape(frames),
        ]
        + [shape(frames)] * 6
        + [shape(lse, F32)]
        + [shape(frames), shape(frames, F32), shape(frames), shape((4,) + parted[0].shape)]
        + [shape((8, WIDTH), F32), shape((4,) + up_w.shape), shape((4,) + down_w.shape)],
        scratch_shapes=[
            *[pltpu.VMEM(v.shape, BF) for v in (mel, noise, extra)], pltpu.VMEM(all_facts, F32),
            pltpu.VMEM((2, 4) + mods.shape, F32), pltpu.VMEM(table.shape, BF),
            pltpu.VMEM(mel_w.shape, BF), pltpu.VMEM(text_w.shape, BF),
            pltpu.VMEM(cosine.shape, F32), pltpu.VMEM(sine.shape, F32),
            pltpu.VMEM(feats, BF), pltpu.VMEM(text, BF), pltpu.VMEM(frames, F32), pltpu.VMEM(frames, BF),
        ]
        + [pltpu.VMEM(frames, BF)] * 6
        + [pltpu.VMEM(lse, F32), pltpu.VMEM(full, BF)]
        + [pltpu.VMEM((4,) + w.shape, BF) for w in parted]
        + [
            pltpu.VMEM(frames, BF), pltpu.VMEM(frames, F32), pltpu.VMEM(frames, F32),
            pltpu.VMEM(frames, BF), pltpu.VMEM(frames, F32), pltpu.VMEM((WIDTH, rows), BF),
            pltpu.VMEM((2,) + up_w.shape, BF), pltpu.VMEM((2,) + down_w.shape, BF),
            pltpu.VMEM((8, WIDTH), F32), pltpu.VMEM((8, 128), F32), pltpu.VMEM((8, WIDTH), F32),
            dma((15,)), dma((24,)), dma((2, 4)), dma((7,)), dma((7,)), dma((7,)), dma((7,)), dma((4,)),
            dma((4,)), dma((2, 4)), dma((2, 4)),
        ]
        + Gather.scratch() * 10,
        compiler_params=comm_params(0),
        name="forward",
    )(
        mel, noise, extra, facts, mods, cot, qkv.reshape(pieces(qkv.shape)), *parted, table, mel_w,
        text_w, cosine, sine,
    )
    outs = list(outs)
    outs[4] = outs[4].reshape(4, 3, WIDTH, width)
    outs[19] = outs[19].reshape((4,) + out_w.shape)
    return outs


def qkv_kernel(x_ref, w_ref, cos_ref, sin_ref, q_ref, k_ref, v_ref, ko_ref, vo_ref, sent, send_sems, recv_sems):
    step = pl.program_id(0)
    last = pl.num_programs(0) - 1
    width = q_ref.shape[1]
    sibling = (flip(lax.axis_index("dp"), 1), lax.axis_index("tp"))

    def copies(index):
        columns = pl.ds(pl.multiple_of(index * width, width), width)
        return [
            pltpu.make_async_remote_copy(
                src_ref=sent.at[kind, index],
                dst_ref=target.at[:, columns],
                send_sem=send_sems.at[kind, index],
                recv_sem=recv_sems.at[kind, index],
                device_id=sibling,
                device_id_type=MESH,
            )
            for kind, target in ((0, ko_ref), (1, vo_ref))
        ]

    @pl.when(step == 0)
    def _():
        greet([sibling])

    x = x_ref[...]
    key = turn(dot(x, w_ref[0, 1]), cos_ref[...], sin_ref[...]).astype(BF)
    value = dot(x, w_ref[0, 2]).astype(BF)
    k_ref[...] = key
    v_ref[...] = value
    sent[0, step] = key
    sent[1, step] = value
    for copy in copies(step):
        copy.start()
    q_ref[...] = turn(dot(x, w_ref[0, 0]), cos_ref[...], sin_ref[...]).astype(BF)

    @pl.when(step == last)
    def _():
        for index in range(WIDTH // width):
            for copy in copies(index):
                copy.wait()


def project_qkv(x, weights, cosine, sine):
    rows = x.shape[0]
    ranks, width = weights.shape[0], weights.shape[3]
    tile = pl.BlockSpec((rows, width), lambda r: (0, r))
    whole = lambda shape: pl.BlockSpec(shape, lambda r: (0, 0))
    dma = pltpu.SemaphoreType.DMA
    return pl.pallas_call(
        qkv_kernel,
        grid=(ranks,),
        in_specs=[
            whole(x.shape),
            pl.BlockSpec((1, 3, WIDTH, width), lambda r: (r, 0, 0, 0)),
            whole((rows, width)),
            whole((rows, width)),
        ],
        out_specs=[tile] * 3 + [ANY] * 2,
        out_shape=[jax.ShapeDtypeStruct((rows, WIDTH), BF)] * 5,
        scratch_shapes=[pltpu.VMEM((2, ranks, rows, width), BF), dma((2, ranks)), dma((2, ranks))],
        compiler_params=comm_params(1),
        name="project_qkv",
    )(x, weights, cosine, sine)


def qkv_back_kernel(
    x_ref, w_ref, cos_ref, sin_ref, dq_ref, dk_ref, dv_ref, dki_ref, dvi_ref, grad_ref, dx_ref, xt
):
    step = pl.program_id(0)

    @pl.when(step == 0)
    def _():
        xt[...] = x_ref[...].T

    dq = dq_ref[...]
    dk = turn(dk_ref[...] + dki_ref[...].astype(F32), cos_ref[...], -sin_ref[...]).astype(BF)
    dv = (dv_ref[...] + dvi_ref[...].astype(F32)).astype(BF)
    total = None
    for part, grad in enumerate((dq, dk, dv)):
        grad_ref[0, part] = dot(xt[...], grad).astype(BF)
        term = dot(grad, w_ref[0, part], 1, 1)
        total = term if total is None else total + term

    @pl.when(step == 0)
    def _():
        dx_ref[...] = total

    @pl.when(step > 0)
    def _():
        dx_ref[...] += total


def project_qkv_back(x, weights, cosine, sine, dq, dk, dv, dk_in, dv_in):
    rows = x.shape[0]
    ranks, width = weights.shape[0], weights.shape[3]
    tile = pl.BlockSpec((rows, width), lambda r: (0, r))
    whole = lambda shape: pl.BlockSpec(shape, lambda r: (0, 0))
    wide = pl.BlockSpec((1, 3, WIDTH, width), lambda r: (r, 0, 0, 0))
    return pl.pallas_call(
        qkv_back_kernel,
        grid=(ranks,),
        in_specs=[whole(x.shape), wide, whole((rows, width)), whole((rows, width))] + [tile] * 5,
        out_specs=[wide, whole((rows, WIDTH))],
        out_shape=[
            jax.ShapeDtypeStruct(weights.shape, BF),
            jax.ShapeDtypeStruct((rows, WIDTH), F32),
        ],
        scratch_shapes=[pltpu.VMEM((WIDTH, rows), BF)],
        compiler_params=pltpu.CompilerParams(vmem_limit_bytes=VMEM_LIMIT),
        name="project_qkv_back",
    )(x, weights, cosine, sine, dq, dk, dv, dk_in, dv_in)


def gelu_parts(up):
    root = math.sqrt(2.0 / math.pi)
    square = up * up
    bent = jnp.tanh(root * (up + 0.044715 * up * square))
    half = 0.5 * (1.0 + bent)
    slope = half + 0.5 * up * (1.0 - bent * bent) * root * (1.0 + 3 * 0.044715 * square)
    return (up * half).astype(BF), slope


def mlp_kernel(
    x_ref, cot_ref, row_ref, mid_ref, sum_ref, heads_ref, out_w_ref, wu_ref, wd_ref,
    layer_ref, mid_grad_ref, heads_grad_ref, out_grad_ref, sums_ref, du_ref, dd_ref,
    xt, grad_ref, y_ref, dx_ref, attn_ref
):
    step = pl.program_id(0)
    last = pl.num_programs(0) - 1

    @pl.when(step == 0)
    def _():
        xt[...] = x_ref[...].T
        grad_ref[...] = (row_ref[5:6] * cot_ref[...].astype(F32)).astype(BF)

    act, slope = gelu_parts(dot(x_ref[...], wu_ref[0]))
    grad = grad_ref[...]
    up_grad = (dot(grad, wd_ref[0], 1, 1) * slope).astype(BF)
    dd_ref[0] = dot(act, grad, 0, 0).astype(BF)
    du_ref[0] = dot(xt[...], up_grad).astype(BF)
    y = dot(act, wd_ref[0])
    dx = dot(up_grad, wu_ref[0], 1, 1)

    @pl.when(step == 0)
    def _():
        y_ref[...] = y
        dx_ref[...] = dx

    @pl.when(step > 0)
    def _():
        y_ref[...] += y
        dx_ref[...] += dx

    @pl.when(step == last)
    def _():
        block = 128
        totals = [jnp.zeros((1, WIDTH), F32) for _ in range(4)]
        for first in range(0, x_ref.shape[0], block):
            here = slice(first, first + block)
            values, dx, y = mid_ref[here], dx_ref[here], y_ref[here]
            out_grad = cot_ref[here].astype(F32)
            layer_ref[here] = (values + row_ref[5:6] * y).astype(BF)
            normed, inverse = norm_parts(values)
            mid_grad = out_grad + norm_back(normed, inverse, row_ref[4:5], dx)
            mid_grad_ref[here] = mid_grad
            attn_ref[here] = (row_ref[2:3] * mid_grad).astype(BF)
            for index, term in enumerate(
                (sum_ref[here] * mid_grad, dx, dx * normed, out_grad * y)
            ):
                totals[index] += jnp.sum(term, axis=0, keepdims=True)
        for index in range(4):
            sums_ref[index : index + 1] = totals[index]
        sums_ref[4:8] = jnp.zeros((4, WIDTH), F32)
        heads_grad_ref[...] = dot(attn_ref[...], out_w_ref[...], 1, 1).astype(BF)
        out_grad_ref[...] = dot(heads_ref[...], attn_ref[...], 0, 0).astype(BF)


def mlp(x, cot, mod_rows, hidden_mid, attn_sum, heads_out, out_full, up_full, down_full):
    rows = x.shape[0]
    ranks, _, units = up_full.shape
    one = lambda shape: pl.BlockSpec(shape, lambda r: (0, 0), pipeline_mode=pl.Buffered(1))
    whole, square, row = one((rows, WIDTH)), one((WIDTH, WIDTH)), one((8, WIDTH))
    up_spec = pl.BlockSpec((1, WIDTH, units), lambda r: (r, 0, 0))
    down_spec = pl.BlockSpec((1, units, WIDTH), lambda r: (r, 0, 0))
    frames = (rows, WIDTH)
    return pl.pallas_call(
        mlp_kernel,
        grid=(ranks,),
        in_specs=[whole, whole, row, whole, whole, whole, square, up_spec, down_spec],
        out_specs=[whole, whole, whole, square, row, up_spec, down_spec],
        out_shape=[
            jax.ShapeDtypeStruct(frames, BF),
            jax.ShapeDtypeStruct(frames, F32),
            jax.ShapeDtypeStruct(frames, BF),
            jax.ShapeDtypeStruct((WIDTH, WIDTH), BF),
            jax.ShapeDtypeStruct((8, WIDTH), F32),
            jax.ShapeDtypeStruct(up_full.shape, BF),
            jax.ShapeDtypeStruct(down_full.shape, BF),
        ],
        scratch_shapes=[
            pltpu.VMEM((WIDTH, rows), BF),
            pltpu.VMEM(frames, BF),
            pltpu.VMEM(frames, F32),
            pltpu.VMEM(frames, F32),
            pltpu.VMEM(frames, BF),
        ],
        compiler_params=pltpu.CompilerParams(vmem_limit_bytes=VMEM_LIMIT),
        name="mlp",
    )(x, cot, mod_rows, hidden_mid, attn_sum, heads_out, out_full, up_full, down_full)


def backward_kernel(
    q, k0, v0, k1, v1, do, o, lse, cos, sin, mine_ref, row_ref, extra_ref, mod_in_ref,
    x_ref, w_ref, value_ref, mid_ref, feat_ref, mel_w_ref, text_w_ref, proj_ref, layer_ref, down_grads, up_grads, out_grads,
    sums_ref, act_ref, mel_out, layer_out, qkv_out, misc_out, down_out, up_out, out_out,
    dq_v, dk_v, dv_v, dki_v, dvi_v, sent, xt, tiles, total_ref, hidden_ref, text_ref, blocks_v,
    qkv_grads, misc_grads, mel_v,
    mod_ref, line, every, part_ref, acts, down_v, up_v, out_v, qkv_v, misc_v,
    down_buffer, up_buffer,
    kv_sends, kv_recvs, load_sems, tile_sems, block_sems, line_sends, line_recvs, every_sends,
    every_recvs, act_sends, act_recvs, end_sends, end_recvs, *scratch
):
    step = pl.program_id(0)
    last = pl.num_programs(0) - 1
    place = Place()
    dp, tp = place.dp, place.tp
    partner = (flip(dp, 1), flip(tp, 1))
    moves = place.core != tp % 2
    stays = jnp.logical_not(moves)
    rows = dq_v.shape[0]
    ranks, width = w_ref.shape[0], w_ref.shape[3]
    pair_width = 2 * HEAD_DIM
    steps = WIDTH // pair_width
    size = 8
    early = [
        Reduce(place, grads.at[:, h], out.at[h], target.at[h], scratch[size * j : size * (j + 1)], buffer)
        for j, (grads, out, target, h, buffer) in enumerate(
            (
                (down_grads, down_v, down_out, 0, down_buffer),
                (up_grads, up_v, up_out, 0, up_buffer),
                (down_grads, down_v, down_out, 1, down_buffer),
                (up_grads, up_v, up_out, 1, up_buffer),
                (out_grads, out_v, out_out, 0, down_buffer),
            )
        )
    ]
    late = [
        Reduce(
            place, qkv_grads.at[part], qkv_v.at[part], qkv_out.at[part],
            scratch[size * (5 + part) : size * (6 + part)],
        )
        for part in range(3)
    ] + [
        Reduce(
            place, misc_grads.at[h], misc_v.at[h], misc_out.at[h],
            scratch[size * (8 + h) : size * (9 + h)], absolute=True,
        )
        for h in range(2)
    ]
    loads = [
        pltpu.make_async_copy(source, target, load_sems.at[index])
        for index, (source, target) in enumerate(
            (
                (x_ref, hidden_ref),
                (text_w_ref, dk_v),
                (feat_ref, dv_v.at[:, pl.ds(0, feat_ref.shape[1])]),
                (mel_w_ref, dki_v.at[pl.ds(0, mel_w_ref.shape[0])]),
            )
        )
    ]
    def tile_load(part, rank):
        number = part * ranks + rank
        return pltpu.make_async_copy(
            w_ref.at[rank, part], tiles.at[number % 2], tile_sems.at[number]
        )

    span = tiles.shape[2]
    proj_loads = [
        pltpu.make_async_copy(
            proj_ref.at[:, pl.ds(index * span, span)], tiles.at[index % 2], tile_sems.at[3 * ranks + index]
        )
        for index in range(proj_ref.shape[1] // span)
    ]
    block = blocks_v.shape[2]
    block_loads = [
        [
            pltpu.make_async_copy(
                source.at[pl.ds(index * block, block)], blocks_v.at[index % 2, kind], block_sems.at[index, kind]
            )
            for kind, source in enumerate((value_ref, mid_ref))
        ]
        for index in range(rows // block)
    ]

    def outward(index, source, target):
        away = remote(source, target, (end_sends, end_recvs), index, partner)
        here = pltpu.make_async_copy(source, target, end_sends.at[2 + index])
        return away, here

    layer_load = pltpu.make_async_copy(layer_ref, dq_v, load_sems.at[4])
    ends = [outward(0, dq_v, layer_out), outward(1, mel_v, mel_out)]
    kv_copies = lambda index: sibling_copies(
        sent, (dki_v, dvi_v), (kv_sends, kv_recvs), index, pair_width, sent.shape[1]
    )

    def send_outward(index):
        @pl.when(moves)
        def _():
            ends[index][0].start()

        @pl.when(stays)
        def _():
            ends[index][1].start()

    @pl.when(step == 0)
    def _():
        loads[0].start()
        for copy in [tile_load(0, 0), tile_load(0, 1)] + block_loads[0] + block_loads[1]:
            copy.start()
        greet(
            [(flip3(dp, k), tp) for k in range(1, 8)]
            + [place.ahead(step) for step in (1, 2, 3)]
            + [partner]
        )

    flow = Flow()
    for index in range(steps):
        if index in JOINS:
            flow.add(early[JOINS.index(index)])
        stages = flow.take()

        @pl.when(step == index)
        def _(stages=stages):
            for stage in stages:
                stage()

    columns = pl.ds(pl.multiple_of(step * pair_width, pair_width), pair_width)
    slots = sent.shape[1]
    length = mine_ref[0:1, 1:2].astype(jnp.int32)
    biases = [
        key_bias(length, place.core * rows, rows),
        key_bias(length, (1 - place.core) * rows, rows),
    ]
    dq, results = attend_back_pair(biases, q, k0, v0, k1, v1, do, o, lse)
    dq_v[:, columns] = turn(dq, cos[...], -sin[...]).astype(BF)
    dk_v[:, columns] = results[0][0].astype(dk_v.dtype)
    dv_v[:, columns] = results[0][1].astype(dv_v.dtype)

    @pl.when(step >= slots)
    def _():
        for copy in kv_copies(step - slots):
            copy.wait_send()

    sent[0, step % slots] = results[1][0].astype(BF)
    sent[1, step % slots] = results[1][1].astype(BF)
    for copy in kv_copies(step):
        copy.start()

    @pl.when(step == last)
    def _():
        loads[0].wait()
        flow.beat()
        xt[...] = hidden_ref[...].T
        total_ref[...] = jnp.zeros_like(total_ref)
        cosine = jnp.concatenate([cos[...]] * (width // pair_width), axis=1)
        sine = -jnp.concatenate([sin[...]] * (width // pair_width), axis=1)
        extras = extra_ref[...].astype(F32)
        ids = (extras[1:2] * 256.0 + extras[2:3]).astype(jnp.int32)
        keep_cond = (1.0 - extras[0:1]) * mine_ref[0:1, 2:3]
        for part in range(3):
            if part == 1:

                @pl.loop(0, steps)
                def _(index):
                    for copy in kv_copies(index):
                        copy.wait_recv()

                @pl.loop(steps - slots, steps)
                def _(index):
                    for copy in kv_copies(index):
                        copy.wait_send()

            def one_rank(rank, part=part):
                side = pl.ds(pl.multiple_of(rank * width, width), width)
                if part == 0:
                    grad = dq_v[:, side]
                elif part == 1:
                    grad = turn(
                        dk_v[:, side].astype(F32) + dki_v[:, side].astype(F32), cosine, sine
                    ).astype(BF)
                else:
                    grad = (dv_v[:, side].astype(F32) + dvi_v[:, side].astype(F32)).astype(BF)
                number = part * ranks + rank
                tile_load(part, rank).wait()
                qkv_grads[part, rank] = (
                    dot(xt[...], grad).astype(BF).reshape(qkv_grads.shape[2:])
                )
                total_ref[...] += dot(grad, tiles[number % 2], 1, 1)

                @pl.when(number + 2 < 3 * ranks)
                def _():
                    tile_load((number + 2) // ranks, (number + 2) % ranks).start()

            pl.loop(0, ranks // 2)(one_rank)
            flow.beat()
            pl.loop(ranks // 2, ranks)(one_rank)
            if part == 0:
                layer_load.start()
            if part == 2:
                layer_load.wait()
                send_outward(0)
                for copy in loads[1:]:
                    copy.start()
            flow.add(late[part])
            flow.beat()

        chunks = mod_ref.shape[1]
        lanes = mod_ref.shape[2]
        totals = [jnp.zeros((1, WIDTH), F32) for _ in range(2)]
        for index in range(rows // block):
            here = slice(index * block, (index + 1) * block)
            for copy in block_loads[index]:
                copy.wait()
            grad = total_ref[here]
            normed, inverse = norm_parts(blocks_v[index % 2, 0])
            hidden_ref[here] = (
                blocks_v[index % 2, 1] + norm_back(normed, inverse, row_ref[1:2], grad)
            ).astype(BF)
            totals[0] += jnp.sum(grad, axis=0, keepdims=True)
            totals[1] += jnp.sum(grad * normed, axis=0, keepdims=True)
            if index + 2 < rows // block:
                for copy in block_loads[index + 2]:
                    copy.start()
        for index in range(4):
            totals.append(mod_in_ref[index : index + 1])
        for index in range(6):
            for chunk in range(WIDTH // lanes):
                row = index * (WIDTH // lanes) + chunk
                mod_ref[row // chunks, row % chunks : row % chunks + 1, :] = totals[index][
                    :, chunk * lanes : (chunk + 1) * lanes
                ]
        line_copies = [
            remote(
                mod_ref.at[(tp + step) % 4], line.at[tp], (line_sends, line_recvs), step - 1, place.ahead(step)
            )
            for step in (1, 2, 3)
        ]
        every_copies = [
            remote(line, every.at[dp], (every_sends, every_recvs), k - 1, (flip3(dp, k), tp))
            for k in range(1, 8)
        ]
        act_copies = [
            remote(part_ref, acts.at[tp], (act_sends, act_recvs), step - 1, place.ahead(step))
            for step in (1, 2, 3)
        ]
        for copy in line_copies:
            copy.start()
        line[tp] = mod_ref[tp]
        flow.beat()

        for copy in loads[1:]:
            copy.wait()
        text_ref[...] = dot(hidden_ref[...], dk_v[...], 1, 1).astype(BF) * mine_ref[0:1, 3:4].astype(BF)
        table_rows = VOCABULARY // ranks
        split = misc_grads.shape[-2] * 16
        shape = misc_grads.shape[2:]

        @pl.loop(0, ranks)
        def _(rank):
            row = lax.broadcasted_iota(jnp.int32, (split, rows), 0) + rank * table_rows
            one_hot = (row == ids).astype(F32).astype(BF)
            misc_grads[0, rank] = dot(one_hot, text_ref[...]).astype(BF).reshape(shape)

        flow.add(late[3])
        flow.beat()
        for copy in line_copies:
            copy.wait()
        every[dp] = line[...]
        for copy in every_copies:
            copy.start()
        feat_rows = feat_ref.shape[1] // ranks
        rest = table_rows - split

        def rest_of(rank, share):
            row = lax.broadcasted_iota(jnp.int32, (rest, rows), 0) + (rank * table_rows + split)
            one_hot = (row == ids).astype(F32).astype(BF)
            table = dot(one_hot, text_ref[...]).astype(BF)
            misc_grads[1, rank] = jnp.concatenate(
                [table, share[:, :TEXT_DIM], share[:, TEXT_DIM:]], axis=0
            ).reshape(shape)

        for rank in range(ranks):
            side = slice(rank * feat_rows, (rank + 1) * feat_rows)
            rest_of(rank, dot(dv_v[:, side], hidden_ref[...], 0, 0).astype(BF))
        flow.add(late[4])
        flow.beat()
        for copy in proj_loads[:2]:
            copy.start()
        mel_part = dot(dki_v[0 : mel_w_ref.shape[0]], hidden_ref[...], 1, 1)
        bins = mel_part.shape[0] // 2
        mel_v[...] = mine_ref[0:1, 0:1] * mel_part[:bins] + keep_cond * mel_part[bins:]
        send_outward(1)
        flow.beat()
        for copy in every_copies:
            copy.wait()
        for pair in range(4):
            sums_ref[pair] = every[2 * pair] + every[2 * pair + 1]
        total = None
        for index, copy in enumerate(proj_loads):
            copy.wait()
            for lane in range(0, span, lanes):
                chunk = (index * span + lane) // lanes
                held = sums_ref[:, :, chunk, :].reshape(16, lanes).astype(BF)
                term = dot(held, tiles[index % 2, :, lane : lane + lanes], 1, 1)
                total = term if total is None else total + term
            if index + 2 < len(proj_loads):
                proj_loads[index + 2].start()
        part_ref[...] = total
        acts[tp] = total
        for copy in act_copies:
            copy.start()
        while flow.beat():
            pass
        for copy in act_copies:
            copy.wait()
        act_ref[...] = acts[...]
        for item in early + late:
            item.save().wait()

        @pl.when(moves)
        def _():
            for away, _ in ends:
                away.wait()

        @pl.when(stays)
        def _():
            for _, here in ends:
                here.wait()


def backward(
    query, own, other, heads_grad, heads_out, lse, cosine, sine, mine, mod_rows, extra, mod_part,
    x, weights, values, mid_grad, feats, mel_w, text_w, mod_proj, layer, down_grad, up_grad, out_grad,
):
    rows = x.shape[0]
    ranks, width = weights.shape[0], weights.shape[3]
    table_rows = VOCABULARY // ranks
    misc_rows = table_rows + 2 * (feats.shape[1] // ranks)
    chunks = mod_proj.shape[1] // 128
    pairs = WIDTH // (2 * HEAD_DIM)
    qkv_block = blocks((WIDTH, width))
    misc_block = blocks((misc_rows // 2, TEXT_DIM))
    dma = pltpu.SemaphoreType.DMA
    vmem = lambda shape, t=BF: pltpu.VMEM(shape, t)
    tile = pl.BlockSpec((rows, 2 * HEAD_DIM), lambda i: (0, i))
    one = lambda v: pl.BlockSpec(v.shape, lambda i: (0,) * v.ndim, pipeline_mode=pl.Buffered(1))
    parts = lambda v, count: v.reshape(
        (ranks, count) + blocks((v.shape[1] // count, v.shape[2]))
    )
    early = (parts(down_grad, 2), parts(up_grad, 2), parts(out_grad, 1))
    scratch = []
    for index in (0, 1, 0, 1, 2):
        block = early[index].shape
        scratch += Reduce.scratch(block[-2] * 16, block[-1])
    for _ in range(3):
        scratch += Reduce.scratch(WIDTH, width)
    for _ in range(2):
        scratch += Reduce.scratch(misc_rows // 2, TEXT_DIM)
    frames = (rows, WIDTH)
    mel_shape = (mel_w.shape[0] // 2, rows)
    sums_shape = jax.ShapeDtypeStruct((4, 4, chunks, 128), F32)
    act_shape = jax.ShapeDtypeStruct((4, 16, WIDTH), F32)
    outs = pl.pallas_call(
        backward_kernel,
        grid=(pairs,),
        in_specs=[tile] * 7
        + [pl.BlockSpec((2, 1, rows), lambda i: (i, 0, 0))]
        + [one(v) for v in (cosine, sine, mine, mod_rows, extra, mod_part)]
        + [ANY] * 12,
        out_specs=[one(sums_shape), one(act_shape)] + [ANY] * 7,
        out_shape=[
            sums_shape,
            act_shape,
            jax.ShapeDtypeStruct(mel_shape, F32),
            jax.ShapeDtypeStruct(frames, BF),
            jax.ShapeDtypeStruct((3,) + qkv_block, BF),
            jax.ShapeDtypeStruct((2,) + misc_block, BF),
        ]
        + [jax.ShapeDtypeStruct(v.shape[1:], BF) for v in early],
        scratch_shapes=[
            vmem(frames), vmem(frames), vmem(frames), vmem(frames), vmem(frames),
            vmem((2, 2, rows, 2 * HEAD_DIM)), vmem((WIDTH, rows)), vmem((2, WIDTH, width)),
            vmem(frames, F32), vmem(frames), vmem((rows, TEXT_DIM)), vmem((2, 2, 64, WIDTH), F32),
            vmem((3, ranks) + qkv_block), vmem((2, ranks) + misc_block), vmem(mel_shape, F32),
            vmem((4, chunks, 128), F32), vmem((4, chunks, 128), F32), vmem((8, 4, chunks, 128), F32),
            vmem((16, WIDTH), F32), vmem((4, 16, WIDTH), F32),
        ]
        + [vmem(v.shape[1:]) for v in early]
        + [vmem((3,) + qkv_block), vmem((2,) + misc_block)]
        + [vmem((ranks,) + v.shape[3:]) for v in early[:2]]
        + [
            dma((2, pairs)), dma((2, pairs)), dma((5,)), dma((3 * ranks + mod_proj.shape[1] // width,)),
            dma((rows // 64, 2)),
            dma((3,)), dma((3,)), dma((7,)), dma((7,)), dma((3,)), dma((3,)), dma((4,)), dma((2,)),
        ]
        + scratch,
        compiler_params=comm_params(4),
        name="backward",
    )(
        query, *own, *other, heads_grad, heads_out, lse, cosine, sine, mine, mod_rows, extra, mod_part,
        x, weights, values, mid_grad, feats, mel_w, text_w, mod_proj, layer, *early,
    )
    outs = list(outs)
    outs[4] = outs[4].reshape(3, WIDTH, width)
    outs[5] = outs[5].reshape(misc_rows, TEXT_DIM)
    outs[6:] = [o.reshape(v.shape[1:]) for o, v in zip(outs[6:], (down_grad, up_grad, out_grad))]
    return outs


def time_features(flow_times, width):
    half_dim = width // 2
    frequency = jnp.exp(
        jnp.arange(half_dim, dtype=F32) * (-math.log(10000.0) / (half_dim - 1))
    )
    angles = 1000.0 * flow_times[:, None] * frequency[None, :]
    return jnp.concatenate([jnp.sin(angles), jnp.cos(angles)], axis=1)


def rope_tables(positions, width):
    lane = jnp.arange(width, dtype=jnp.int32)
    pair = ((lane % HEAD_DIM) // 2).astype(F32)
    inverse = jnp.exp(pair * (-2.0 * math.log(10000.0) / HEAD_DIM))
    angles = positions.astype(F32)[:, None] * inverse[None, :]
    sign = jnp.where(lane % 2 == 0, -1.0, 1.0)
    return jnp.cos(angles), jnp.sin(angles) * sign[None, :]


def norm_parts(values):
    average = jnp.mean(values, axis=-1, keepdims=True)
    centered = values - average
    spread = jnp.mean(centered * centered, axis=-1, keepdims=True)
    inverse = lax.rsqrt(spread + 1e-06)
    return centered * inverse, inverse


def norm_back(normed, inverse, scale_part, grad):
    inner = grad * (1.0 + scale_part)
    first = jnp.mean(inner, axis=-1, keepdims=True)
    second = jnp.mean(inner * normed, axis=-1, keepdims=True)
    return inverse * (inner - first - normed * second)


def body(
    mel_frames, noise_frames, text_ids, span_mask, lengths, audio_drop, text_drop, flow_times,
    in_proj, text_table, time_proj, mod_proj, qkv_proj, out_proj, up_proj, down_proj, cotangent,
):
    dp_size = lax.axis_size("dp")
    tp_size = lax.axis_size("tp")
    dp_rank = lax.axis_index("dp")
    tp_rank = lax.axis_index("tp")
    local_rows = mel_frames.shape[0]
    per_group = flow_times.shape[0]
    utt_total = per_group * dp_size
    dp_low = dp_rank % 2
    tp_low = tp_rank % 2
    stay = dp_low == tp_low
    direct = dp_size == 8 and tp_size == 4
    pairs = []
    for d in range(dp_size):
        for t in range(tp_size):
            if d % 2 != t % 2:
                pairs.append((d * tp_size + t, (d ^ 1) * tp_size + (t ^ 1)))

    def swap(values):
        return jnp.where(stay, values, lax.ppermute(values, AXES, pairs))

    source_dp = dp_rank - dp_low + tp_low
    utterance = source_dp * per_group + tp_rank // 2
    half = dp_low

    def relative(values):
        return jnp.roll(values, -tp_rank, axis=0)

    def gather(shard):
        return relative(lax.all_gather(shard, "tp", axis=0))

    lane = jnp.arange(TIME_DIM + 128, dtype=jnp.int32)[None, :]
    half_dim = TIME_DIM // 2
    frequency = jnp.exp((lane % half_dim).astype(F32) * (-math.log(10000.0) / (half_dim - 1)))
    column = lambda v: v[:, None]
    angles = 1000.0 * column(flow_times) * frequency
    facts = jnp.where(lane < half_dim, jnp.sin(angles), jnp.cos(angles))
    for index, fact in enumerate((flow_times, lengths, 1 - audio_drop, 1 - text_drop)):
        facts = jnp.where(lane == TIME_DIM + index, column(fact).astype(F32), facts)
    sinus_own = facts[:, :TIME_DIM]
    act_own = jax.nn.silu(dot(sinus_own.astype(BF), time_proj)).astype(BF)
    mod_cols = dot(act_own, mod_proj)
    spare = -MEL_BINS % 16
    bins = MEL_BINS + spare
    line = jnp.arange(16, dtype=jnp.int32)[:, None]
    extra = jnp.where(
        line == 0,
        span_mask[None, :],
        jnp.where(line == 1, text_ids[None, :] // 256, jnp.where(line == 2, text_ids[None, :] % 256, 0)),
    ).astype(BF)
    padded = lambda v: jnp.pad(v, ((0, spare), (0, 0)))
    mel, noise = padded(mel_frames.T), padded(noise_frames.T)
    mel_w = jnp.concatenate(
        [padded(in_proj[:MEL_BINS]), padded(in_proj[MEL_BINS : 2 * MEL_BINS])], axis=0
    )
    text_w = in_proj[2 * MEL_BINS :]
    qkv_shard = qkv_proj.transpose(1, 0, 2)
    positions = half * local_rows + jnp.arange(local_rows, dtype=jnp.int32)
    cosine, sine = rope_tables(positions, 2 * HEAD_DIM)
    wide = lambda table: jnp.tile(table, (1, WIDTH // tp_size // (2 * HEAD_DIM)))
    if direct:
        pad = ((0, 8 - per_group), (0, 0))
        (
            facts_all, mod_rows, mine, extra, qkv_full, feats, text_emb, hidden, normed_attn,
            query, key, value, key_in, value_in, heads_out, lse,
            layer, mid_grad, heads_grad, out_grad_w, mlp_sums, up_grad, down_grad,
        ) = forward(
            mel, noise, extra, jnp.pad(facts, pad), jnp.pad(mod_cols, pad), cotangent, qkv_shard, out_proj, up_proj,
            down_proj, text_table, mel_w, text_w, cosine, sine,
        )
        facts_all = facts_all[:, :per_group].reshape(utt_total, -1)
    else:
        facts_all = lax.all_gather(facts, "dp", axis=0, tiled=True)
        near = lax.all_gather(lax.all_gather(mod_cols, "tp", axis=1, tiled=True), "dp", axis=0, tiled=True)
        mod_row = lax.dynamic_slice_in_dim(near, utterance, 1, 0)
        mel, noise, extra, cot = swap(mel), swap(noise), swap(extra), swap(cotangent)
        mine = lax.dynamic_slice_in_dim(facts_all, utterance, 1, 0)[:, TIME_DIM:]
    if not direct:
        shift_attn, scale_attn, gate_attn, shift_mlp, scale_mlp, gate_mlp = jnp.split(mod_row, 6, axis=1)
        time_here, length, keep_audio, keep_text = (mine[0, i] for i in range(4))
        length = length.astype(jnp.int32)
        extra = extra[:3].astype(jnp.int32)
        ids = extra[1] * 256 + extra[2]
        keep_cond = (1.0 - extra[0].astype(F32))[None, :] * keep_audio
        info = jnp.stack([length, half * local_rows, (1 - half) * local_rows])
        mel, noise = mel.astype(F32), noise.astype(F32)
        noisy = (1.0 - time_here) * noise + time_here * mel
        feats = jnp.concatenate([noisy, mel * keep_cond], axis=0).astype(BF)
        text_emb = (jnp.take(text_table, ids, axis=0).astype(F32) * keep_text).astype(BF)
    features = jnp.concatenate([feats[:MEL_BINS].T, feats[bins : bins + MEL_BINS].T, text_emb], axis=1)
    if not direct:
        qkv_full = gather(qkv_shard)
        hidden = dot(features, in_proj)
        norm_a, inv_a = norm_parts(hidden)
        normed_attn = (norm_a * (1.0 + scale_attn) + shift_attn).astype(BF)
        query, key, value, key_in, value_in = project_qkv(normed_attn, qkv_full, wide(cosine), wide(sine))
        heads_out, lse = attend(info, query, (key, value), (key_in, value_in))
        out_full, up_full, down_full = (gather(shard) for shard in (out_proj, up_proj, down_proj))
    own, other = (key, value), (key_in, value_in)
    if not direct:
        out_full = out_full.reshape(WIDTH, WIDTH)
        attn_sum = dot(heads_out, out_full)
        hidden_mid = hidden + gate_attn * attn_sum
        normed, _ = norm_parts(hidden_mid)
        normed_mlp = (normed * (1.0 + scale_mlp) + shift_mlp).astype(BF)
        mod_rows = jnp.pad(mod_row.reshape(6, WIDTH), ((0, 2), (0, 0)))
        layer, mid_grad, heads_grad, out_grad_w, mlp_sums, up_grad, down_grad = mlp(
            normed_mlp, cot, mod_rows, hidden_mid, attn_sum, heads_out, out_full, up_full, down_full
        )
        out_grad_w = out_grad_w.reshape(tp_size, -1, WIDTH)
    sinus = facts_all[:, :TIME_DIM].astype(BF)
    time_embed = dot(sinus, time_proj)
    time_act = jax.nn.silu(time_embed).astype(BF)
    in_rows = in_proj.shape[0] // tp_size
    in_pad = -in_rows % 64
    table_rows = VOCABULARY // tp_size
    spaced = lambda v, axis: jnp.concatenate(
        [
            jnp.pad(
                lax.slice_in_dim(v, i * in_rows, (i + 1) * in_rows, axis=axis),
                [(0, in_pad if d == axis else 0) for d in range(2)],
            )
            for i in range(tp_size)
        ],
        axis=axis,
    )
    if direct:
        sums, act_parts, mel_grad, layer_out, qkv_out, misc_out, *early_out = backward(
            query, own, other, heads_grad, heads_out, lse, cosine, sine, mine, mod_rows, extra, mlp_sums,
            normed_attn, qkv_full, hidden, mid_grad, spaced(features, 1), mel_w, text_w, mod_proj,
            layer, down_grad, up_grad, out_grad_w,
        )
        mel_grad = mel_grad[:MEL_BINS].T
        order = lambda v: v.reshape((4, 2, 2) + v.shape[2:]).swapaxes(1, 2)
        mod_sums = order(sums).reshape(utt_total, -1).astype(BF)
        act_grad = jnp.sum(act_parts, axis=0)
        act_grad = order(act_grad.reshape(4, 4, WIDTH)).reshape(utt_total, WIDTH)
    else:
        layer_out = swap(layer)
        mod_rest = mlp_sums[:4].reshape(1, 4 * WIDTH)
        column_sum = lambda values: jnp.sum(values, axis=0, keepdims=True)
        dq, dk, dv, dk_in, dv_in = attend_back(
            info, query, own, other, heads_grad, heads_out, lse, cosine, sine
        )
        qkv_grad, normed_attn_grad = project_qkv_back(
            normed_attn, qkv_full, wide(cosine), wide(sine), dq, dk, dv, dk_in, dv_in
        )
        hidden_grad = (mid_grad + norm_back(norm_a, inv_a, scale_attn, normed_attn_grad)).astype(BF)
        in_grad = dot(features, hidden_grad, 0, 0).astype(BF)
        mel_part = dot(in_proj[: 2 * MEL_BINS], hidden_grad, 1, 1)
        mel_grad = swap(
            (time_here * mel_part[:MEL_BINS] + keep_cond * mel_part[MEL_BINS:]).T
        )
        text_grad = dot(hidden_grad, in_proj[2 * MEL_BINS :], 1, 1).astype(BF) * keep_text.astype(BF)
        one_hot = (ids[None, :] == jnp.arange(VOCABULARY, dtype=jnp.int32)[:, None]).astype(BF)
        table_grad = dot(one_hot, text_grad).astype(BF).reshape(tp_size, table_rows, TEXT_DIM)
        in_grad = spaced(in_grad, 0).reshape(tp_size, in_rows + in_pad, WIDTH)
        misc = jnp.concatenate(
            [table_grad, in_grad[:, :, :TEXT_DIM], in_grad[:, :, TEXT_DIM:]], axis=1
        )
        mod_part = jnp.concatenate(
            [column_sum(normed_attn_grad), column_sum(normed_attn_grad * norm_a), mod_rest], axis=1
        )
        slot = (jnp.arange(utt_total, dtype=jnp.int32) == utterance).astype(F32)[:, None]
        mod_sums = lax.psum(
            lax.psum_scatter(slot * mod_part, "tp", scatter_dimension=1, tiled=True), "dp"
        ).astype(BF)
        act_grad = lax.psum(dot(mod_sums, mod_proj, 1, 1), "tp")

        def reduce(values):
            return lax.psum(
                lax.psum_scatter(values, "tp", scatter_dimension=0, tiled=True)[0], "dp"
            )

        absolute = lambda values: jnp.roll(values, tp_rank, axis=0)
        early_out = [reduce(absolute(values)) for values in (down_grad, up_grad, out_grad_w)]
        qkv_out = reduce(absolute(qkv_grad))
        misc_out = reduce(misc)
    mod_grad = dot(time_act, mod_sums, 0, 0)
    embed_grad = jax.vjp(jax.nn.silu, time_embed)[1](act_grad)[0].astype(BF)
    time_rows = TIME_DIM // tp_size
    sinus_share = lax.dynamic_slice_in_dim(sinus, tp_rank * time_rows, time_rows, 1)
    time_grad = dot(sinus_share, embed_grad, 0, 0)
    down_out, up_out, out_out = (values.astype(F32) for values in early_out)
    misc_out = misc_out.astype(F32)
    right = table_rows + in_rows + in_pad
    in_out = jnp.concatenate(
        [misc_out[table_rows : table_rows + in_rows], misc_out[right : right + in_rows]], axis=1
    )
    return (
        layer_out, mel_grad, in_out, misc_out[:table_rows], time_grad, mod_grad,
        qkv_out.astype(F32).transpose(1, 0, 2), out_out, up_out, down_out,
    )


def solution(mesh):
    frames = P(("dp", "tp"), None)
    frame = P(("dp", "tp"))
    return jax.shard_map(
        body,
        mesh=mesh,
        in_specs=(
            frames, frames, frame, frame, P("dp"), P("dp"), P("dp"), P("dp"),
            P(), P(), P(), P(None, "tp"), P(None, None, "tp"), P("tp", None), P(None, "tp"),
            P("tp", None), frames,
        ),
        out_specs=(
            frames, frames, P("tp", None), P("tp", None), P("tp", None), P(None, "tp"),
            P(None, None, "tp"), P("tp", None), P(None, "tp"), P("tp", None),
        ),
        check_vma=False,
    )
```
